32 devices in a mesh: wide: 16 (over z, y, x), narrow: 2 (over core).
Axes of the slice: x: 2, y: 2, z: 4, core: 2. Of those that a mesh axis runs over, the one named last changes fastest.
Arguments:
- tokens: bfloat16 [31360, 512], P(('wide', 'narrow')), may hold values from -6 to 6
- mask: int32 [160, 196], P(('wide', 'narrow')), may hold values 0 or 1
- ln1_gain: float32 [2, 512], replicated, may hold values from 0.5 to 1.5
- ln1_bias: float32 [2, 512], replicated, may hold values from -4 to 4
- in_weight: bfloat16 [2, 512, 3072], P(None, ('wide', 'narrow')), may hold values from -0.25 to 0.25
- in_bias: float32 [2, 3072], replicated, may hold values from -6 to 6
- ln2_gain: float32 [2, 1536], replicated, may hold values from 0.5 to 1.5
- ln2_bias: float32 [2, 1536], replicated, may hold values from -4 to 4
- spatial_weight: bfloat16 [2, 196, 196], replicated, may hold values from -0.4375 to 0.4375
- spatial_bias: float32 [2, 196], replicated, may hold values from -6 to 6
- out_weight: bfloat16 [2, 1536, 512], P(None, ('wide', 'narrow')), may hold values from -0.15625 to 0.15625
- out_bias: float32 [2, 512], replicated, may hold values from -4 to 4
- cotangent: bfloat16 [31360, 512], P(('wide', 'narrow')), may hold values from -6 to 6
Outputs:
- layer_out: bfloat16 [31360, 512], P(('wide', 'narrow'))
- input_grad: float32 [31360, 512], P(('wide', 'narrow'))
- ln1_gain_grad: float32 [2, 512], replicated
- ln1_bias_grad: float32 [2, 512], replicated
- in_weight_grad: float32 [2, 512, 3072], P(None, ('wide', 'narrow'))
- in_bias_grad: float32 [2, 3072], replicated
- ln2_gain_grad: float32 [2, 1536], replicated
- ln2_bias_grad: float32 [2, 1536], replicated
- spatial_weight_grad: float32 [2, 196, 196], replicated
- spatial_bias_grad: float32 [2, 196], replicated
- out_weight_grad: float32 [2, 1536, 512], P(None, ('wide', 'narrow'))
- out_bias_grad: float32 [2, 512], replicated
The draws below stay inside these ranges and needn't reach their ends.
All inputs are finite; a program needn't handle non-finite values. No bound on the sum of `mask` on one device may be relied on, other than what follows from the above.
Results may differ from the reference program's by a relative error of at most 0.009.
Values may be sent and summed in bfloat16 or wider, within the bound.
No kernel may reach another device: no remote copies, remote signals or barrier semaphores. Data moves between devices by JAX's collectives and lax.ppermute only.
A program may use at most 192 MiB of HBM per device.

```python
import jax
import jax.numpy as jnp
from jax import lax

D = 512
H = 3072
G = 1536
P_SIZE = 196
LAYERS = 2
IMG_DEV = 5
IMAGES = 160
TOKENS = 31360


def set_ends(result, key, least, high):
    longest = result.shape.index(max(result.shape))
    spots = []
    for shift in (0, 1):
        where = [jax.random.randint(jax.random.fold_in(key, axis), (), 0, length) for axis, length in enumerate(result.shape)]
        where[longest] = (where[longest] + shift) % result.shape[longest]
        spots.append(tuple(where))
    return result.at[spots[0]].set(least).at[spots[1]].set(high)


def shard_levels(own_key, dims, cuts, smallest, high):
    def one(dim, shards_of):
        heights = jax.random.uniform(jax.random.fold_in(jax.random.fold_in(own_key, 6), dim), (shards_of,), jnp.float32, smallest / len(cuts), high / len(cuts))
        return jnp.repeat(jnp.exp(heights), dims[dim] // shards_of).reshape((-1,) + (1,) * (len(dims) - dim - 1))

    level = one(*cuts[0])
    for cut in cuts[1:]:
        level = level * one(*cut)
    return level


def scatter_about(own_key, shape, deviation, limit, shards=(), dtype=jnp.bfloat16):
    loudness = shard_levels(own_key, shape, shards, -0.22, 0.18) if shards else 1.0
    entries = jax.random.normal(own_key, shape, jnp.float32) * deviation * loudness
    return jnp.minimum(jnp.maximum(entries, -limit), limit).astype(dtype)


def setup_inputs(seed: int = 0) -> dict:
    keys = jax.random.split(jax.random.key(seed), 14)
    return {
        "tokens": scatter_about(keys[0], (TOKENS, D), 1.0, 6.0, ((0, 32),)),
        "mask": set_ends((jax.random.randint(keys[1], (IMAGES, P_SIZE), 0, 4) < 3).astype(jnp.int32), jax.random.fold_in(keys[1], 1), 0, 1),
        "ln1_gain": jnp.clip(1.0 + 0.1 * jax.random.normal(keys[2], (LAYERS, D), jnp.float32), 0.5, 1.5),
        "ln1_bias": scatter_about(keys[3], (LAYERS, D), 0.3, 4.0, (), jnp.float32),
        "in_weight": scatter_about(keys[4], (LAYERS, D, H), D ** -0.5, 0.25, ((1, 32),)),
        "in_bias": scatter_about(keys[5], (LAYERS, H), 0.5, 6.0, (), jnp.float32),
        "ln2_gain": jnp.clip(1.0 + 0.1 * jax.random.normal(keys[6], (LAYERS, G), jnp.float32), 0.5, 1.5),
        "ln2_bias": scatter_about(keys[7], (LAYERS, G), 0.3, 4.0, (), jnp.float32),
        "spatial_weight": scatter_about(keys[8], (LAYERS, P_SIZE, P_SIZE), P_SIZE ** -0.5, 0.4375),
        "spatial_bias": scatter_about(keys[9], (LAYERS, P_SIZE), 0.5, 6.0, (), jnp.float32),
        "out_weight": scatter_about(keys[10], (LAYERS, G, D), G ** -0.5, 0.15625, ((1, 32),)),
        "out_bias": scatter_about(keys[11], (LAYERS, D), 0.3, 4.0, (), jnp.float32),
        "cotangent": scatter_about(keys[12], (TOKENS, D), 1.0, 6.0, ((0, 32),)),
    }


EPS = 1e-05
HIGH = lax.Precision.HIGHEST

@jax.custom_vjp
def low(v):
    return lax.optimization_barrier(v.astype(jnp.bfloat16)).astype(jnp.float32)

@jax.custom_vjp
def low_back(v):
    return v

def low_keep(v):
    return (low(v), None)

def low_pass(kept, grad):
    return (grad,)

def back_keep(v):
    return (v, None)

def back_low(kept, grad):
    return (low(grad),)
low.defvjp(low_keep, low_pass)
low_back.defvjp(back_keep, back_low)

def layer_norm(values, norm_gain, norm_bias):
    average = lax.optimization_barrier(jnp.mean(values, -1, keepdims=True))
    centred = values - average
    spread = lax.optimization_barrier(jnp.mean(centred * centred, -1, keepdims=True))
    return centred * lax.rsqrt(spread + EPS) * norm_gain + norm_bias

def gmlp_block(weights, inputs, valid):
    gain_one, bias_one, w_in, b_in, gain_two, bias_two, w_sp, b_sp, w_out, b_out = weights
    normed = low(layer_norm(inputs, gain_one, bias_one))
    hidden = low_back(jnp.dot(normed, w_in, precision=HIGH) + b_in)
    active = jax.nn.gelu(hidden)
    half_width = w_out.shape[0]
    left_part = active[:, :half_width]
    right_part = active[:, half_width:]
    spatial_in = low(layer_norm(right_part, gain_two, bias_two) * valid)
    slots = w_sp.shape[0]
    cube = spatial_in.reshape(-1, slots, half_width)
    mixed = jnp.einsum('pq,iqg->ipg', w_sp, cube, precision=HIGH) + b_sp[None, :, None]
    mixed = low_back(mixed.reshape(-1, half_width))
    gated = low(left_part * mixed * valid)
    branch = low_back(jnp.dot(gated, w_out, precision=HIGH) + b_out)
    return inputs + branch

def forward(weights, inputs, valid):
    for layer_pos in range(LAYERS):
        inputs = gmlp_block(tuple((w[layer_pos] for w in weights)), inputs, valid)
    return inputs

def reference(tokens, mask, ln1_gain, ln1_bias, in_weight, in_bias, ln2_gain, ln2_bias, spatial_weight, spatial_bias, out_weight, out_bias, cotangent):
    weights = tuple((w.astype(jnp.float32) for w in (ln1_gain, ln1_bias, in_weight, in_bias, ln2_gain, ln2_bias, spatial_weight, spatial_bias, out_weight, out_bias)))
    groups = IMAGES // IMG_DEV
    rows_group = IMG_DEV * P_SIZE
    token_groups = tokens.astype(jnp.float32).reshape(groups, rows_group, D)
    valid_groups = mask.astype(jnp.float32).reshape(groups, rows_group, 1)
    cot_groups = cotangent.astype(jnp.float32).reshape(groups, rows_group, D)

    def one_group(totals, pieces):
        inputs, valid, upstream = pieces

        def run(weights_now, inputs_now):
            return forward(weights_now, inputs_now, valid)
        outputs, pullback = jax.vjp(run, weights, inputs)
        weight_grads, input_grad = pullback(upstream)
        totals = jax.tree.map(lambda a, b: a + b, totals, weight_grads)
        return (totals, (outputs, input_grad))
    zeros = jax.tree.map(jnp.zeros_like, weights)
    totals, (outputs, input_grads) = lax.scan(one_group, zeros, (token_groups, valid_groups, cot_groups))
    return (outputs.reshape(-1, D).astype(jnp.bfloat16), input_grads.reshape(-1, D), totals[0], totals[1], totals[2], totals[3], totals[4], totals[5], totals[6], totals[7], totals[8], totals[9])
```

```python
import jax
import jax.numpy as jnp
from jax import lax
from jax.experimental import pallas as pl
from jax.experimental.pallas import tpu as pltpu
from jax.sharding import PartitionSpec as P

EPS = 1e-05
AXES = ("wide", "narrow")
F32 = jnp.float32
BF16 = jnp.bfloat16
TANH_ONE = 2 * 0.7978845608028654
TANH_THREE = 8 * 0.7978845608028654 * 0.044715
COLUMNS = 256
BLOCK = 16
GROUP = 512
VMEM_BYTES = 60 * 1024 * 1024
WEIGHTS = ("b_in", "gain_one", "bias_one", "gain_two", "bias_two", "b_out")
SUMS = ("b_out", "b_in", "spatial", "gain_two", "bias_two", "gain_one", "bias_one")


def dot(a, b):
    return jnp.dot(a, b, preferred_element_type=F32)


def dot_last(a, b):
    return lax.dot_general(a, b, (((1,), (1,)), ((), ())), preferred_element_type=F32)


def dot_first(a, b):
    return lax.dot_general(a, b, (((0,), (0,)), ((), ())), preferred_element_type=F32)


def gelu_pair(half):
    square = half * half
    tanh = jnp.tanh(half * (TANH_ONE + TANH_THREE * square))
    upper = 1.0 + tanh
    value = half * upper
    slope = upper + value * (1.0 - tanh) * (TANH_ONE + (3 * TANH_THREE) * square)
    return value, slope


def fold_rows(values):
    total = values[:8]
    for row in range(8, values.shape[0], 8):
        total = total + values[row : row + 8]
    return total


def fold_columns(values):
    total = values[:, :128]
    for column in range(128, values.shape[1], 128):
        total = total + values[:, column : column + 128]
    return total


def white_of(values):
    centred = values - jnp.mean(values, -1, keepdims=True)
    inverse = lax.rsqrt(jnp.mean(centred * centred, -1, keepdims=True) + EPS)
    return centred * inverse, inverse


def cuts(width):
    return [slice(c, c + COLUMNS) for c in range(0, width, COLUMNS)]


def in_columns(w_in, start):
    at = start % GROUP
    return w_in[start // GROUP, :, at : at + COLUMNS]


def forward_image(values, live, valid, mixer, slot_pad, w, t, slots):
    rows = values.shape[0]
    half_width = t["white"].shape[1]
    cut = slots // BLOCK * BLOCK
    white_one, unused_inverse = white_of(values)
    t["normed"][...] = (white_one * w["gain_one"][...] + w["bias_one"][...]).astype(BF16)
    total = None
    for sl in cuts(half_width):
        at = half_width + sl.start
        half = dot(t["normed"][...], in_columns(w["w_in"], at)) + w["b_in"][:, at : at + COLUMNS]
        value, slope = gelu_pair(half)
        t["right"][:, sl] = value
        t["right_slope"][:, sl] = slope.astype(BF16)
        part = fold_columns(value)
        total = part if total is None else total + part
    average = jnp.sum(total, -1, keepdims=True) * (1.0 / half_width)
    total = None
    for sl in cuts(half_width):
        centred = t["right"][:, sl] - average
        part = fold_columns(centred * centred)
        total = part if total is None else total + part
    spread = jnp.sum(total, -1, keepdims=True) * (1.0 / half_width)
    inverse = lax.rsqrt(spread + EPS) * live
    row = lax.broadcasted_iota(jnp.int32, (rows - cut, COLUMNS), 0)
    for sl in cuts(half_width):
        white = (t["right"][:, sl] - average) * inverse
        t["white"][:, sl] = white.astype(BF16)
        slot_in = white * w["gain_two"][:, sl] + w["bias_two"][:, sl]
        t["slot_in"][:cut, sl] = slot_in[:cut].astype(BF16)
        last = jnp.where(row < slots - cut, slot_in[cut:], slot_pad[:, sl])
        t["slot_in"][cut:, sl] = last.astype(BF16)
    for sl in cuts(half_width):
        half = dot(t["normed"][...], in_columns(w["w_in"], sl.start)) + w["b_in"][:, sl]
        left, slope = gelu_pair(half)
        mixed = dot(mixer, t["slot_in"][:, sl])
        t["gated"][:, sl] = (left * mixed).astype(BF16)
        t["left"][:, sl] = left.astype(BF16)
        t["left_slope"][:, sl] = (mixed * slope).astype(BF16)
    branch = dot(t["gated"][...], w["w_out"][...].reshape(half_width, -1)) * valid
    return values + (branch + w["b_out"][...]), inverse


def backward_image(upstream, valid, mixer_back, inverse, w, t, hidden_grad, sums, slots):
    rows = upstream.shape[0]
    half_width = t["white"].shape[1]
    cut = slots // BLOCK * BLOCK
    for sl in cuts(half_width):
        blocks = slice(sl.start // BLOCK, sl.stop // BLOCK)
        gated_grad = dot_last(upstream, w["w_out"][blocks].reshape(COLUMNS, -1))
        t["mixed_grad"][:, sl] = (gated_grad * t["left"][:, sl].astype(F32)).astype(BF16)
        left_grad = gated_grad * t["left_slope"][:, sl].astype(F32)
        hidden_grad[:, sl] = left_grad.astype(BF16)
        sums["b_in"][:, sl] += fold_rows(left_grad)
    outer = dot_last(t["slot_in"][...], t["mixed_grad"][...])
    is_slot = lax.broadcasted_iota(jnp.int32, (rows, 1), 0) < slots
    sums["spatial"][...] += outer * jnp.where(is_slot, valid, 1.0)
    back = mixer_back.astype(F32)
    by_bias = outer[slots + 2 : slots + 3] + outer[slots + 3 : slots + 4]
    by_gain = outer[slots + 4 : slots + 5] + outer[slots + 5 : slots + 6]
    mean_scaled = jnp.sum(back * by_gain, -1, keepdims=True) * (1.0 / half_width)
    mean_white = jnp.sum(back * (outer - by_bias), -1, keepdims=True) * (1.0 / half_width)
    for sl in cuts(half_width):
        at = half_width + sl.start
        slot_grad = dot(mixer_back, t["mixed_grad"][:, sl])
        white = t["white"][:, sl].astype(F32)
        sums["gain_two"][:, sl] += fold_rows(slot_grad * white)
        sums["bias_two"][:, sl] += slot_grad[cut:]
        scaled = slot_grad * w["gain_two"][:, sl] - mean_scaled - white * mean_white
        right_grad = scaled * inverse * t["right_slope"][:, sl].astype(F32)
        hidden_grad[:, at : at + COLUMNS] = right_grad.astype(BF16)
        sums["b_in"][:, at : at + COLUMNS] += fold_rows(right_grad)


def backward_norm(values, hidden_grad, upstream, w, sums):
    white, inverse = white_of(values)
    normed_grad = None
    for group in range(w["w_in"].shape[0]):
        part = dot_last(hidden_grad[:, group * GROUP : (group + 1) * GROUP], w["w_in"][group])
        normed_grad = part if normed_grad is None else normed_grad + part
    sums["gain_one"][...] += fold_rows(normed_grad * white)
    sums["bias_one"][...] += fold_rows(normed_grad)
    scaled = normed_grad * w["gain_one"][...]
    mean = jnp.mean(scaled, -1, keepdims=True)
    mean_white = jnp.mean(scaled * white, -1, keepdims=True)
    return upstream + inverse * (scaled - mean - white * mean_white)


def load_blocks(owner, pieces, w_in, w_out, sem):
    per = w_out.shape[0] * BLOCK // w_out.shape[2] if w_out is not None else pieces[0].shape[1] - w_in.shape[0]
    groups = pieces[0].shape[1] - per
    position = 0
    for piece in pieces:
        count = piece.shape[0]

        def start(at, carry, piece=piece, position=position):
            block = owner[position + at]
            if w_in is not None:
                rows = pl.ds(pl.multiple_of(block * BLOCK, BLOCK), BLOCK)
                pltpu.make_async_copy(piece.at[at, :groups], w_in.at[:, rows], sem).start()
            if w_out is not None:
                rows = pl.ds(block * per, per)
                pltpu.make_async_copy(piece.at[at, groups:], w_out.at[rows], sem).start()
            return carry

        lax.fori_loop(0, count, start, 0)
        position += count
    if w_in is not None:
        pltpu.make_async_copy(w_in, w_in, sem).wait()
    if w_out is not None:
        pltpu.make_async_copy(w_out, w_out, sem).wait()


def zero(refs):
    for ref in refs:
        ref[...] = jnp.zeros_like(ref)


def whole(shape):
    return pl.BlockSpec(shape, lambda *i: (0,) * len(shape))


def image(rows, columns):
    return pl.BlockSpec((1, rows, columns), lambda i, *unused: (i, 0, 0))


def anywhere(count):
    return [pl.BlockSpec(memory_space=pl.ANY)] * count


def call(kernel, name, grid, in_specs, outs, out_specs, scratch, flops, table=0, aliases=None):
    return pl.pallas_call(
        kernel,
        grid_spec=pltpu.PrefetchScalarGridSpec(
            num_scalar_prefetch=table,
            grid=grid,
            in_specs=in_specs,
            out_specs=out_specs,
            scratch_shapes=scratch,
        ),
        out_shape=[jax.ShapeDtypeStruct(shape, dtype) for shape, dtype in outs],
        input_output_aliases=aliases or {},
        compiler_params=pltpu.CompilerParams(vmem_limit_bytes=VMEM_BYTES),
        cost_estimate=pl.CostEstimate(flops=flops, bytes_accessed=20_000_000, transcendentals=0),
        name=name,
    )


def weight_scratch(width, hidden):
    return [
        pltpu.VMEM((hidden // GROUP, width, GROUP), BF16),
        pltpu.VMEM((hidden // 2 // BLOCK, BLOCK, width), BF16),
        pltpu.SemaphoreType.DMA,
    ]


def sum_shapes(rows, width, hidden, slots):
    return {
        "b_out": (8, width),
        "b_in": (8, hidden),
        "spatial": (rows, rows),
        "gain_two": (8, hidden // 2),
        "bias_two": (rows - slots // BLOCK * BLOCK, hidden // 2),
        "gain_one": (8, width),
        "bias_one": (8, width),
    }


def forward_save(values, valid, live, mixer, slot_pad, w, owner, pieces, slots):
    images, rows, width = values.shape
    hidden = w["b_in"].shape[1]
    gate = hidden // 2
    outs = {
        "values": (width, F32),
        "normed": (width, BF16),
        "left": (gate, BF16),
        "left_slope": (gate, BF16),
        "white": (gate, BF16),
        "right_slope": (gate, BF16),
        "slot_in": (gate, BF16),
        "gated": (gate, BF16),
        "inverse": (1, F32),
    }
    n_w, n_p, n_o = len(WEIGHTS), len(pieces), len(outs)

    def kernel(owner_ref, values_ref, valid_ref, live_ref, mixer_ref, pad_ref, *refs):
        weights = dict(zip(WEIGHTS, refs[:n_w]))
        out = dict(zip(outs, refs[n_w + n_p : n_w + n_p + n_o]))
        right, weights["w_in"], weights["w_out"], sem = refs[n_w + n_p + n_o :]

        @pl.when(pl.program_id(0) == 0)
        def _():
            load_blocks(owner_ref, refs[n_w : n_w + n_p], weights["w_in"], weights["w_out"], sem)

        kept = {name: ref.at[0] for name, ref in out.items()}
        kept["right"] = right
        result, inverse = forward_image(
            values_ref[0].astype(F32), live_ref[...], valid_ref[0], mixer_ref[0], pad_ref, weights, kept, slots
        )
        out["values"][0] = result
        out["inverse"][0] = inverse

    results = call(
        kernel,
        "forward_save",
        (images,),
        [image(rows, width), image(rows, 1), whole((rows, 1)), image(rows, rows), whole(slot_pad.shape)]
        + [whole(w[name].shape) for name in WEIGHTS]
        + anywhere(n_p),
        [((images, rows, columns), dtype) for columns, dtype in outs.values()],
        [image(rows, columns) for columns, unused in outs.values()],
        [pltpu.VMEM((rows, gate), F32)] + weight_scratch(width, hidden),
        12_000_000_000,
        table=1,
    )(owner, values, valid, live, mixer, slot_pad, *[w[name] for name in WEIGHTS], *pieces)
    return dict(zip(outs, results))


def forward_backward(values, cotangent, valid, live, mixer, mixer_back, slot_pad, w, owner, pieces, slots):
    images, rows, width = values.shape
    hidden = w["b_in"].shape[1]
    gate = hidden // 2
    outs = {
        "values": (width, BF16),
        "normed": (width, BF16),
        "gated": (gate, BF16),
        "hidden_grad": (hidden, BF16),
        "masked": (width, BF16),
        "upstream": (width, F32),
    }
    shapes = sum_shapes(rows, width, hidden, slots)
    scratch_names = ("right", "left", "left_slope", "white", "right_slope", "slot_in", "mixed_grad")
    n_w, n_p, n_o, n_s = len(WEIGHTS), len(pieces), len(outs), len(SUMS)

    def kernel(owner_ref, values_ref, cot_ref, valid_ref, live_ref, mixer_ref, back_ref, pad_ref, *refs):
        weights = dict(zip(WEIGHTS, refs[:n_w]))
        rest = refs[n_w + n_p :]
        out = dict(zip(outs, rest[:n_o]))
        sums = dict(zip(SUMS, rest[n_o : n_o + n_s]))
        kept = dict(zip(scratch_names, rest[n_o + n_s :]))
        weights["w_in"], weights["w_out"], sem = rest[n_o + n_s + len(scratch_names) :]

        @pl.when(pl.program_id(0) == 0)
        def _():
            load_blocks(owner_ref, refs[n_w : n_w + n_p], weights["w_in"], weights["w_out"], sem)
            zero(sums.values())

        kept["normed"] = out["normed"].at[0]
        kept["gated"] = out["gated"].at[0]
        here = values_ref[0]
        result, inverse = forward_image(
            here, live_ref[...], valid_ref[0], mixer_ref[0], pad_ref, weights, kept, slots
        )
        out["values"][0] = result.astype(BF16)
        upstream = cot_ref[0].astype(F32)
        sums["b_out"][...] += fold_rows(upstream)
        masked = (upstream * valid_ref[0]).astype(BF16)
        out["masked"][0] = masked
        hidden_grad = out["hidden_grad"].at[0]
        backward_image(masked, valid_ref[0], back_ref[0], inverse, weights, kept, hidden_grad, sums, slots)
        out["upstream"][0] = backward_norm(here, hidden_grad, upstream, weights, sums)

    results = call(
        kernel,
        "forward_backward",
        (images,),
        [image(rows, width)] * 2
        + [image(rows, 1), whole((rows, 1)), image(rows, rows), image(rows, rows), whole(slot_pad.shape)]
        + [whole(w[name].shape) for name in WEIGHTS]
        + anywhere(n_p),
        [((images, rows, columns), dtype) for columns, dtype in outs.values()]
        + [(shapes[name], F32) for name in SUMS],
        [image(rows, columns) for columns, unused in outs.values()] + [whole(shapes[name]) for name in SUMS],
        [pltpu.VMEM((rows, gate), F32)] + [pltpu.VMEM((rows, gate), BF16)] * 6 + weight_scratch(width, hidden),
        24_000_000_000,
        table=1,
    )(owner, values, cotangent, valid, live, mixer, mixer_back, slot_pad, *[w[name] for name in WEIGHTS], *pieces)
    return dict(zip(outs, results)), dict(zip(SUMS, results[n_o:]))


def backward_gate(upstream, kept, valid, mixer_back, w, owner, pieces, slots):
    images, rows, width = upstream.shape
    hidden = w["b_in"].shape[1]
    gate = hidden // 2
    shapes = sum_shapes(rows, width, hidden, slots)
    names = SUMS[:5]
    reads = ("left", "left_slope", "white", "right_slope", "slot_in", "inverse")
    n_p, n_r = len(pieces), len(reads)

    def kernel(owner_ref, up_ref, valid_ref, back_ref, gain_ref, *refs):
        t = {name: ref.at[0] for name, ref in zip(reads, refs)}
        rest = refs[n_r + n_p :]
        hidden_grad, masked_ref = rest[:2]
        sums = dict(zip(names, rest[2 : 2 + len(names)]))
        t["mixed_grad"], w_out, sem = rest[2 + len(names) :]

        @pl.when(pl.program_id(0) == 0)
        def _():
            load_blocks(owner_ref, refs[n_r : n_r + n_p], None, w_out, sem)
            zero(sums.values())

        branch_grad = up_ref[0].astype(BF16).astype(F32)
        sums["b_out"][...] += fold_rows(branch_grad)
        masked = (branch_grad * valid_ref[0]).astype(BF16)
        masked_ref[0] = masked
        weights = {"w_out": w_out, "gain_two": gain_ref}
        backward_image(
            masked, valid_ref[0], back_ref[0], t["inverse"][...], weights, t, hidden_grad.at[0], sums, slots
        )

    results = call(
        kernel,
        "backward_gate",
        (images,),
        [image(rows, width), image(rows, 1), image(rows, rows), whole((1, gate))]
        + [image(rows, gate)] * 5
        + [image(rows, 1)]
        + anywhere(n_p),
        [((images, rows, hidden), BF16), ((images, rows, width), BF16)] + [(shapes[name], F32) for name in names],
        [image(rows, hidden), image(rows, width)] + [whole(shapes[name]) for name in names],
        [pltpu.VMEM((rows, gate), BF16)] + weight_scratch(width, hidden)[1:],
        9_000_000_000,
        table=1,
    )(owner, upstream, valid, mixer_back, w["gain_two"], *[kept[name] for name in reads], *pieces)
    return results[0], results[1], dict(zip(names, results[2:]))


def backward_first(values, hidden_grad, upstream, w, owner, pieces):
    images, rows, width = values.shape
    hidden = hidden_grad.shape[2]
    n_p = len(pieces)

    def kernel(owner_ref, values_ref, grad_ref, up_ref, gain_ref, *refs):
        out, gain_sum, bias_sum, w_in, sem = refs[n_p:]

        @pl.when(pl.program_id(0) == 0)
        def _():
            load_blocks(owner_ref, refs[:n_p], w_in, None, sem)
            zero((gain_sum, bias_sum))

        out[0] = backward_norm(
            values_ref[0].astype(F32),
            grad_ref.at[0],
            up_ref[0],
            {"w_in": w_in, "gain_one": gain_ref},
            {"gain_one": gain_sum, "bias_one": bias_sum},
        )

    scratch = weight_scratch(width, hidden)
    return call(
        kernel,
        "backward_first",
        (images,),
        [image(rows, width), image(rows, hidden), image(rows, width), whole((1, width))] + anywhere(n_p),
        [((images, rows, width), F32)] + [((8, width), F32)] * 2,
        [image(rows, width)] + [whole((8, width))] * 2,
        [scratch[0], scratch[2]],
        6_000_000_000,
        table=1,
    )(owner, values, hidden_grad, upstream, w["gain_one"], *pieces)


def in_weight_blocks(owner, normed, hidden_grad, first, count, held):
    depth, width = normed.shape
    half = width // BLOCK // 2

    def kernel(owner_ref, left, right, one, other, result):
        result[...] = dot_first(left[...], right[...])
        for at in range(half):
            for out, block in ((one, owner_ref[at]), (other, owner_ref[half + at])):
                rows = pl.ds(pl.multiple_of(block * BLOCK, BLOCK), BLOCK)
                out[at, 0] = result[rows].astype(BF16)

    spec = pl.BlockSpec((half, 1, BLOCK, GROUP), lambda g, *unused: (0, g, 0, 0))
    return call(
        kernel,
        "in_weight_blocks",
        (count,),
        [whole((depth, width)), pl.BlockSpec((depth, GROUP), lambda g, *unused: (0, first + g))],
        [((half, held, BLOCK, GROUP), BF16)] * 2,
        [spec] * 2,
        [pltpu.VMEM((width, GROUP), F32)],
        2 * depth * width * GROUP * count,
        table=1,
    )(owner, normed, hidden_grad)


def out_weight_blocks(owner, gated, masked, into=None):
    depth, gate = gated.shape
    width = masked.shape[1]
    half = width // BLOCK // 2
    per = gate // width
    steps = gate // GROUP
    held = into[0].shape[1] if into else per
    assert held % per == 0

    def kernel(owner_ref, left, right, *refs):
        one, other, result = refs[-3:]
        step = pl.program_id(0)
        result[pl.ds(pl.multiple_of(step * GROUP, GROUP), GROUP)] = dot_first(left[...], right[...])

        @pl.when(step == steps - 1)
        def _():
            for at in range(half):
                for out, block in ((one, owner_ref[at]), (other, owner_ref[half + at])):
                    for part in range(per):
                        rows = pl.ds(pl.multiple_of((block * per + part) * BLOCK, BLOCK), BLOCK)
                        out[at, part] = result[rows].astype(BF16)

    spec = pl.BlockSpec((half, per, BLOCK, width), lambda g, *unused: (0, held // per - 1, 0, 0))
    return call(
        kernel,
        "out_weight_blocks",
        (steps,),
        [pl.BlockSpec((depth, GROUP), lambda g, *unused: (0, g)), whole((depth, width))]
        + anywhere(2 if into else 0),
        [((half, held, BLOCK, width), BF16)] * 2,
        [spec] * 2,
        [pltpu.VMEM((gate, width), F32)],
        2 * depth * width * gate,
        table=1,
        aliases={3: 0, 4: 1} if into else None,
    )(owner, gated, masked, *(into or ()))


class Tree:
    def __init__(self, devices):
        self.devices = devices
        self.far = devices // 8

    def swap(self, values, one, other=None):
        other = one if other is None else other
        pairs = [(i, i ^ (other if i % 2 else one)) for i in range(self.devices)]
        return lax.ppermute(values, AXES, pairs)

    def owners(self):
        me = lax.axis_index(AXES).astype(jnp.int32)
        odd = me % 2
        near, next_ = 2 + 2 * odd, 4 - 2 * odd
        side = jnp.arange(2, dtype=jnp.int32)[:, None, None, None]
        first = jnp.arange(2, dtype=jnp.int32)[None, :, None, None]
        second = jnp.arange(2, dtype=jnp.int32)[None, None, :, None]
        far = jnp.arange(self.far, dtype=jnp.int32)[None, None, None, :]
        one = jnp.where(side == 0, near, next_)
        two = jnp.where(side == 0, next_, near)
        return ((me ^ side) ^ (first * one) ^ (second * two) ^ (far * 8)).reshape(-1)

    def gather(self, own):
        column = jnp.stack([own] + [self.swap(own, 8 * m) for m in range(1, self.far)])
        first = self.swap(column, 2, 4)
        second = self.swap(column, 4, 2)
        both = self.swap(first, 4, 2)
        mine = [column, second, first, both]
        return mine + [self.swap(piece, 1) for piece in mine]

    def scatter(self, mine, theirs):
        far = self.far
        total = mine.astype(F32) + self.swap(theirs, 1).astype(F32)
        got = self.swap(total[2 * far :].astype(BF16), 2, 4)
        total = total[: 2 * far] + got.astype(F32)
        got = self.swap(total[far:].astype(BF16), 4, 2)
        total = total[:far] + got.astype(F32)
        last = total.astype(BF16)
        got = [self.swap(last[m], 8 * m) for m in range(1, far)]
        result = total[0]
        for part in got:
            result = result + part.astype(F32)
        return result

    def rows(self, block, groups):
        parts = []
        if groups:
            parts.append(block[:groups].transpose(1, 0, 2).reshape(BLOCK, -1))
        if groups < block.shape[0]:
            parts.append(block[groups:].reshape(-1, block.shape[2]))
        return parts

    def total(self, values):
        odd = lax.axis_index("narrow") % 2 == 1
        mine = jnp.where(odd, values[1], values[0])
        theirs = jnp.where(odd, values[0], values[1])
        mine = mine + self.swap(theirs, 1)
        mine = mine + self.swap(mine, 2, 4)
        mine = mine + self.swap(mine, 4, 2)
        bit = 8
        while bit < self.devices:
            mine = mine + self.swap(mine, bit)
            bit *= 2
        theirs = self.swap(mine, 1)
        return jnp.stack([jnp.where(odd, theirs, mine), jnp.where(odd, mine, theirs)])


class Plain:
    def __init__(self, width, gate):
        self.width, self.gate = width, gate
        self.blocks = width // BLOCK

    def owners(self):
        return jnp.arange(self.blocks, dtype=jnp.int32)

    def gather(self, own):
        w_in, w_out = (lax.all_gather(part, AXES, axis=0, tiled=True) for part in own)
        return [pack_blocks(w_in, w_out, self.blocks)]

    def scatter(self, mine, theirs):
        return jnp.concatenate([mine, theirs]).astype(F32)

    def rows(self, blocks, groups):
        parts = []
        if groups:
            parts.append(blocks[:, :groups].transpose(0, 2, 1, 3).reshape(self.width, -1))
        if groups < blocks.shape[1]:
            parts.append(blocks[:, groups:].reshape(self.gate, -1))
        return [lax.psum_scatter(part, AXES, scatter_dimension=0, tiled=True) for part in parts]

    def total(self, values):
        return lax.psum(values, AXES)


def pack_blocks(w_in, w_out, blocks):
    groups = w_in.shape[1] // GROUP
    inner = w_in.reshape(blocks, BLOCK, groups, GROUP).transpose(0, 2, 1, 3)
    outer = w_out.reshape(blocks, -1, BLOCK, GROUP)
    return jnp.concatenate([inner, outer], 1)


def bfloat_pair(values):
    top = lax.reduce_precision(values, 8, 7)
    return top.astype(BF16), lax.reduce_precision(values - top, 8, 7).astype(BF16)


def spatial_operands(valid, w_sp, b_sp, gain_two, bias_two, rows):
    images, slots = valid.shape
    gate = gain_two.shape[0]
    cut = slots // BLOCK * BLOCK
    spare = rows - slots
    masked = w_sp[None] * valid[:, None, :].astype(BF16)
    bias = jnp.broadcast_to(jnp.stack(bfloat_pair(b_sp), -1)[None], (images, slots, 2))
    mixer = jnp.concatenate([masked, bias], 2)
    mixer = jnp.pad(mixer, ((0, 0), (0, spare), (0, spare - 2)))
    column_sum = jnp.einsum("ir,pr->ip", valid.astype(BF16), w_sp, preferred_element_type=F32)
    back = jnp.concatenate([jnp.swapaxes(masked, 1, 2), jnp.stack(bfloat_pair(column_sum), 1)], 1)
    back = jnp.pad(back, ((0, 0), (0, spare - 2), (0, spare)))
    one = jnp.ones((gate,), BF16)
    pad = jnp.stack([one, one, *bfloat_pair(bias_two), *bfloat_pair(gain_two)])
    pad = jnp.pad(pad, ((slots - cut, rows - slots - 6), (0, 0))).astype(F32)
    return mixer, back, pad


def shards(
    tokens,
    mask,
    ln1_gain,
    ln1_bias,
    in_weight,
    in_bias,
    ln2_gain,
    ln2_bias,
    spatial_weight,
    spatial_bias,
    out_weight,
    out_bias,
    cotangent,
):
    devices = lax.axis_size(AXES)
    images, slots = mask.shape
    width = tokens.shape[1]
    hidden = in_weight.shape[2]
    gate = hidden // 2
    per = gate // width
    groups = hidden // GROUP
    rows = -(-(slots + 6) // BLOCK) * BLOCK
    spare = rows - slots
    pairwise = devices * BLOCK == width and devices >= 16 and devices & (devices - 1) == 0
    links = Tree(devices) if pairwise else Plain(width, gate)

    def blocks_of(layer):
        if pairwise:
            return pack_blocks(in_weight[layer], out_weight[layer], 1)[0]
        return in_weight[layer], out_weight[layer]

    owner = links.owners()
    pieces = [links.gather(blocks_of(layer)) for layer in range(2)]

    valid = mask.astype(F32)
    padded = lambda array: jnp.pad(array.reshape(images, slots, width), ((0, 0), (0, spare), (0, 0)))
    valid_column = jnp.pad(valid, ((0, 0), (0, spare)))[:, :, None]
    live = (jnp.arange(rows) < slots).astype(F32)[:, None]
    values = padded(tokens)
    layers, spatial = [], []
    for layer in range(2):
        layers.append(
            {
                "b_in": 0.5 * in_bias[layer][None],
                "gain_one": 0.5 * ln1_gain[layer][None],
                "bias_one": 0.5 * ln1_bias[layer][None],
                "gain_two": ln2_gain[layer][None],
                "bias_two": ln2_bias[layer][None],
                "b_out": out_bias[layer][None],
            }
        )
        spatial.append(
            spatial_operands(
                valid, spatial_weight[layer], spatial_bias[layer], ln2_gain[layer], ln2_bias[layer], rows
            )
        )
    flat = lambda array: array.reshape(images * rows, array.shape[2])
    mixer, back, pad = zip(*spatial)

    kept = forward_save(values, valid_column, live, mixer[0], pad[0], layers[0], owner, pieces[0], slots)
    last, last_sums = forward_backward(
        kept["values"], padded(cotangent), valid_column, live, mixer[1], back[1], pad[1], layers[1], owner, pieces[1], slots
    )

    def small_of(sums):
        cut = slots // BLOCK * BLOCK
        column = lambda name: sums[name].sum(0)
        at = slots - cut
        parts = (
            0.5 * column("gain_one"),
            0.5 * column("bias_one"),
            0.5 * column("b_in"),
            column("gain_two"),
            sums["bias_two"][at] + sums["bias_two"][at + 1],
            sums["spatial"][:slots, :slots].T.reshape(-1),
            sums["spatial"][slots, :slots],
            column("b_out"),
        )
        joined = jnp.concatenate(parts)
        size = joined.shape[0]
        full = -(-size // 2048) * 2048
        summed = links.total(jnp.pad(joined, (0, full - size)).reshape(2, -1, 128)).reshape(-1)
        ends, start = [], 0
        for part in parts:
            ends.append(summed[start : start + part.shape[0]])
            start += part.shape[0]
        ends[5] = ends[5].reshape(slots, slots)
        return ends

    mine, theirs = in_weight_blocks(owner, flat(last["normed"]), flat(last["hidden_grad"]), 0, groups, groups + per)
    mine, theirs = out_weight_blocks(owner, flat(last["gated"]), flat(last["masked"]), (mine, theirs))
    in_grad_one, out_grad_one = links.rows(links.scatter(mine, theirs), groups)
    small_one = small_of(last_sums)

    hidden_grad, masked, sums = backward_gate(
        last["upstream"], kept, valid_column, back[0], layers[0], owner, pieces[0], slots
    )
    mine, theirs = out_weight_blocks(owner, flat(kept["gated"]), flat(masked))
    (out_grad_zero,) = links.rows(links.scatter(mine, theirs), 0)
    mine, theirs = in_weight_blocks(owner, flat(kept["normed"]), flat(hidden_grad), 0, groups, groups)
    (in_grad_zero,) = links.rows(links.scatter(mine, theirs), groups)
    input_grad, sums["gain_one"], sums["bias_one"] = backward_first(
        values, hidden_grad, last["upstream"], layers[0], owner, pieces[0]
    )
    small_zero = small_of(sums)

    unpadded = lambda array: array[:, :slots].reshape(images * slots, width)
    small = [jnp.stack(pair) for pair in zip(small_zero, small_one)]
    return (
        unpadded(last["values"]),
        unpadded(input_grad),
        small[0],
        small[1],
        jnp.stack([in_grad_zero, in_grad_one]),
        small[2],
        small[3],
        small[4],
        small[5],
        small[6],
        jnp.stack([out_grad_zero, out_grad_one]),
        small[7],
    )


def solution(mesh):
    both = P(AXES, None)
    second = P(None, AXES, None)
    in_specs = (both, both, P(), P(), second, P(), P(), P(), P(), P(), second, P(), both)
    out_specs = (both, both, P(), P(), second, P(), P(), P(), P(), P(), second, P())
    return jax.shard_map(shards, mesh=mesh, in_specs=in_specs, out_specs=out_specs, check_vma=False)
```

```python
import jax
import jax.numpy as jnp
import numpy as np
from jax import lax
from jax.experimental import pallas as pl
from jax.experimental.pallas import tpu as pltpu
from jax.sharding import PartitionSpec as P

EPS = 1e-05
AXES = ("wide", "narrow")
F32 = jnp.float32
BF16 = jnp.bfloat16
TANH_ONE = 2 * 0.7978845608028654
TANH_THREE = 8 * 0.7978845608028654 * 0.044715
COLUMNS = 256
BLOCK = 16
GROUP = 512
STRIP = 256
WEIGHTS = ("b_in", "gain_one", "bias_one", "gain_two", "bias_two")
SUMS = ("b_out", "b_left", "b_right", "spatial", "gain_two", "bias_two", "gain_one", "bias_one")


def dot(a, b):
    return jnp.dot(a, b, preferred_element_type=F32)


def dot_last(a, b):
    return lax.dot_general(a, b, (((1,), (1,)), ((), ())), preferred_element_type=F32)


def dot_first(a, b):
    return lax.dot_general(a, b, (((0,), (0,)), ((), ())), preferred_element_type=F32)


def gelu_pair(half):
    square = half * half
    tanh = jnp.tanh(half * (TANH_ONE + TANH_THREE * square))
    upper = 1.0 + tanh
    value = half * upper
    slope = upper + value * (1.0 - tanh) * (TANH_ONE + (3 * TANH_THREE) * square)
    return value, slope


def fold_rows(values):
    total = values[:8]
    for row in range(8, values.shape[0], 8):
        total = total + values[row : row + 8]
    return total


def fold_columns(values):
    total = values[:, :128]
    for column in range(128, values.shape[1], 128):
        total = total + values[:, column : column + 128]
    return total


def white_of(values):
    centred = values - jnp.mean(values, -1, keepdims=True)
    inverse = lax.rsqrt(jnp.mean(centred * centred, -1, keepdims=True) + EPS)
    return centred * inverse, inverse


def cuts(width):
    return [slice(c, c + COLUMNS) for c in range(0, width, COLUMNS)]


def in_columns(w_in, start):
    at = start % GROUP
    return w_in[start // GROUP, :, at : at + COLUMNS]


def forward_image(values, live, mixer, slot_pad, w, t, slots):
    rows = values.shape[0]
    half_width = t["white"].shape[1]
    cut = slots // BLOCK * BLOCK
    white_one, unused_inverse = white_of(values)
    t["normed"][...] = (white_one * w["gain_one"][...] + w["bias_one"][...]).astype(BF16)
    total = None
    for sl in cuts(half_width):
        at = half_width + sl.start
        half = dot(t["normed"][...], in_columns(w["w_in"], at)) + w["b_in"][:, at : at + COLUMNS]
        value, slope = gelu_pair(half)
        t["right"][:, sl] = value
        t["right_slope"][:, sl] = slope.astype(BF16)
        part = fold_columns(value)
        total = part if total is None else total + part
    average = jnp.sum(total, -1, keepdims=True) * (1.0 / half_width)
    total = None
    for sl in cuts(half_width):
        centred = t["right"][:, sl] - average
        part = fold_columns(centred * centred)
        total = part if total is None else total + part
    spread = jnp.sum(total, -1, keepdims=True) * (1.0 / half_width)
    inverse = lax.rsqrt(spread + EPS) * live
    row = lax.broadcasted_iota(jnp.int32, (rows - cut, COLUMNS), 0)
    for sl in cuts(half_width):
        white = (t["right"][:, sl] - average) * inverse
        t["white"][:, sl] = white.astype(BF16)
        slot_in = white * w["gain_two"][:, sl] + w["bias_two"][:, sl]
        t["slot_in"][:cut, sl] = slot_in[:cut].astype(BF16)
        last = jnp.where(row < slots - cut, slot_in[cut:], slot_pad[:, sl])
        t["slot_in"][cut:, sl] = last.astype(BF16)
    for sl in cuts(half_width):
        half = dot(t["normed"][...], in_columns(w["w_in"], sl.start)) + w["b_in"][:, sl]
        left, slope = gelu_pair(half)
        mixed = dot(mixer, t["slot_in"][:, sl])
        t["gated"][:, sl] = (left * mixed).astype(BF16)
        t["left"][:, sl] = left.astype(BF16)
        t["left_slope"][:, sl] = (mixed * slope).astype(BF16)
    return inverse


def add_branch(values, gated, valid, w_out, b_out):
    branch = dot(gated, w_out[...].reshape(gated.shape[1], -1)) * valid
    return values + (branch + b_out[...])


def backward_left(upstream, w_out, left, left_slope, mixed_grad, hidden_grad, b_in_sum):
    for sl in cuts(mixed_grad.shape[1]):
        blocks = slice(sl.start // BLOCK, sl.stop // BLOCK)
        gated_grad = dot_last(upstream, w_out[blocks].reshape(COLUMNS, -1))
        mixed_grad[:, sl] = (gated_grad * left[:, sl].astype(F32)).astype(BF16)
        left_grad = gated_grad * left_slope[:, sl].astype(F32)
        hidden_grad[:, sl] = left_grad.astype(BF16)
        b_in_sum[:, sl] += fold_rows(left_grad)


def backward_right(valid, mixer_back, inverse, gain_two, t, hidden_grad, b_in_sum, sums, slots):
    rows = valid.shape[0]
    half_width = t["white"].shape[1]
    cut = slots // BLOCK * BLOCK
    outer = dot_last(t["slot_in"][...], t["mixed_grad"][...])
    is_slot = lax.broadcasted_iota(jnp.int32, (rows, 1), 0) < slots
    sums["spatial"][:rows, :rows] += outer * jnp.where(is_slot, valid, 1.0)
    back = mixer_back.astype(F32)
    by_bias = outer[slots + 2 : slots + 3] + outer[slots + 3 : slots + 4]
    by_gain = outer[slots + 4 : slots + 5] + outer[slots + 5 : slots + 6]
    mean_scaled = jnp.sum(back * by_gain, -1, keepdims=True) * (1.0 / half_width)
    mean_white = jnp.sum(back * (outer - by_bias), -1, keepdims=True) * (1.0 / half_width)
    for sl in cuts(half_width):
        slot_grad = dot(mixer_back, t["mixed_grad"][:, sl])
        white = t["white"][:, sl].astype(F32)
        sums["gain_two"][:, sl] += fold_rows(slot_grad * white)
        sums["bias_two"][:, sl] += slot_grad[cut:]
        scaled = slot_grad * gain_two[:, sl] - mean_scaled - white * mean_white
        right_grad = scaled * inverse * t["right_slope"][:, sl].astype(F32)
        hidden_grad[:, sl] = right_grad.astype(BF16)
        b_in_sum[:, sl] += fold_rows(right_grad)


def backward_norm(values, halves, upstream, w, sums):
    white, inverse = white_of(values)
    normed_grad = None
    per_half = w["w_in"].shape[0] // 2
    for group in range(2 * per_half):
        at = group % per_half * GROUP
        part = dot_last(halves[group // per_half][:, at : at + GROUP], w["w_in"][group])
        normed_grad = part if normed_grad is None else normed_grad + part
    sums["gain_one"][...] += fold_rows(normed_grad * white)
    sums["bias_one"][...] += fold_rows(normed_grad)
    scaled = normed_grad * w["gain_one"][...]
    mean = jnp.mean(scaled, -1, keepdims=True)
    mean_white = jnp.mean(scaled * white, -1, keepdims=True)
    return upstream + inverse * (scaled - mean - white * mean_white)


def load_blocks(owner, pieces, places, sem):
    position = 0
    for piece in pieces:
        blocks = piece.shape[0]

        def start(at, carry, piece=piece, position=position):
            block = owner[position + at]
            for first, ref in places:
                if ref.shape[1] == BLOCK:
                    count = ref.shape[0] * BLOCK // ref.shape[2]
                    target = ref.at[pl.ds(block * count, count)]
                else:
                    count = ref.shape[0]
                    target = ref.at[:, pl.ds(pl.multiple_of(block * BLOCK, BLOCK), BLOCK)]
                pltpu.make_async_copy(piece.at[at, first : first + count], target, sem).start()
            return carry

        lax.fori_loop(0, blocks, start, 0)
        position += blocks
    for unused, ref in places:
        pltpu.make_async_copy(ref, ref, sem).wait()


def put_weight_grads(owner, jobs, result, stage, outs, sem):
    half = stage.shape[1]

    def send(group, rows):
        for side in range(2):
            for at in range(half):
                stage[side, at, group] = result[rows(owner[side * half + at])]
            pltpu.make_async_copy(stage.at[side, :, group], outs[side].at[:, group], sem).start()

    for left, right, place in jobs:
        if left.shape[1] > right.shape[1]:
            for start in range(0, left.shape[1], GROUP):
                stop = start + GROUP
                result[start:stop] = dot_first(left[:, start:stop], right[...]).astype(BF16)
            per = left.shape[1] // right.shape[1]
            for part in range(per):
                spot = lambda block: pl.ds(pl.multiple_of((block * per + part) * BLOCK, BLOCK), BLOCK)
                send(place + part, spot)
        else:
            for group in range(right.shape[1] // GROUP):
                columns = slice(group * GROUP, (group + 1) * GROUP)
                result[: left.shape[1]] = dot_first(left[...], right[:, columns]).astype(BF16)
                send(place + group, lambda block: pl.ds(pl.multiple_of(block * BLOCK, BLOCK), BLOCK))
    for side in range(2):
        pltpu.make_async_copy(stage.at[side], outs[side], sem).wait()


def zero(refs):
    for ref in refs:
        ref[...] = jnp.zeros_like(ref)


def whole(shape):
    return pl.BlockSpec(shape, lambda *i: (0,) * len(shape))


def image(rows, columns):
    return pl.BlockSpec((1, rows, columns), lambda i, *unused: (i, 0, 0))


def anywhere(count):
    return [pl.BlockSpec(memory_space=pl.ANY)] * count


def call(kernel, name, grid, in_specs, outs, out_specs, scratch, flops, megabytes, table=0, aliases=None):
    return pl.pallas_call(
        kernel,
        grid_spec=pltpu.PrefetchScalarGridSpec(
            num_scalar_prefetch=table,
            grid=grid,
            in_specs=in_specs,
            out_specs=out_specs,
            scratch_shapes=scratch,
        ),
        out_shape=[jax.ShapeDtypeStruct(shape, dtype) for shape, dtype in outs],
        input_output_aliases=aliases or {},
        compiler_params=pltpu.CompilerParams(vmem_limit_bytes=megabytes << 20),
        cost_estimate=pl.CostEstimate(flops=flops, bytes_accessed=20_000_000, transcendentals=0),
        name=name,
    )


def in_scratch(width, hidden):
    return pltpu.VMEM((hidden // GROUP, width, GROUP), BF16)


def out_scratch(width, hidden):
    return pltpu.VMEM((hidden // 2 // BLOCK, BLOCK, width), BF16)


def strips_of(rows, gate):
    strips = gate // STRIP
    return strips, -(-rows // strips // 8) * 8


def sum_shapes(rows, width, hidden, slots):
    strips, high = strips_of(rows, hidden // 2)
    return {
        "b_out": (8, width),
        "b_left": (8, hidden // 2),
        "b_right": (8, hidden // 2),
        "spatial": (strips * high, STRIP),
        "gain_two": (8, hidden // 2),
        "bias_two": (rows - slots // BLOCK * BLOCK, hidden // 2),
        "gain_one": (8, width),
        "bias_one": (8, width),
    }


def forward_save(values, live, mixer, slot_pad, w, owner, pieces, place, slots, first, count, into=()):
    images, rows, width = values.shape
    hidden = w["b_in"].shape[1]
    gate = hidden // 2
    outs = {name: (gate, BF16) for name in KEPT[:6]}
    outs["normed"] = (width, BF16)
    outs["inverse"] = (1, F32)
    n_w, n_p, n_o, n_i = len(WEIGHTS), len(pieces), len(outs), len(into)

    def kernel(owner_ref, values_ref, live_ref, mixer_ref, pad_ref, *refs):
        weights = dict(zip(WEIGHTS, refs[:n_w]))
        rest = refs[n_w + n_p + n_i :]
        out = dict(zip(outs, rest[:n_o]))
        right, weights["w_in"], sem = rest[n_o:]

        @pl.when(pl.program_id(0) == 0)
        def _():
            load_blocks(owner_ref, refs[n_w : n_w + n_p], [(place, weights["w_in"])], sem)

        kept = {name: ref.at[0] for name, ref in out.items()}
        kept["right"] = right
        here = values_ref[0].astype(F32)
        out["inverse"][0] = forward_image(here, live_ref[...], mixer_ref[0], pad_ref, weights, kept, slots)

    some = lambda columns: pl.BlockSpec((1, rows, columns), lambda i, *unused: (first + i, 0, 0))
    results = call(
        kernel,
        "forward_save",
        (count,),
        [some(width), whole((rows, 1)), some(rows), whole(slot_pad.shape)]
        + [whole(w[name].shape) for name in WEIGHTS]
        + anywhere(n_p + n_i),
        [((images, rows, columns), dtype) for columns, dtype in outs.values()],
        [some(columns) for columns, unused in outs.values()],
        [pltpu.VMEM((rows, gate), F32), in_scratch(width, hidden), pltpu.SemaphoreType.DMA],
        2_000_000_000 * count,
        60,
        table=1,
        aliases={5 + n_w + n_p + at: at for at in range(n_i)},
    )(owner, values, live, mixer, slot_pad, *[w[name] for name in WEIGHTS], *pieces, *into)
    return results


KEPT = ("left", "left_slope", "white", "right_slope", "slot_in", "gated", "normed", "inverse")


def forward_backward(
    values, kept_before, b_out, cotangent, valid, live, mixer, mixer_back, slot_pad, w, owner, pieces, places, slots
):
    images, rows, width = values.shape
    hidden = w["b_in"].shape[1]
    gate = hidden // 2
    groups, per, half = hidden // GROUP, gate // width, width // BLOCK // 2
    outs = {
        "values": (width, BF16),
        "upstream": (width, F32),
        "left_grad_before": (gate, BF16),
        "mixed_grad_before": (gate, BF16),
    }
    shapes = sum_shapes(rows, width, hidden, slots)
    shapes = {name: shapes[name] for name in SUMS} | {
        "b_out_before": shapes["b_out"],
        "b_left_before": shapes["b_left"],
    }
    image_scratch = {"right": F32} | dict.fromkeys(
        ("left", "left_slope", "white", "right_slope", "slot_in", "mixed_grad"), BF16
    )
    all_scratch = {
        "normed": width,
        "gated": gate,
        "hidden_grad": hidden,
        "masked": width,
        "normed_before": width,
        "gated_before": gate,
        "left_grad_before": gate,
        "masked_before": width,
    }
    reads = ("gated", "left", "left_slope", "normed")
    last_shape = (half, groups + per, BLOCK, GROUP)
    before_shape = (half, groups // 2 + per, BLOCK, GROUP)
    n_w, n_p, n_o, n_s, n_r = len(WEIGHTS), len(pieces), len(outs), len(shapes), len(reads)

    def kernel(owner_ref, values_ref, b_out_ref, cot_ref, valid_ref, live_ref, mixer_ref, back_ref, pad_ref, *refs):
        before = {name: ref.at[0] for name, ref in zip(reads, refs)}
        refs = refs[n_r:]
        weights = dict(zip(WEIGHTS, refs[:n_w]))
        rest = refs[n_w + n_p :]
        out = {name: ref.at[0] for name, ref in zip(outs, rest)}
        sums = dict(zip(shapes, rest[n_o:]))
        last_outs, before_outs = rest[n_o + n_s :][:2], rest[n_o + n_s + 2 :][:2]
        rest = rest[n_o + n_s + 4 :]
        kept = dict(zip(image_scratch, rest))
        rest = rest[len(image_scratch) :]
        every = dict(zip(all_scratch, rest))
        w_out_before, weights["w_in"], weights["w_out"], result, last_stage, before_stage, sem, out_sem = rest[len(every) :]
        step = pl.program_id(0)

        @pl.when(step == 0)
        def _():
            targets = (w_out_before, weights["w_in"], weights["w_out"])
            load_blocks(owner_ref, refs[n_w : n_w + n_p], list(zip(places, targets)), sem)
            zero(sums.values())

        mine = pl.ds(pl.multiple_of(step * rows, BLOCK), rows)
        here = {name: ref.at[mine] for name, ref in every.items()}
        kept["normed"], kept["gated"] = here["normed"], here["gated"]
        left_grad, right_grad = (here["hidden_grad"].at[:, at : at + gate] for at in (0, gate))
        here["normed_before"][...] = before["normed"][...]
        here["gated_before"][...] = before["gated"][...]
        valid_column = valid_ref[0]
        inputs = add_branch(values_ref[0].astype(F32), before["gated"][...], valid_column, w_out_before, b_out_ref.at[:1])
        inverse = forward_image(inputs, live_ref[...], mixer_ref[0], pad_ref, weights, kept, slots)
        outputs = add_branch(inputs, kept["gated"][...], valid_column, weights["w_out"], b_out_ref.at[1:])
        out["values"][...] = outputs.astype(BF16)
        upstream = cot_ref[0].astype(F32)
        sums["b_out"][...] += fold_rows(upstream)
        masked = (upstream * valid_column).astype(BF16)
        here["masked"][...] = masked
        backward_left(
            masked, weights["w_out"], kept["left"], kept["left_slope"], kept["mixed_grad"], left_grad, sums["b_left"]
        )
        backward_right(
            valid_column, back_ref[0], inverse, weights["gain_two"], kept, right_grad, sums["b_right"], sums, slots
        )
        upstream = backward_norm(inputs, (left_grad, right_grad), upstream, weights, sums)
        out["upstream"][...] = upstream
        branch_grad = upstream.astype(BF16).astype(F32)
        sums["b_out_before"][...] += fold_rows(branch_grad)
        masked = (branch_grad * valid_column).astype(BF16)
        here["masked_before"][...] = masked
        backward_left(
            masked,
            w_out_before,
            before["left"],
            before["left_slope"],
            out["mixed_grad_before"],
            here["left_grad_before"],
            sums["b_left_before"],
        )
        out["left_grad_before"][...] = here["left_grad_before"][...]

        @pl.when(step == images - 1)
        def _():
            jobs = [(every["normed"], every["hidden_grad"], 0), (every["gated"], every["masked"], groups)]
            put_weight_grads(owner_ref, jobs, result, last_stage, last_outs, out_sem.at[0])
            jobs = [
                (every["normed_before"], every["left_grad_before"], 0),
                (every["gated_before"], every["masked_before"], groups // 2),
            ]
            put_weight_grads(owner_ref, jobs, result, before_stage, before_outs, out_sem.at[1])

    results = call(
        kernel,
        "forward_backward",
        (images,),
        [image(rows, width), whole(b_out.shape), image(rows, width), image(rows, 1), whole((rows, 1))]
        + [image(rows, rows), image(rows, rows), whole(slot_pad.shape)]
        + [image(rows, kept_before[name].shape[2]) for name in reads]
        + [whole(w[name].shape) for name in WEIGHTS]
        + anywhere(n_p),
        [((images, rows, columns), dtype) for columns, dtype in outs.values()]
        + [(shape, F32) for shape in shapes.values()]
        + [(last_shape, BF16)] * 2
        + [(before_shape, BF16)] * 2,
        [image(rows, columns) for columns, unused in outs.values()]
        + [whole(shape) for shape in shapes.values()]
        + anywhere(4),
        [pltpu.VMEM((rows, gate), dtype) for dtype in image_scratch.values()]
        + [pltpu.VMEM((images * rows, columns), BF16) for columns in all_scratch.values()]
        + [out_scratch(width, hidden), in_scratch(width, hidden), out_scratch(width, hidden)]
        + [pltpu.VMEM((gate, GROUP), BF16), pltpu.VMEM((2,) + last_shape, BF16), pltpu.VMEM((2,) + before_shape, BF16)]
        + [pltpu.SemaphoreType.DMA, pltpu.SemaphoreType.DMA((2,))],
        40_000_000_000,
        60,
        table=1,
    )(
        owner,
        values,
        b_out,
        cotangent,
        valid,
        live,
        mixer,
        mixer_back,
        slot_pad,
        *[kept_before[name] for name in reads],
        *[w[name] for name in WEIGHTS],
        *pieces,
    )
    blocks = results[n_o + n_s :]
    return dict(zip(outs, results)), dict(zip(shapes, results[n_o:])), blocks[:2], blocks[2:]


def backward_slots(kept, mixed_grad, valid, mixer_back, w, owner, slots):
    images, rows, gate = mixed_grad.shape
    width = w["gain_one"].shape[1]
    half = width // BLOCK // 2
    shapes = sum_shapes(rows, width, 2 * gate, slots)
    names = ("b_right", "spatial", "gain_two", "bias_two")
    reads = ("white", "right_slope", "slot_in", "inverse", "normed")
    block_shape = (half, gate // GROUP, BLOCK, GROUP)
    n_r, n_s = len(reads), len(names)

    def kernel(owner_ref, mixed_ref, valid_ref, back_ref, gain_two, *refs):
        t = {name: ref.at[0] for name, ref in zip(reads, refs)}
        t["mixed_grad"] = mixed_ref.at[0]
        out, sums, outs = refs[n_r], dict(zip(names, refs[n_r + 1 :])), refs[n_r + 1 + n_s :][:2]
        normed, right_grad, result, stage, out_sem = refs[n_r + 3 + n_s :]
        step = pl.program_id(0)

        @pl.when(step == 0)
        def _():
            zero(sums.values())

        mine = pl.ds(pl.multiple_of(step * rows, BLOCK), rows)
        normed[mine] = t["normed"][...]
        here = right_grad.at[mine]
        backward_right(valid_ref[0], back_ref[0], t["inverse"][...], gain_two, t, here, sums["b_right"], sums, slots)
        out[0] = here[...]

        @pl.when(step == images - 1)
        def _():
            put_weight_grads(owner_ref, [(normed, right_grad, 0)], result, stage, outs, out_sem)

    results = call(
        kernel,
        "backward_slots",
        (images,),
        [image(rows, gate), image(rows, 1), image(rows, rows), whole((1, gate))]
        + [image(rows, kept[name].shape[2]) for name in reads],
        [((images, rows, gate), BF16)] + [(shapes[name], F32) for name in names] + [(block_shape, BF16)] * 2,
        [image(rows, gate)] + [whole(shapes[name]) for name in names] + anywhere(2),
        [pltpu.VMEM((images * rows, width), BF16), pltpu.VMEM((images * rows, gate), BF16)]
        + [pltpu.VMEM((width, GROUP), BF16), pltpu.VMEM((2,) + block_shape, BF16), pltpu.SemaphoreType.DMA],
        9_000_000_000,
        60,
        table=1,
    )(owner, mixed_grad, valid, mixer_back, w["gain_two"], *[kept[name] for name in reads])
    return results[0], dict(zip(names, results[1:])), results[1 + n_s :]


def backward_first(values, left_grad, right_grad, upstream, w, owner, pieces, place):
    images, rows, width = values.shape
    gate = left_grad.shape[2]
    n_p = len(pieces)

    def kernel(owner_ref, values_ref, left_ref, right_ref, up_ref, gain_ref, *refs):
        out, line, gain_sum, bias_sum, w_in, sem = refs[n_p:]
        step = pl.program_id(0)

        @pl.when(step == 0)
        def _():
            load_blocks(owner_ref, refs[:n_p], [(place, w_in)], sem)
            zero((gain_sum, bias_sum))

        weights = {"w_in": w_in, "gain_one": gain_ref}
        sums = {"gain_one": gain_sum, "bias_one": bias_sum}
        out[0] = backward_norm(values_ref[0].astype(F32), (left_ref.at[0], right_ref.at[0]), up_ref[0], weights, sums)

        @pl.when(step == images - 1)
        def _():
            line[...] = jnp.zeros_like(line)
            for at, ref in enumerate((gain_sum, bias_sum)):
                line[5:6, (1 + at) * width : (2 + at) * width] = 0.5 * jnp.sum(ref[...], 0, keepdims=True)

    return call(
        kernel,
        "backward_first",
        (images,),
        [image(rows, width), image(rows, gate), image(rows, gate), image(rows, width), whole((1, width))]
        + anywhere(n_p),
        [((images, rows, width), F32), ((8, gate), F32)],
        [image(rows, width), whole((8, gate))],
        [pltpu.VMEM((8, width), F32)] * 2 + [in_scratch(width, 2 * gate), pltpu.SemaphoreType.DMA],
        6_000_000_000,
        60,
        table=1,
    )(owner, values, left_grad, right_grad, upstream, w["gain_one"], *pieces)


def pack_sums(both, slots):
    gate = both[0]["gain_two"].shape[1]
    rows = slots // BLOCK * BLOCK + both[0]["bias_two"].shape[0]
    strips, high = strips_of(rows, gate)
    at = slots % BLOCK
    flat = [(block, name) for block in range(2) for name in SUMS if name in both[block]]

    def kernel(*refs):
        out = refs[-1]
        row = lax.broadcasted_iota(jnp.int32, (8, gate), 0)
        for block in range(2):
            sums = {name: ref for (at_block, name), ref in zip(flat, refs) if at_block == block}
            out[block, :high] = jnp.concatenate(
                [sums["spatial"][strip * high : (strip + 1) * high] for strip in range(strips)], 1
            )
            one = lambda name: jnp.sum(sums[name][...], 0, keepdims=True)
            narrow = one("b_out")
            if "gain_one" in sums:
                narrow = jnp.concatenate([narrow, 0.5 * one("gain_one"), 0.5 * one("bias_one")], 1)
            bias_two = sums["bias_two"][at : at + 1] + sums["bias_two"][at + 1 : at + 2]
            lines = [0.5 * one("b_left"), 0.5 * one("b_right"), one("gain_two"), bias_two]
            total = jnp.zeros((8, gate), F32)
            for place, line in enumerate(lines):
                total = jnp.where(row == place, line, total)
            out[block, high:] = total
            out[block, high + 4 : high + 5, : narrow.shape[1]] = narrow

    return pl.pallas_call(
        kernel,
        out_shape=jax.ShapeDtypeStruct((2, high + 8, gate), F32),
        compiler_params=pltpu.CompilerParams(vmem_limit_bytes=60 << 20),
        name="pack_sums",
    )(*[both[block][name] for block, name in flat])


def unpack_sums(odd, mine, theirs, slots, width):
    gate = mine.shape[1]
    high = mine.shape[0] - 8
    strips = gate // STRIP

    def kernel(odd_ref, mine_ref, theirs_ref, gain_one, bias_one, b_in, gain_two, bias_two, spatial, b_sp, b_out):
        is_odd = odd_ref[0] == 1
        held = mine_ref[...].astype(F32), theirs_ref[...].astype(F32)
        for block in range(2):
            value = jnp.where(is_odd, held[1 - block], held[block])
            square = [value[:high, strip * STRIP : (strip + 1) * STRIP] for strip in range(strips)]
            square = jnp.concatenate(square + [jnp.zeros((STRIP, STRIP), F32)], 0)[:STRIP]
            b_sp[block : block + 1] = square[slots : slots + 1, :slots]
            spatial[:, block, :] = square.T[:slots, :slots]
            line = lambda place: value[high + place : high + place + 1]
            b_in[block : block + 1, :gate] = line(0)
            b_in[block : block + 1, gate:] = line(1)
            gain_two[block : block + 1] = line(2)
            bias_two[block : block + 1] = line(3)
            narrow = line(4)
            if block == 0:
                narrow = narrow + (held[0][high + 5 : high + 6] + held[1][high + 5 : high + 6])
            for place, out in enumerate((b_out, gain_one, bias_one)):
                out[block : block + 1] = narrow[:, place * width : (place + 1) * width]

    shapes = [(2, width), (2, width), (2, 2 * gate), (2, gate), (2, gate), (slots, 2, slots), (2, slots), (2, width)]
    results = pl.pallas_call(
        kernel,
        in_specs=[pl.BlockSpec(memory_space=pltpu.SMEM)] + [pl.BlockSpec(memory_space=pltpu.VMEM)] * 2,
        out_shape=[jax.ShapeDtypeStruct(shape, F32) for shape in shapes],
        compiler_params=pltpu.CompilerParams(vmem_limit_bytes=60 << 20),
        name="unpack_sums",
    )(odd, mine, theirs)
    return [*results[:5], results[5].transpose(1, 0, 2), *results[6:]]


def add_blocks(chains, places, groups, per):
    counts = [len(chain) for chain in chains]
    flat = [array for chain in chains for array in chain]
    width = flat[0].shape[-1]

    def kernel(*refs):
        in_out, out_out = refs[-2:]
        start = 0
        for count, spots in zip(counts, places):
            for at, (block, group) in enumerate(spots):
                total = None
                for ref in refs[start : start + count]:
                    part = (ref[0, at] if len(ref.shape) == 4 else ref[at]).astype(F32)
                    total = part if total is None else total + part
                if group < groups:
                    in_out[block, :, group * GROUP : (group + 1) * GROUP] = total
                else:
                    first = (group - groups) * BLOCK
                    out_out[block, first : first + BLOCK] = total
            start += count

    def spec(array):
        if array.ndim == 4:
            return pl.BlockSpec((1,) + array.shape[1:], lambda i: (0, 0, 0, 0))
        return pl.BlockSpec(array.shape, lambda i: (0, 0, 0))

    shapes = [(2, BLOCK, groups * GROUP), (2, per * BLOCK, width)]
    return pl.pallas_call(
        kernel,
        grid=(1,),
        in_specs=[spec(array) for array in flat],
        out_specs=[whole(shape) for shape in shapes],
        out_shape=[jax.ShapeDtypeStruct(shape, F32) for shape in shapes],
        compiler_params=pltpu.CompilerParams(vmem_limit_bytes=60 << 20),
        name="add_blocks",
    )(*flat)


class Tree:
    def __init__(self, devices):
        self.devices = devices
        far = [1 << bit for bit in range(3, devices.bit_length() - 1)]
        self.bits = far + [2, 4], far[::-1] + [4, 2]
        self.steps = len(far) + 2

    def swap(self, values, *steps):
        bits = [sum(bits[step] for step in steps) or 1 for bits in self.bits]
        return lax.ppermute(values, AXES, [(i, i ^ bits[i % 2]) for i in range(self.devices)])

    def owners(self):
        offsets = np.zeros((2, 1 << self.steps), np.int32)
        for core in range(2):
            for step in range(self.steps):
                offsets[core] ^= (np.arange(1 << self.steps, dtype=np.int32) >> step & 1) * self.bits[core][step]
        me = lax.axis_index(AXES).astype(jnp.int32)
        odd = me % 2 == 1
        mine = me ^ jnp.where(odd, offsets[1], offsets[0])
        theirs = (me ^ 1) ^ jnp.where(odd, offsets[0], offsets[1])
        return jnp.concatenate([mine, theirs])

    def gather(self, own):
        held = pack_blocks(own, 1)
        far = self.steps - 2
        got = [
            self.swap(held, *[step for step in range(far) if index >> step & 1]) for index in range(1, 1 << far)
        ]
        wait = yield held, got
        held = jnp.concatenate(after([held, *got], wait))
        first, second = self.swap(held, far), self.swap(held, far + 1)
        wait = yield held, (first, second)
        last = self.swap(after(first, wait), far + 1)
        pieces = [held, first, second]
        others = [self.swap(piece) for piece in pieces]
        wait = yield held, last
        last = after(last, wait)
        yield [*pieces, last, *others, self.swap(last)]

    def scatter(self, mine, theirs):
        parts = [mine, self.swap(theirs)]
        wait = yield theirs, parts[1]
        for step in reversed(range(self.steps)):
            keep = 1 << step
            sent = self.add(after(parts, wait), slice(keep, 2 * keep)).astype(BF16)
            parts.append(self.swap(sent, step))
            wait = yield sent, parts[-1]
        yield parts

    def add(self, parts, at):
        total = parts[0][at].astype(F32)
        for part in parts[1:]:
            total = total + part[at].astype(F32)
        return total

    def finish(self, chains, places, groups, per):
        return add_blocks(chains, places, groups, per)

    def total(self, values):
        odd = lax.axis_index("narrow") % 2
        mine = jnp.where(odd == 1, values[1], values[0]).astype(BF16)
        theirs = jnp.where(odd == 1, values[0], values[1]).astype(BF16)
        got = self.swap(theirs)
        late = yield theirs, got
        wait = None
        for step in [*reversed(range(self.steps)), -1]:
            got = after(got, wait)
            mine = mine.astype(F32) + got.astype(F32)
            if step == self.steps - 1:
                mine = mine + jnp.pad(late, ((mine.shape[0] - late.shape[0], 0), (0, 0)))
            mine = mine.astype(BF16)
            got = self.swap(mine, *([step] if step >= 0 else []))
            wait = yield mine, got
        yield odd, mine, got


class Plain:
    def __init__(self, width, gate):
        self.width, self.gate = width, gate
        self.steps = 4
        self.blocks = width // BLOCK

    def owners(self):
        return jnp.arange(self.blocks, dtype=jnp.int32)

    def gather(self, own):
        gathered = [lax.all_gather(part, AXES, axis=0, tiled=True) for part in own]
        for unused in range(3):
            yield gathered, gathered
        yield [pack_blocks(gathered, self.blocks)]

    def scatter(self, mine, theirs):
        for unused in range(self.steps + 1):
            yield theirs, mine
        yield jnp.concatenate([mine, theirs]).astype(F32)

    def finish(self, chains, places, groups, per):
        spots = {spot: chain[:, at] for chain, place in zip(chains, places) for at, spot in enumerate(place)}
        in_grad, out_grad = [], []
        for block in range(2):
            inner = jnp.concatenate([spots[block, group] for group in range(groups)], 2)
            outer = jnp.concatenate([spots[block, groups + part] for part in range(per)], 1)
            in_grad.append(inner.reshape(self.width, -1))
            out_grad.append(outer.reshape(self.gate, -1))
        return [
            lax.psum_scatter(jnp.stack(grad), AXES, scatter_dimension=1, tiled=True) for grad in (in_grad, out_grad)
        ]

    def total(self, values):
        late = yield values, values
        late = jnp.pad(late, ((values.shape[1] - late.shape[0], 0), (0, 0)))
        values = lax.psum(jnp.stack([values[0] + late, values[1]]), AXES)
        for unused in range(self.steps + 1):
            yield values, values
        yield jnp.int32(0), values[0], values[1]


def pack_blocks(parts, blocks):
    packed = []
    for part in parts:
        if part.shape[1] > GROUP:
            packed.append(part.reshape(blocks, BLOCK, -1, GROUP).transpose(0, 2, 1, 3))
        else:
            packed.append(part.reshape(blocks, -1, BLOCK, GROUP))
    return jnp.concatenate(packed, 1)


def after(values, *others):
    return lax.optimization_barrier((values, others))[0] if others != (None,) else values


def bfloat_pair(values):
    top = lax.reduce_precision(values, 8, 7)
    return top.astype(BF16), lax.reduce_precision(values - top, 8, 7).astype(BF16)


def spatial_operands(valid, w_sp, b_sp, gain_two, bias_two, rows):
    images, slots = valid.shape
    gate = gain_two.shape[0]
    cut = slots // BLOCK * BLOCK
    spare = rows - slots
    masked = w_sp[None] * valid[:, None, :].astype(BF16)
    bias = jnp.broadcast_to(jnp.stack(bfloat_pair(b_sp), -1)[None], (images, slots, 2))
    mixer = jnp.concatenate([masked, bias], 2)
    mixer = jnp.pad(mixer, ((0, 0), (0, spare), (0, spare - 2)))
    column_sum = jnp.einsum("ir,pr->ip", valid.astype(BF16), w_sp, preferred_element_type=F32)
    back = jnp.concatenate([jnp.swapaxes(masked, 1, 2), jnp.stack(bfloat_pair(column_sum), 1)], 1)
    back = jnp.pad(back, ((0, 0), (0, spare - 2), (0, spare)))
    one = jnp.ones((gate,), BF16)
    pad = jnp.stack([one, one, *bfloat_pair(bias_two), *bfloat_pair(gain_two)])
    pad = jnp.pad(pad, ((slots - cut, rows - slots - 6), (0, 0))).astype(F32)
    return mixer, back, pad


def shards(
    tokens,
    mask,
    ln1_gain,
    ln1_bias,
    in_weight,
    in_bias,
    ln2_gain,
    ln2_bias,
    spatial_weight,
    spatial_bias,
    out_weight,
    out_bias,
    cotangent,
):
    devices = lax.axis_size(AXES)
    images, slots = mask.shape
    width = tokens.shape[1]
    hidden = in_weight.shape[2]
    gate = hidden // 2
    per = gate // width
    groups = hidden // GROUP
    rows = -(-(slots + 6) // BLOCK) * BLOCK
    spare = rows - slots
    pairwise = devices * BLOCK == width and devices >= 16 and devices & (devices - 1) == 0
    links = Tree(devices) if pairwise else Plain(width, gate)

    owner = links.owners()
    gather_one = links.gather([in_weight[0]])
    unused, got = next(gather_one)
    gather_rest = links.gather(after([out_weight[0], in_weight[1], out_weight[1]], got))
    unused, got = next(gather_rest)
    next(gather_one)
    gather_one.send(got)
    pieces_one = gather_one.send(None)
    column_rest, got_rest = gather_rest.send(None)

    valid = mask.astype(F32)
    padded = lambda array: jnp.pad(array.reshape(images, slots, width), ((0, 0), (0, spare), (0, 0)))
    valid_column = jnp.pad(valid, ((0, 0), (0, spare)))[:, :, None]
    live = (jnp.arange(rows) < slots).astype(F32)[:, None]
    values = padded(tokens)
    layers, spatial = [], []
    for layer in range(2):
        layers.append(
            {
                "b_in": 0.5 * in_bias[layer][None],
                "gain_one": 0.5 * ln1_gain[layer][None],
                "bias_one": 0.5 * ln1_bias[layer][None],
                "gain_two": ln2_gain[layer][None],
                "bias_two": ln2_bias[layer][None],
                "b_out": out_bias[layer][None],
            }
        )
        spatial.append(
            spatial_operands(
                valid, spatial_weight[layer], spatial_bias[layer], ln2_gain[layer], ln2_bias[layer], rows
            )
        )
    cot = padded(cotangent)
    mixer, back, pad = zip(*spatial)

    halfway = images * 2 // 5
    save = lambda array, start, count, into: forward_save(
        array, live, mixer[0], pad[0], layers[0], owner, pieces_one, 0, slots, start, count, into
    )
    kept = save(after(values, column_rest), 0, halfway, ())
    gather_rest.send(kept[0])
    ahead = got_rest[0], valid_column, cot, mixer[1], back, pad[1]
    kept = save(after(values, ahead), halfway, images - halfway, kept)
    pieces_rest = gather_rest.send(kept[0])
    kept = dict(zip(KEPT, kept))
    last, last_sums, last_blocks, before_blocks = forward_backward(
        values,
        kept,
        out_bias,
        cot,
        valid_column,
        live,
        mixer[1],
        back[1],
        pad[1],
        layers[1],
        owner,
        pieces_rest,
        (0, per, per + groups),
        slots,
    )

    one = links.scatter(*last_blocks)
    sent, got_one = next(one)
    left = links.scatter(before_blocks[0], after(before_blocks[1], sent))
    sent, got_left = next(left)
    sent, got_one = one.send(sent)
    right_grad, sums, blocks = backward_slots(
        kept, after(last["mixed_grad_before"], sent), valid_column, back[0], layers[0], owner, slots
    )
    sums["b_out"], sums["b_left"] = last_sums["b_out_before"], last_sums["b_left_before"]
    right = links.scatter(*after(blocks, got_one, got_left))
    sent, got_right = next(right)
    sent, got_left = left.send(sent)
    sent, got_one = one.send(sent)
    small = links.total(pack_sums((sums, last_sums), slots))
    sent_small, got_small = next(small)
    input_grad, late = after(
        backward_first(
            values,
            last["left_grad_before"],
            right_grad,
            after(last["upstream"], sent, sent_small),
            layers[0],
            owner,
            pieces_one,
            0,
        ),
        got_right,
        got_left,
        got_one,
        got_small,
    )
    sent = input_grad
    for turn in range(links.steps):
        for chain, turns in ((right, 0), (left, 1), (one, 2)):
            if turn + turns < links.steps:
                sent, unused = chain.send(sent)
        unused, sent_small = small.send(late if turn == 0 else sent)
    small.send(None)
    small_sent = small.send(None)
    chains = [next(chain) for chain in (one, left, right)]
    odd, *summed = small_sent
    steps = groups // 2
    places = (
        [(1, group) for group in range(groups + per)],
        [(0, group) for group in range(steps)] + [(0, groups + part) for part in range(per)],
        [(0, steps + group) for group in range(steps)],
    )
    in_grad, out_grad = links.finish(chains, places, groups, per)
    gain_one, bias_one, b_in, gain_two, bias_two, spatial_grad, b_sp, b_out = unpack_sums(
        odd.reshape(1), *summed, slots, width
    )

    unpadded = lambda array: array[:, :slots].reshape(images * slots, width)
    return (
        unpadded(last["values"]),
        unpadded(input_grad),
        gain_one,
        bias_one,
        in_grad,
        b_in,
        gain_two,
        bias_two,
        spatial_grad,
        b_sp,
        out_grad,
        b_out,
    )


def solution(mesh):
    both = P(AXES, None)
    second = P(None, AXES, None)
    in_specs = (both, both, P(), P(), second, P(), P(), P(), P(), P(), second, P(), both)
    out_specs = (both, both, P(), P(), second, P(), P(), P(), P(), P(), second, P())
    return jax.shard_map(shards, mesh=mesh, in_specs=in_specs, out_specs=out_specs, check_vma=False)
```

```python
import jax
import jax.numpy as jnp
import numpy as np
from jax import lax
from jax.experimental import pallas as pl
from jax.experimental.pallas import tpu as pltpu
from jax.sharding import PartitionSpec as P

EPS = 1e-05
AXES = ("wide", "narrow")
F32 = jnp.float32
BF16 = jnp.bfloat16
TANH_ONE = 2 * 0.7978845608028654
TANH_THREE = 8 * 0.7978845608028654 * 0.044715
COLUMNS = 256
BLOCK = 16
GROUP = 512
STRIP = 256
WEIGHTS = ("b_in", "gain_one", "bias_one", "gain_two", "bias_two")
SUMS = ("b_out", "b_left", "b_right", "spatial", "gain_two", "bias_two", "gain_one", "bias_one")


def dot(a, b):
    return jnp.dot(a, b, preferred_element_type=F32)


def dot_last(a, b):
    return lax.dot_general(a, b, (((1,), (1,)), ((), ())), preferred_element_type=F32)


def dot_first(a, b):
    return lax.dot_general(a, b, (((0,), (0,)), ((), ())), preferred_element_type=F32)


def gelu_pair(half):
    square = half * half
    tanh = jnp.tanh(half * (TANH_ONE + TANH_THREE * square))
    upper = 1.0 + tanh
    value = half * upper
    slope = upper + value * (1.0 - tanh) * (TANH_ONE + (3 * TANH_THREE) * square)
    return value, slope


def fold_rows(values):
    total = values[:8]
    for row in range(8, values.shape[0], 8):
        total = total + values[row : row + 8]
    return total


def fold_columns(values):
    total = values[:, :128]
    for column in range(128, values.shape[1], 128):
        total = total + values[:, column : column + 128]
    return total


def white_of(values):
    centred = values - jnp.mean(values, -1, keepdims=True)
    inverse = lax.rsqrt(jnp.mean(centred * centred, -1, keepdims=True) + EPS)
    return centred * inverse, inverse


def cuts(width):
    return [slice(c, c + COLUMNS) for c in range(0, width, COLUMNS)]


def in_columns(w_in, start):
    at = start % GROUP
    return w_in[start // GROUP, :, at : at + COLUMNS]


def forward_image(values, live, mixer, slot_pad, w, t, slots):
    rows = values.shape[0]
    half_width = t["white"].shape[1]
    cut = slots // BLOCK * BLOCK
    white_one, unused_inverse = white_of(values)
    t["normed"][...] = (white_one * w["gain_one"][...] + w["bias_one"][...]).astype(BF16)
    total = None
    for sl in cuts(half_width):
        at = half_width + sl.start
        half = dot(t["normed"][...], in_columns(w["w_in"], at)) + w["b_in"][:, at : at + COLUMNS]
        value, slope = gelu_pair(half)
        t["right"][:, sl] = value
        t["right_slope"][:, sl] = slope.astype(BF16)
        part = fold_columns(value)
        total = part if total is None else total + part
    average = jnp.sum(total, -1, keepdims=True) * (1.0 / half_width)
    total = None
    for sl in cuts(half_width):
        centred = t["right"][:, sl] - average
        part = fold_columns(centred * centred)
        total = part if total is None else total + part
    spread = jnp.sum(total, -1, keepdims=True) * (1.0 / half_width)
    inverse = lax.rsqrt(spread + EPS) * live
    row = lax.broadcasted_iota(jnp.int32, (rows - cut, COLUMNS), 0)
    for sl in cuts(half_width):
        white = (t["right"][:, sl] - average) * inverse
        t["white"][:, sl] = white.astype(BF16)
        slot_in = white * w["gain_two"][:, sl] + w["bias_two"][:, sl]
        t["slot_in"][:cut, sl] = slot_in[:cut].astype(BF16)
        last = jnp.where(row < slots - cut, slot_in[cut:], slot_pad[:, sl])
        t["slot_in"][cut:, sl] = last.astype(BF16)
    for sl in cuts(half_width):
        half = dot(t["normed"][...], in_columns(w["w_in"], sl.start)) + w["b_in"][:, sl]
        left, slope = gelu_pair(half)
        mixed = dot(mixer, t["slot_in"][:, sl])
        t["gated"][:, sl] = (left * mixed).astype(BF16)
        t["left"][:, sl] = left.astype(BF16)
        t["left_slope"][:, sl] = (mixed * slope).astype(BF16)
    return inverse


def add_branch(values, gated, valid, w_out, b_out):
    branch = dot(gated, w_out[...].reshape(gated.shape[1], -1)) * valid
    return values + (branch + b_out[...])


def backward_left(upstream, w_out, left, left_slope, mixed_grad, hidden_grad, b_in_sum):
    for sl in cuts(mixed_grad.shape[1]):
        blocks = slice(sl.start // BLOCK, sl.stop // BLOCK)
        gated_grad = dot_last(upstream, w_out[blocks].reshape(COLUMNS, -1))
        mixed_grad[:, sl] = (gated_grad * left[:, sl].astype(F32)).astype(BF16)
        left_grad = gated_grad * left_slope[:, sl].astype(F32)
        hidden_grad[:, sl] = left_grad.astype(BF16)
        b_in_sum[:, sl] += fold_rows(left_grad)


def backward_right(valid, mixer_back, inverse, gain_two, t, hidden_grad, b_in_sum, sums, slots):
    rows = valid.shape[0]
    half_width = t["white"].shape[1]
    cut = slots // BLOCK * BLOCK
    outer = dot_last(t["slot_in"][...], t["mixed_grad"][...])
    is_slot = lax.broadcasted_iota(jnp.int32, (rows, 1), 0) < slots
    sums["spatial"][:rows, :rows] += outer * jnp.where(is_slot, valid, 1.0)
    back = mixer_back.astype(F32)
    by_bias = outer[slots + 2 : slots + 3] + outer[slots + 3 : slots + 4]
    by_gain = outer[slots + 4 : slots + 5] + outer[slots + 5 : slots + 6]
    mean_scaled = jnp.sum(back * by_gain, -1, keepdims=True) * (1.0 / half_width)
    mean_white = jnp.sum(back * (outer - by_bias), -1, keepdims=True) * (1.0 / half_width)
    for sl in cuts(half_width):
        slot_grad = dot(mixer_back, t["mixed_grad"][:, sl])
        white = t["white"][:, sl].astype(F32)
        sums["gain_two"][:, sl] += fold_rows(slot_grad * white)
        sums["bias_two"][:, sl] += slot_grad[cut:]
        scaled = slot_grad * gain_two[:, sl] - mean_scaled - white * mean_white
        right_grad = scaled * inverse * t["right_slope"][:, sl].astype(F32)
        hidden_grad[:, sl] = right_grad.astype(BF16)
        b_in_sum[:, sl] += fold_rows(right_grad)


def backward_norm(values, halves, upstream, w, sums):
    white, inverse = white_of(values)
    normed_grad = None
    per_half = w["w_in"].shape[0] // 2
    for group in range(2 * per_half):
        at = group % per_half * GROUP
        part = dot_last(halves[group // per_half][:, at : at + GROUP], w["w_in"][group])
        normed_grad = part if normed_grad is None else normed_grad + part
    sums["gain_one"][...] += fold_rows(normed_grad * white)
    sums["bias_one"][...] += fold_rows(normed_grad)
    scaled = normed_grad * w["gain_one"][...]
    mean = jnp.mean(scaled, -1, keepdims=True)
    mean_white = jnp.mean(scaled * white, -1, keepdims=True)
    return upstream + inverse * (scaled - mean - white * mean_white)


def load_blocks(owner, pieces, places, sem):
    position = 0
    for piece in pieces:
        blocks = piece.shape[0]

        def start(at, carry, piece=piece, position=position):
            block = owner[position + at]
            for first, ref in places:
                if ref.shape[1] == BLOCK:
                    count = ref.shape[0] * BLOCK // ref.shape[2]
                    target = ref.at[pl.ds(block * count, count)]
                else:
                    count = ref.shape[0]
                    target = ref.at[:, pl.ds(pl.multiple_of(block * BLOCK, BLOCK), BLOCK)]
                pltpu.make_async_copy(piece.at[at, first : first + count], target, sem).start()
            return carry

        lax.fori_loop(0, blocks, start, 0)
        position += blocks
    for unused, ref in places:
        pltpu.make_async_copy(ref, ref, sem).wait()


def put_weight_grads(owner, jobs, result, stage, outs, sem):
    half = stage.shape[1]

    def send(group, rows):
        for side in range(2):
            for at in range(half):
                stage[side, at, group] = result[rows(owner[side * half + at])]
            pltpu.make_async_copy(stage.at[side, :, group], outs[side].at[:, group], sem).start()

    for left, right, place in jobs:
        if left.shape[1] > right.shape[1]:
            for start in range(0, left.shape[1], GROUP):
                stop = start + GROUP
                result[start:stop] = dot_first(left[:, start:stop], right[...]).astype(BF16)
            per = left.shape[1] // right.shape[1]
            for part in range(per):
                spot = lambda block: pl.ds(pl.multiple_of((block * per + part) * BLOCK, BLOCK), BLOCK)
                send(place + part, spot)
        else:
            for group in range(right.shape[1] // GROUP):
                columns = slice(group * GROUP, (group + 1) * GROUP)
                result[: left.shape[1]] = dot_first(left[...], right[:, columns]).astype(BF16)
                send(place + group, lambda block: pl.ds(pl.multiple_of(block * BLOCK, BLOCK), BLOCK))
    for side in range(2):
        pltpu.make_async_copy(stage.at[side], outs[side], sem).wait()


def put_sums(both, slots, outs, odd):
    gate = both[0]["gain_two"].shape[1]
    rows = slots // BLOCK * BLOCK + both[0]["bias_two"].shape[0]
    strips, high = strips_of(rows, gate)
    at = slots % BLOCK
    row = lax.broadcasted_iota(jnp.int32, (8, gate), 0)
    packed = []
    for sums in both:
        one = lambda name: jnp.sum(sums[name][...], 0, keepdims=True)
        bias_two = sums["bias_two"][at : at + 1] + sums["bias_two"][at + 1 : at + 2]
        narrow = [one("b_out")]
        if "gain_one" in sums:
            narrow += [0.5 * one("gain_one"), 0.5 * one("bias_one")]
        filled = sum(part.shape[1] for part in narrow)
        if filled < gate:
            narrow.append(jnp.zeros((1, gate - filled), F32))
        narrow = jnp.concatenate(narrow, 1)
        lines = [0.5 * one("b_left"), 0.5 * one("b_right"), one("gain_two"), bias_two, narrow]
        total = jnp.zeros((8, gate), F32)
        for place, line in enumerate(lines):
            total = jnp.where(row == place, line, total)
        square = [sums["spatial"][strip * high : (strip + 1) * high] for strip in range(strips)]
        packed.append(jnp.concatenate([jnp.concatenate(square, 1), total], 0).astype(BF16))
    outs[0][...] = jnp.where(odd, packed[1], packed[0])
    outs[1][...] = jnp.where(odd, packed[0], packed[1])


def zero(refs):
    for ref in refs:
        ref[...] = jnp.zeros_like(ref)


def whole(shape):
    return pl.BlockSpec(shape, lambda *i: (0,) * len(shape))


def image(rows, columns):
    return pl.BlockSpec((1, rows, columns), lambda i, *unused: (i, 0, 0))


def anywhere(count):
    return [pl.BlockSpec(memory_space=pl.ANY)] * count


def call(kernel, name, grid, in_specs, outs, out_specs, scratch, flops, megabytes, table=0, aliases=None):
    return pl.pallas_call(
        kernel,
        grid_spec=pltpu.PrefetchScalarGridSpec(
            num_scalar_prefetch=table,
            grid=grid,
            in_specs=in_specs,
            out_specs=out_specs,
            scratch_shapes=scratch,
        ),
        out_shape=[jax.ShapeDtypeStruct(shape, dtype) for shape, dtype in outs],
        input_output_aliases=aliases or {},
        compiler_params=pltpu.CompilerParams(vmem_limit_bytes=megabytes << 20),
        cost_estimate=pl.CostEstimate(flops=flops, bytes_accessed=20_000_000, transcendentals=0),
        name=name,
    )


def in_scratch(width, hidden):
    return pltpu.VMEM((hidden // GROUP, width, GROUP), BF16)


def out_scratch(width, hidden):
    return pltpu.VMEM((hidden // 2 // BLOCK, BLOCK, width), BF16)


def strips_of(rows, gate):
    strips = gate // STRIP
    return strips, -(-rows // strips // 8) * 8


def sum_shapes(rows, width, hidden, slots):
    strips, high = strips_of(rows, hidden // 2)
    return {
        "b_out": (8, width),
        "b_left": (8, hidden // 2),
        "b_right": (8, hidden // 2),
        "spatial": (strips * high, STRIP),
        "gain_two": (8, hidden // 2),
        "bias_two": (rows - slots // BLOCK * BLOCK, hidden // 2),
        "gain_one": (8, width),
        "bias_one": (8, width),
    }


def forward_save(values, live, mixer, slot_pad, w, owner, pieces, place, slots, first, count, into=()):
    images, rows, width = values.shape
    hidden = w["b_in"].shape[1]
    gate = hidden // 2
    outs = {name: (gate, BF16) for name in KEPT[:6]}
    outs["normed"] = (width, BF16)
    outs["inverse"] = (1, F32)
    n_w, n_p, n_o, n_i = len(WEIGHTS), len(pieces), len(outs), len(into)

    def kernel(owner_ref, values_ref, live_ref, mixer_ref, pad_ref, *refs):
        weights = dict(zip(WEIGHTS, refs[:n_w]))
        rest = refs[n_w + n_p + n_i :]
        out = dict(zip(outs, rest[:n_o]))
        right, weights["w_in"], sem = rest[n_o:]

        @pl.when(pl.program_id(0) == 0)
        def _():
            load_blocks(owner_ref, refs[n_w : n_w + n_p], [(place, weights["w_in"])], sem)

        kept = {name: ref.at[0] for name, ref in out.items()}
        kept["right"] = right
        here = values_ref[0].astype(F32)
        out["inverse"][0] = forward_image(here, live_ref[...], mixer_ref[0], pad_ref, weights, kept, slots)

    some = lambda columns: pl.BlockSpec((1, rows, columns), lambda i, *unused: (first + i, 0, 0))
    results = call(
        kernel,
        "forward_save",
        (count,),
        [some(width), whole((rows, 1)), some(rows), whole(slot_pad.shape)]
        + [whole(w[name].shape) for name in WEIGHTS]
        + anywhere(n_p + n_i),
        [((images, rows, columns), dtype) for columns, dtype in outs.values()],
        [some(columns) for columns, unused in outs.values()],
        [pltpu.VMEM((rows, gate), F32), in_scratch(width, hidden), pltpu.SemaphoreType.DMA],
        2_000_000_000 * count,
        60,
        table=1,
        aliases={5 + n_w + n_p + at: at for at in range(n_i)},
    )(owner, values, live, mixer, slot_pad, *[w[name] for name in WEIGHTS], *pieces, *into)
    return results


KEPT = ("left", "left_slope", "white", "right_slope", "slot_in", "gated", "normed", "inverse")


def forward_backward(
    values, kept_before, b_out, cotangent, valid, live, mixer, mixer_back, slot_pad, w, owner, pieces, places, slots
):
    images, rows, width = values.shape
    hidden = w["b_in"].shape[1]
    gate = hidden // 2
    groups, per, half = hidden // GROUP, gate // width, width // BLOCK // 2
    outs = {
        "values": (width, BF16),
        "upstream": (width, F32),
        "left_grad_before": (gate, BF16),
        "mixed_grad_before": (gate, BF16),
    }
    shapes = sum_shapes(rows, width, hidden, slots)
    shapes = {name: shapes[name] for name in SUMS} | {
        "b_out_before": shapes["b_out"],
        "b_left_before": shapes["b_left"],
    }
    image_scratch = {"right": F32} | dict.fromkeys(
        ("left", "left_slope", "white", "right_slope", "slot_in", "mixed_grad"), BF16
    )
    all_scratch = {
        "normed": width,
        "gated": gate,
        "hidden_grad": hidden,
        "masked": width,
        "normed_before": width,
        "gated_before": gate,
        "left_grad_before": gate,
        "masked_before": width,
    }
    reads = ("gated", "left", "left_slope", "normed")
    last_shape = (half, groups + per, BLOCK, GROUP)
    before_shape = (half, groups // 2 + per, BLOCK, GROUP)
    n_w, n_p, n_o, n_s, n_r = len(WEIGHTS), len(pieces), len(outs), len(shapes), len(reads)

    def kernel(owner_ref, values_ref, b_out_ref, cot_ref, valid_ref, live_ref, mixer_ref, back_ref, pad_ref, *refs):
        before = {name: ref.at[0] for name, ref in zip(reads, refs)}
        refs = refs[n_r:]
        weights = dict(zip(WEIGHTS, refs[:n_w]))
        rest = refs[n_w + n_p :]
        out = {name: ref.at[0] for name, ref in zip(outs, rest)}
        sums = dict(zip(shapes, rest[n_o:]))
        last_outs, before_outs = rest[n_o + n_s :][:2], rest[n_o + n_s + 2 :][:2]
        rest = rest[n_o + n_s + 4 :]
        kept = dict(zip(image_scratch, rest))
        rest = rest[len(image_scratch) :]
        every = dict(zip(all_scratch, rest))
        w_out_before, weights["w_in"], weights["w_out"], result, last_stage, before_stage, sem, out_sem = rest[len(every) :]
        step = pl.program_id(0)

        @pl.when(step == 0)
        def _():
            targets = (w_out_before, weights["w_in"], weights["w_out"])
            load_blocks(owner_ref, refs[n_w : n_w + n_p], list(zip(places, targets)), sem)
            zero(sums.values())

        mine = pl.ds(pl.multiple_of(step * rows, BLOCK), rows)
        here = {name: ref.at[mine] for name, ref in every.items()}
        kept["normed"], kept["gated"] = here["normed"], here["gated"]
        left_grad, right_grad = (here["hidden_grad"].at[:, at : at + gate] for at in (0, gate))
        here["normed_before"][...] = before["normed"][...]
        here["gated_before"][...] = before["gated"][...]
        valid_column = valid_ref[0]
        inputs = add_branch(values_ref[0].astype(F32), before["gated"][...], valid_column, w_out_before, b_out_ref.at[:1])
        inverse = forward_image(inputs, live_ref[...], mixer_ref[0], pad_ref, weights, kept, slots)
        outputs = add_branch(inputs, kept["gated"][...], valid_column, weights["w_out"], b_out_ref.at[1:])
        out["values"][...] = outputs.astype(BF16)
        upstream = cot_ref[0].astype(F32)
        sums["b_out"][...] += fold_rows(upstream)
        masked = (upstream * valid_column).astype(BF16)
        here["masked"][...] = masked
        backward_left(
            masked, weights["w_out"], kept["left"], kept["left_slope"], kept["mixed_grad"], left_grad, sums["b_left"]
        )
        backward_right(
            valid_column, back_ref[0], inverse, weights["gain_two"], kept, right_grad, sums["b_right"], sums, slots
        )
        upstream = backward_norm(inputs, (left_grad, right_grad), upstream, weights, sums)
        out["upstream"][...] = upstream
        branch_grad = upstream.astype(BF16).astype(F32)
        sums["b_out_before"][...] += fold_rows(branch_grad)
        masked = (branch_grad * valid_column).astype(BF16)
        here["masked_before"][...] = masked
        backward_left(
            masked,
            w_out_before,
            before["left"],
            before["left_slope"],
            out["mixed_grad_before"],
            here["left_grad_before"],
            sums["b_left_before"],
        )
        out["left_grad_before"][...] = here["left_grad_before"][...]

        @pl.when(step == images - 1)
        def _():
            jobs = [(every["normed"], every["hidden_grad"], 0), (every["gated"], every["masked"], groups)]
            put_weight_grads(owner_ref, jobs, result, last_stage, last_outs, out_sem.at[0])
            jobs = [
                (every["normed_before"], every["left_grad_before"], 0),
                (every["gated_before"], every["masked_before"], groups // 2),
            ]
            put_weight_grads(owner_ref, jobs, result, before_stage, before_outs, out_sem.at[1])

    results = call(
        kernel,
        "forward_backward",
        (images,),
        [image(rows, width), whole(b_out.shape), image(rows, width), image(rows, 1), whole((rows, 1))]
        + [image(rows, rows), image(rows, rows), whole(slot_pad.shape)]
        + [image(rows, kept_before[name].shape[2]) for name in reads]
        + [whole(w[name].shape) for name in WEIGHTS]
        + anywhere(n_p),
        [((images, rows, columns), dtype) for columns, dtype in outs.values()]
        + [(shape, F32) for shape in shapes.values()]
        + [(last_shape, BF16)] * 2
        + [(before_shape, BF16)] * 2,
        [image(rows, columns) for columns, unused in outs.values()]
        + [whole(shape) for shape in shapes.values()]
        + anywhere(4),
        [pltpu.VMEM((rows, gate), dtype) for dtype in image_scratch.values()]
        + [pltpu.VMEM((images * rows, columns), BF16) for columns in all_scratch.values()]
        + [out_scratch(width, hidden), in_scratch(width, hidden), out_scratch(width, hidden)]
        + [pltpu.VMEM((gate, GROUP), BF16), pltpu.VMEM((2,) + last_shape, BF16), pltpu.VMEM((2,) + before_shape, BF16)]
        + [pltpu.SemaphoreType.DMA, pltpu.SemaphoreType.DMA((2,))],
        40_000_000_000,
        60,
        table=1,
    )(
        owner,
        values,
        b_out,
        cotangent,
        valid,
        live,
        mixer,
        mixer_back,
        slot_pad,
        *[kept_before[name] for name in reads],
        *[w[name] for name in WEIGHTS],
        *pieces,
    )
    blocks = results[n_o + n_s :]
    return dict(zip(outs, results)), dict(zip(shapes, results[n_o:])), blocks[:2], blocks[2:]


def backward_slots(kept, mixed_grad, valid, mixer_back, w, owner, both, slots):
    images, rows, gate = mixed_grad.shape
    width = w["gain_one"].shape[1]
    half = width // BLOCK // 2
    shapes = sum_shapes(rows, width, 2 * gate, slots)
    names = ("b_right", "spatial", "gain_two", "bias_two")
    reads = ("white", "right_slope", "slot_in", "inverse", "normed")
    block_shape = (half, gate // GROUP, BLOCK, GROUP)
    high = strips_of(rows, gate)[1]
    flat = [(block, name) for block in range(2) for name in both[block]]
    n_r, n_f, n_s = len(reads), len(flat), len(names)

    def kernel(owner_ref, mixed_ref, valid_ref, back_ref, gain_two, *refs):
        t = {name: ref.at[0] for name, ref in zip(reads, refs)}
        t["mixed_grad"] = mixed_ref.at[0]
        out, *outs = refs[n_r + n_f :][:5]
        rest = refs[n_r + n_f + 5 :]
        own = dict(zip(names, rest))
        normed, right_grad, result, stage, out_sem = rest[n_s:]
        step = pl.program_id(0)

        @pl.when(step == 0)
        def _():
            zero(own.values())

        mine = pl.ds(pl.multiple_of(step * rows, BLOCK), rows)
        normed[mine] = t["normed"][...]
        here = right_grad.at[mine]
        backward_right(valid_ref[0], back_ref[0], t["inverse"][...], gain_two, t, here, own["b_right"], own, slots)
        out[0] = here[...]

        @pl.when(step == images - 1)
        def _():
            put_weight_grads(owner_ref, [(normed, right_grad, 0)], result, stage, outs[:2], out_sem)
            sums = {}, {}
            for (block, name), ref in zip(flat, refs[n_r:]):
                sums[block][name] = ref
            sums[0].update(own)
            put_sums(sums, slots, outs[2:], owner_ref[0] % 2 == 1)

    results = call(
        kernel,
        "backward_slots",
        (images,),
        [image(rows, gate), image(rows, 1), image(rows, rows), whole((1, gate))]
        + [image(rows, kept[name].shape[2]) for name in reads]
        + [whole(both[block][name].shape) for block, name in flat],
        [((images, rows, gate), BF16)] + [(block_shape, BF16)] * 2 + [((high + 8, gate), BF16)] * 2,
        [image(rows, gate)] + anywhere(2) + [whole((high + 8, gate))] * 2,
        [pltpu.VMEM(shapes[name], F32) for name in names]
        + [pltpu.VMEM((images * rows, width), BF16), pltpu.VMEM((images * rows, gate), BF16)]
        + [pltpu.VMEM((width, GROUP), BF16), pltpu.VMEM((2,) + block_shape, BF16), pltpu.SemaphoreType.DMA],
        9_000_000_000,
        60,
        table=1,
    )(
        owner,
        mixed_grad,
        valid,
        mixer_back,
        w["gain_two"],
        *[kept[name] for name in reads],
        *[both[block][name] for block, name in flat],
    )
    return results[0], results[1:3], results[3:]


def backward_first(values, left_grad, right_grad, upstream, w, owner, pieces, place, slots):
    images, rows, width = values.shape
    gate = left_grad.shape[2]
    n_p = len(pieces)

    def kernel(owner_ref, values_ref, left_ref, right_ref, up_ref, gain_ref, *refs):
        out, line, gain_sum, bias_sum, w_in, sem = refs[n_p:]
        step = pl.program_id(0)

        @pl.when(step == 0)
        def _():
            load_blocks(owner_ref, refs[:n_p], [(place, w_in)], sem)
            zero((gain_sum, bias_sum))

        weights = {"w_in": w_in, "gain_one": gain_ref}
        own = {"gain_one": gain_sum, "bias_one": bias_sum}
        halves = left_ref.at[0], right_ref.at[0]
        result = backward_norm(values_ref[0].astype(F32), halves, up_ref[0], weights, own)
        for at in range(images):

            @pl.when(step == at)
            def _(at=at):
                out[at * slots : (at + 1) * slots] = result[:slots]

        @pl.when(step == images - 1)
        def _():
            zero((line,))
            for at, ref in enumerate((gain_sum, bias_sum)):
                line[5:6, (1 + at) * width : (2 + at) * width] = 0.5 * jnp.sum(ref[...], 0, keepdims=True)

    return call(
        kernel,
        "backward_first",
        (images,),
        [image(rows, width), image(rows, gate), image(rows, gate), image(rows, width), whole((1, width))]
        + anywhere(n_p),
        [((images * slots, width), F32), ((8, gate), F32)],
        [whole((images * slots, width)), whole((8, gate))],
        [pltpu.VMEM((8, width), F32)] * 2 + [in_scratch(width, 2 * gate), pltpu.SemaphoreType.DMA],
        6_000_000_000,
        60,
        table=1,
    )(owner, values, left_grad, right_grad, upstream, w["gain_one"], *pieces)


def unpack_sums(odd, mine, theirs, slots, width):
    gate = mine.shape[1]
    high = mine.shape[0] - 8
    strips = gate // STRIP

    def kernel(odd_ref, mine_ref, theirs_ref, gain_one, bias_one, b_in, gain_two, bias_two, spatial, b_sp, b_out):
        is_odd = odd_ref[0] == 1
        held = mine_ref[...].astype(F32), theirs_ref[...].astype(F32)
        for block in range(2):
            value = jnp.where(is_odd, held[1 - block], held[block])
            square = [value[:high, strip * STRIP : (strip + 1) * STRIP] for strip in range(strips)]
            square = jnp.concatenate(square + [jnp.zeros((STRIP, STRIP), F32)], 0)[:STRIP]
            b_sp[block : block + 1] = square[slots : slots + 1, :slots]
            spatial[:, block, :] = square.T[:slots, :slots]
            line = lambda place: value[high + place : high + place + 1]
            b_in[block : block + 1, :gate] = line(0)
            b_in[block : block + 1, gate:] = line(1)
            gain_two[block : block + 1] = line(2)
            bias_two[block : block + 1] = line(3)
            narrow = line(4)
            if block == 0:
                narrow = narrow + (held[0][high + 5 : high + 6] + held[1][high + 5 : high + 6])
            for place, out in enumerate((b_out, gain_one, bias_one)):
                out[block : block + 1] = narrow[:, place * width : (place + 1) * width]

    shapes = [(2, width), (2, width), (2, 2 * gate), (2, gate), (2, gate), (slots, 2, slots), (2, slots), (2, width)]
    results = pl.pallas_call(
        kernel,
        in_specs=[pl.BlockSpec(memory_space=pltpu.SMEM)] + [pl.BlockSpec(memory_space=pltpu.VMEM)] * 2,
        out_shape=[jax.ShapeDtypeStruct(shape, F32) for shape in shapes],
        compiler_params=pltpu.CompilerParams(vmem_limit_bytes=60 << 20),
        name="unpack_sums",
    )(odd, mine, theirs)
    return [*results[:5], results[5].transpose(1, 0, 2), *results[6:]]


def add_blocks(terms, groups, per):
    arrays = []
    for pairs in terms.values():
        arrays += [array for array, unused in pairs if not any(array is other for other in arrays)]
    index = {id(array): at for at, array in enumerate(arrays)}
    width = arrays[0].shape[-1]

    def kernel(*refs):
        in_out, out_out = refs[-2:]
        for (block, group), pairs in terms.items():
            total = None
            for array, at in pairs:
                part = refs[index[id(array)]][0, at].astype(F32)
                total = part if total is None else total + part
            if group < groups:
                in_out[block, :, group * GROUP : (group + 1) * GROUP] = total
            else:
                first = (group - groups) * BLOCK
                out_out[block, first : first + BLOCK] = total

    shapes = [(2, BLOCK, groups * GROUP), (2, per * BLOCK, width)]
    return pl.pallas_call(
        kernel,
        grid=(1,),
        in_specs=[pl.BlockSpec((1,) + array.shape[1:], lambda i: (0, 0, 0, 0)) for array in arrays],
        out_specs=[whole(shape) for shape in shapes],
        out_shape=[jax.ShapeDtypeStruct(shape, F32) for shape in shapes],
        compiler_params=pltpu.CompilerParams(vmem_limit_bytes=60 << 20),
        name="add_blocks",
    )(*arrays)


class Tree:
    def __init__(self, devices):
        self.devices = devices
        far = [1 << bit for bit in range(3, devices.bit_length() - 1)]
        self.bits = far + [2, 4], far[::-1] + [4, 2]
        self.steps = len(far) + 2

    def swap(self, values, *steps):
        bits = [sum(bits[step] for step in steps) or 1 for bits in self.bits]
        return lax.ppermute(values, AXES, [(i, i ^ bits[i % 2]) for i in range(self.devices)])

    def owners(self):
        offsets = np.zeros((2, 1 << self.steps), np.int32)
        for core in range(2):
            for step in range(self.steps):
                offsets[core] ^= (np.arange(1 << self.steps, dtype=np.int32) >> step & 1) * self.bits[core][step]
        me = lax.axis_index(AXES).astype(jnp.int32)
        odd = me % 2 == 1
        mine = me ^ jnp.where(odd, offsets[1], offsets[0])
        theirs = (me ^ 1) ^ jnp.where(odd, offsets[0], offsets[1])
        return jnp.concatenate([mine, theirs])

    def gather(self, own):
        held = pack_blocks(own, 1)
        far = self.steps - 2
        got = [
            self.swap(held, *[step for step in range(far) if index >> step & 1]) for index in range(1, 1 << far)
        ]
        wait = yield held, got
        held = jnp.concatenate(after([held, *got], wait))
        first, second = self.swap(held, far), self.swap(held, far + 1)
        wait = yield held, (first, second)
        last = self.swap(after(first, wait), far + 1)
        pieces = [held, first, second]
        others = [self.swap(piece) for piece in pieces]
        wait = yield held, last
        last = after(last, wait)
        yield [*pieces, last, *others, self.swap(last)]

    def sum(self, mine, theirs):
        return TreeSum(self, mine, theirs)

    def finish(self, terms, groups, per):
        return add_blocks(terms, groups, per)

    def total(self, mine, theirs):
        far = self.steps - 2
        order = [*reversed(range(far)), far, far + 1]
        add = lambda one, other: (one.astype(F32) + other.astype(F32)).astype(BF16)
        got = self.swap(theirs)
        wait = yield theirs
        mine = add(mine, after(got, wait))
        got = self.swap(mine, order[0])
        late = yield mine
        late = late.astype(BF16)
        late_got = self.swap(late, order[0])
        wait = yield late
        late = late.astype(F32) + late_got.astype(F32)
        mine = mine.astype(F32) + after(got, wait).astype(F32)
        mine = (mine + jnp.pad(late, ((mine.shape[0] - late.shape[0], 0), (0, 0)))).astype(BF16)
        for step in order[1:]:
            got = self.swap(mine, step)
            wait = yield mine
            mine = add(mine, after(got, wait))
        yield lax.axis_index("narrow") % 2, mine, self.swap(mine)


class TreeSum:
    def __init__(self, links, mine, theirs):
        self.links, self.step = links, links.steps
        self.sent, self.got = theirs, links.swap(theirs)
        self.columns, self.shared = [[mine, self.got]], []

    def add(self, at):
        total = []
        for column in self.columns:
            total.append(column[0][at].astype(F32))
            for part in column[1:]:
                total[-1] = total[-1] + part[at].astype(F32)
        total = jnp.concatenate(total, 1) if len(total) > 1 else total[0]
        for part in self.shared:
            total = total + part[at].astype(F32)
        return total

    def send(self, wait):
        self.columns, self.shared = after((self.columns, self.shared), wait)
        self.step -= 1
        keep = 1 << self.step
        self.sent = self.add(slice(keep, 2 * keep)).astype(BF16)
        self.got = self.links.swap(self.sent, self.step)
        (self.columns[0] if len(self.columns) == 1 else self.shared).append(self.got)
        return self.sent

    def join(self, other):
        self.columns = self.columns + other.columns
        return self

    def terms(self):
        terms = []
        for column in self.columns:
            for at in range(column[0].shape[1]):
                terms.append([(part, at) for part in column] + [(part, len(terms)) for part in self.shared])
        return terms


class PlainSum:
    def __init__(self, mine, theirs):
        self.blocks = jnp.concatenate([mine, theirs]).astype(F32)
        self.sent = self.got = theirs

    def send(self, wait):
        return self.sent

    def join(self, other):
        self.blocks = jnp.concatenate([self.blocks, other.blocks], 1)
        return self

    def terms(self):
        return [self.blocks[:, at] for at in range(self.blocks.shape[1])]


class Plain:
    def __init__(self, width, gate):
        self.width, self.gate = width, gate
        self.steps = 4
        self.blocks = width // BLOCK

    def owners(self):
        return jnp.arange(self.blocks, dtype=jnp.int32)

    def gather(self, own):
        gathered = [lax.all_gather(part, AXES, axis=0, tiled=True) for part in own]
        for unused in range(3):
            yield gathered, gathered
        yield [pack_blocks(gathered, self.blocks)]

    def sum(self, mine, theirs):
        return PlainSum(mine, theirs)

    def finish(self, terms, groups, per):
        in_grad, out_grad = [], []
        for block in range(2):
            inner = jnp.concatenate([terms[block, group] for group in range(groups)], 2)
            outer = jnp.concatenate([terms[block, groups + part] for part in range(per)], 1)
            in_grad.append(inner.reshape(self.width, -1))
            out_grad.append(outer.reshape(self.gate, -1))
        return [
            lax.psum_scatter(jnp.stack(grad), AXES, scatter_dimension=1, tiled=True) for grad in (in_grad, out_grad)
        ]

    def total(self, mine, theirs):
        yield mine
        late = yield mine
        mine = mine.astype(F32) + jnp.pad(late, ((mine.shape[0] - late.shape[0], 0), (0, 0)))
        yield late
        for unused in range(self.steps - 1):
            yield mine
        yield jnp.int32(0), *lax.psum((mine, theirs.astype(F32)), AXES)


def pack_blocks(parts, blocks):
    packed = []
    for part in parts:
        if part.shape[1] > GROUP:
            packed.append(part.reshape(blocks, BLOCK, -1, GROUP).transpose(0, 2, 1, 3))
        else:
            packed.append(part.reshape(blocks, -1, BLOCK, GROUP))
    return jnp.concatenate(packed, 1)


def after(values, *others):
    return lax.optimization_barrier((values, others))[0] if others != (None,) else values


def bfloat_pair(values):
    top = lax.reduce_precision(values, 8, 7)
    return top.astype(BF16), lax.reduce_precision(values - top, 8, 7).astype(BF16)


def spatial_operands(valid, w_sp, b_sp, gain_two, bias_two, rows):
    images, slots = valid.shape
    gate = gain_two.shape[0]
    cut = slots // BLOCK * BLOCK
    spare = rows - slots
    masked = w_sp[None] * valid[:, None, :].astype(BF16)
    bias = jnp.broadcast_to(jnp.stack(bfloat_pair(b_sp), -1)[None], (images, slots, 2))
    mixer = jnp.concatenate([masked, bias], 2)
    mixer = jnp.pad(mixer, ((0, 0), (0, spare), (0, spare - 2)))
    column_sum = jnp.einsum("ir,pr->ip", valid.astype(BF16), w_sp, preferred_element_type=F32)
    back = jnp.concatenate([jnp.swapaxes(masked, 1, 2), jnp.stack(bfloat_pair(column_sum), 1)], 1)
    back = jnp.pad(back, ((0, 0), (0, spare - 2), (0, spare)))
    one = jnp.ones((gate,), BF16)
    pad = jnp.stack([one, one, *bfloat_pair(bias_two), *bfloat_pair(gain_two)])
    pad = jnp.pad(pad, ((slots - cut, rows - slots - 6), (0, 0))).astype(F32)
    return mixer, back, pad


def shards(
    tokens,
    mask,
    ln1_gain,
    ln1_bias,
    in_weight,
    in_bias,
    ln2_gain,
    ln2_bias,
    spatial_weight,
    spatial_bias,
    out_weight,
    out_bias,
    cotangent,
):
    devices = lax.axis_size(AXES)
    images, slots = mask.shape
    width = tokens.shape[1]
    hidden = in_weight.shape[2]
    gate = hidden // 2
    per = gate // width
    groups = hidden // GROUP
    rows = -(-(slots + 6) // BLOCK) * BLOCK
    spare = rows - slots
    pairwise = devices * BLOCK == width and devices >= 16 and devices & (devices - 1) == 0
    links = Tree(devices) if pairwise else Plain(width, gate)

    owner = links.owners()
    gather_one = links.gather([in_weight[0]])
    unused, got = next(gather_one)
    gather_rest = links.gather(after([out_weight[0], in_weight[1], out_weight[1]], got))
    unused, got = next(gather_rest)
    next(gather_one)
    gather_one.send(got)
    pieces_one = gather_one.send(None)
    column_rest, got_rest = gather_rest.send(None)

    valid = mask.astype(F32)
    padded = lambda array: jnp.pad(array.reshape(images, slots, width), ((0, 0), (0, spare), (0, 0)))
    valid_column = jnp.pad(valid, ((0, 0), (0, spare)))[:, :, None]
    live = (jnp.arange(rows) < slots).astype(F32)[:, None]
    values = padded(tokens)
    layers, spatial = [], []
    for layer in range(2):
        layers.append(
            {
                "b_in": 0.5 * in_bias[layer][None],
                "gain_one": 0.5 * ln1_gain[layer][None],
                "bias_one": 0.5 * ln1_bias[layer][None],
                "gain_two": ln2_gain[layer][None],
                "bias_two": ln2_bias[layer][None],
                "b_out": out_bias[layer][None],
            }
        )
        spatial.append(
            spatial_operands(
                valid, spatial_weight[layer], spatial_bias[layer], ln2_gain[layer], ln2_bias[layer], rows
            )
        )
    cot = padded(cotangent)
    mixer, back, pad = zip(*spatial)

    halfway = images * 2 // 5
    save = lambda array, start, count, into: forward_save(
        array, live, mixer[0], pad[0], layers[0], owner, pieces_one, 0, slots, start, count, into
    )
    kept = save(after(values, column_rest), 0, halfway, ())
    gather_rest.send(kept[0])
    ahead = got_rest[0], valid_column, cot, mixer[1], back, pad[1]
    kept = save(after(values, ahead), halfway, images - halfway, kept)
    pieces_rest = gather_rest.send(kept[0])
    kept = dict(zip(KEPT, kept))
    last, last_sums, last_blocks, before_blocks = forward_backward(
        values,
        kept,
        out_bias,
        cot,
        valid_column,
        live,
        mixer[1],
        back[1],
        pad[1],
        layers[1],
        owner,
        pieces_rest,
        (0, per, per + groups),
        slots,
    )

    unpadded = lambda array: array[:, :slots].reshape(images * slots, width)
    one = links.sum(*last_blocks)
    left = links.sum(before_blocks[0], after(before_blocks[1], one.sent))
    layer_out = unpadded(after(last["values"], left.sent))
    sent = one.send((left.sent, layer_out))
    sums = {"b_out": last_sums.pop("b_out_before"), "b_left": last_sums.pop("b_left_before")}
    right_grad, blocks, packed = backward_slots(
        kept,
        after(last["mixed_grad_before"], sent),
        valid_column,
        back[0],
        layers[0],
        owner,
        (sums, last_sums),
        slots,
    )
    right = links.sum(*after(blocks, one.got, left.got))
    small = links.total(*packed)
    sent = next(small)
    sent = left.send((sent, right.sent))
    sent = one.send(sent)
    sent = right.send(sent)
    sent = small.send(sent)
    input_grad, line = backward_first(
        values, last["left_grad_before"], right_grad, after(last["upstream"], sent), layers[0], owner, pieces_one, 0, slots
    )
    line = after(line, left.got, one.got, right.got)
    sent = small.send(line)
    both = left.join(right)
    sent = both.send(sent)
    for step in range(links.steps - 2):
        sent = one.send(sent)
        sent = small.send(sent)
        sent = both.send(sent)
    for unused in range(2):
        small_end = small.send(sent)
    odd, *summed = small_end
    steps = groups // 2
    spots = [(1, group) for group in range(groups + per)]
    terms = dict(zip(spots, one.terms()))
    spots = [(0, group) for group in range(steps)] + [(0, groups + part) for part in range(per)]
    spots += [(0, steps + group) for group in range(steps)]
    terms |= zip(spots, both.terms())
    in_grad, out_grad = links.finish(terms, groups, per)
    gain_one, bias_one, b_in, gain_two, bias_two, spatial_grad, b_sp, b_out = unpack_sums(
        odd.reshape(1), *summed, slots, width
    )

    return (
        layer_out,
        input_grad,
        gain_one,
        bias_one,
        in_grad,
        b_in,
        gain_two,
        bias_two,
        spatial_grad,
        b_sp,
        out_grad,
        b_out,
    )


def solution(mesh):
    both = P(AXES, None)
    second = P(None, AXES, None)
    in_specs = (both, both, P(), P(), second, P(), P(), P(), P(), P(), second, P(), both)
    out_specs = (both, both, P(), P(), second, P(), P(), P(), P(), P(), second, P())
    return jax.shard_map(shards, mesh=mesh, in_specs=in_specs, out_specs=out_specs, check_vma=False)
```

```python
import jax
import jax.numpy as jnp
import numpy as np
from jax import lax
from jax.experimental import pallas as pl
from jax.experimental.pallas import tpu as pltpu
from jax.sharding import PartitionSpec as P

EPS = 1e-05
AXES = ("wide", "narrow")
F32 = jnp.float32
BF16 = jnp.bfloat16
TANH_ONE = 2 * 0.7978845608028654
TANH_THREE = 8 * 0.7978845608028654 * 0.044715
COLUMNS = 256
BLOCK = 16
GROUP = 512
STRIP = 256
WEIGHTS = ("b_in", "gain_one", "bias_one", "gain_two", "bias_two")
SUMS = ("b_out", "b_left", "b_right", "spatial", "gain_two", "bias_two", "gain_one", "bias_one")


def dot(a, b):
    return jnp.dot(a, b, preferred_element_type=F32)


def dot_last(a, b):
    return lax.dot_general(a, b, (((1,), (1,)), ((), ())), preferred_element_type=F32)


def dot_first(a, b):
    return lax.dot_general(a, b, (((0,), (0,)), ((), ())), preferred_element_type=F32)


def gelu_pair(half):
    square = half * half
    tanh = jnp.tanh(half * (TANH_ONE + TANH_THREE * square))
    upper = 1.0 + tanh
    value = half * upper
    slope = upper + value * (1.0 - tanh) * (TANH_ONE + (3 * TANH_THREE) * square)
    return value, slope


def fold_rows(values):
    total = values[:8]
    for row in range(8, values.shape[0], 8):
        total = total + values[row : row + 8]
    return total


def fold_columns(values):
    total = values[:, :128]
    for column in range(128, values.shape[1], 128):
        total = total + values[:, column : column + 128]
    return total


def white_of(values):
    centred = values - jnp.mean(values, -1, keepdims=True)
    inverse = lax.rsqrt(jnp.mean(centred * centred, -1, keepdims=True) + EPS)
    return centred * inverse, inverse


def cuts(width):
    return [slice(c, c + COLUMNS) for c in range(0, width, COLUMNS)]


def in_columns(w_in, start):
    at = start % GROUP
    return w_in[start // GROUP, :, at : at + COLUMNS]


def forward_image(values, live, mixer, slot_pad, w, t, slots):
    rows = values.shape[0]
    half_width = t["white"].shape[1]
    cut = slots // BLOCK * BLOCK
    white_one, unused_inverse = white_of(values)
    t["normed"][...] = (white_one * w["gain_one"][...] + w["bias_one"][...]).astype(BF16)
    total = None
    for sl in cuts(half_width):
        at = half_width + sl.start
        half = dot(t["normed"][...], in_columns(w["w_in"], at)) + w["b_in"][:, at : at + COLUMNS]
        value, slope = gelu_pair(half)
        t["right"][:, sl] = value
        t["right_slope"][:, sl] = slope.astype(BF16)
        part = fold_columns(value)
        total = part if total is None else total + part
    average = jnp.sum(total, -1, keepdims=True) * (1.0 / half_width)
    total = None
    for sl in cuts(half_width):
        centred = t["right"][:, sl] - average
        part = fold_columns(centred * centred)
        total = part if total is None else total + part
    spread = jnp.sum(total, -1, keepdims=True) * (1.0 / half_width)
    inverse = lax.rsqrt(spread + EPS) * live
    row = lax.broadcasted_iota(jnp.int32, (rows - cut, COLUMNS), 0)
    for sl in cuts(half_width):
        white = (t["right"][:, sl] - average) * inverse
        t["white"][:, sl] = white.astype(BF16)
        slot_in = white * w["gain_two"][:, sl] + w["bias_two"][:, sl]
        t["slot_in"][:cut, sl] = slot_in[:cut].astype(BF16)
        last = jnp.where(row < slots - cut, slot_in[cut:], slot_pad[:, sl])
        t["slot_in"][cut:, sl] = last.astype(BF16)
    for sl in cuts(half_width):
        half = dot(t["normed"][...], in_columns(w["w_in"], sl.start)) + w["b_in"][:, sl]
        left, slope = gelu_pair(half)
        mixed = dot(mixer, t["slot_in"][:, sl])
        t["gated"][:, sl] = (left * mixed).astype(BF16)
        t["left"][:, sl] = left.astype(BF16)
        t["left_slope"][:, sl] = (mixed * slope).astype(BF16)
    return inverse


def add_branch(values, gated, valid, w_out, b_out):
    branch = dot(gated, w_out[...].reshape(gated.shape[1], -1)) * valid
    return values + (branch + b_out[...])


def backward_left(upstream, w_out, left, left_slope, mixed_grad, hidden_grad, b_in_sum):
    for sl in cuts(mixed_grad.shape[1]):
        blocks = slice(sl.start // BLOCK, sl.stop // BLOCK)
        gated_grad = dot_last(upstream, w_out[blocks].reshape(COLUMNS, -1))
        mixed_grad[:, sl] = (gated_grad * left[:, sl].astype(F32)).astype(BF16)
        left_grad = gated_grad * left_slope[:, sl].astype(F32)
        hidden_grad[:, sl] = left_grad.astype(BF16)
        b_in_sum[:, sl] += fold_rows(left_grad)


def backward_right(valid, mixer_back, inverse, gain_two, t, hidden_grad, b_in_sum, sums, slots):
    rows = valid.shape[0]
    half_width = t["white"].shape[1]
    cut = slots // BLOCK * BLOCK
    outer = dot_last(t["slot_in"][...], t["mixed_grad"][...])
    is_slot = lax.broadcasted_iota(jnp.int32, (rows, 1), 0) < slots
    sums["spatial"][:rows, :rows] += outer * jnp.where(is_slot, valid, 1.0)
    back = mixer_back.astype(F32)
    by_bias = outer[slots + 2 : slots + 3] + outer[slots + 3 : slots + 4]
    by_gain = outer[slots + 4 : slots + 5] + outer[slots + 5 : slots + 6]
    mean_scaled = jnp.sum(back * by_gain, -1, keepdims=True) * (1.0 / half_width)
    mean_white = jnp.sum(back * (outer - by_bias), -1, keepdims=True) * (1.0 / half_width)
    for sl in cuts(half_width):
        slot_grad = dot(mixer_back, t["mixed_grad"][:, sl])
        white = t["white"][:, sl].astype(F32)
        sums["gain_two"][:, sl] += fold_rows(slot_grad * white)
        sums["bias_two"][:, sl] += slot_grad[cut:]
        scaled = slot_grad * gain_two[:, sl] - mean_scaled - white * mean_white
        right_grad = scaled * inverse * t["right_slope"][:, sl].astype(F32)
        hidden_grad[:, sl] = right_grad.astype(BF16)
        b_in_sum[:, sl] += fold_rows(right_grad)


def backward_norm(values, halves, upstream, w, sums):
    white, inverse = white_of(values)
    normed_grad = None
    per_half = w["w_in"].shape[0] // 2
    for group in range(2 * per_half):
        at = group % per_half * GROUP
        part = dot_last(halves[group // per_half][:, at : at + GROUP], w["w_in"][group])
        normed_grad = part if normed_grad is None else normed_grad + part
    sums["gain_one"][...] += fold_rows(normed_grad * white)
    sums["bias_one"][...] += fold_rows(normed_grad)
    scaled = normed_grad * w["gain_one"][...]
    mean = jnp.mean(scaled, -1, keepdims=True)
    mean_white = jnp.mean(scaled * white, -1, keepdims=True)
    return upstream + inverse * (scaled - mean - white * mean_white)


def load_blocks(owner, pieces, places, sem):
    position = 0
    for piece in pieces:
        blocks = piece.shape[0]

        def start(at, carry, piece=piece, position=position):
            block = owner[position + at]
            for first, ref in places:
                if ref.shape[1] == BLOCK:
                    count = ref.shape[0] * BLOCK // ref.shape[2]
                    target = ref.at[pl.ds(block * count, count)]
                else:
                    count = ref.shape[0]
                    target = ref.at[:, pl.ds(pl.multiple_of(block * BLOCK, BLOCK), BLOCK)]
                pltpu.make_async_copy(piece.at[at, first : first + count], target, sem).start()
            return carry

        lax.fori_loop(0, blocks, start, 0)
        position += blocks
    for unused, ref in places:
        pltpu.make_async_copy(ref, ref, sem).wait()

def put_weight_grads(owner, jobs, result, stage, outs, sem):
    half = stage.shape[1]
    spots = [(0, 0, outs[0])] + [(1, at * outs[1].shape[0], out) for at, out in enumerate(outs[1:])]

    def send(group, rows):
        for side in range(2):
            for at in range(half):
                stage[side, at, group] = result[rows(owner[side * half + at])]
        for side, first, out in spots:
            part = stage.at[side, first : first + out.shape[0], group]
            pltpu.make_async_copy(part, out.at[:, group], sem).start()

    for left, right, place in jobs:
        if left.shape[1] > right.shape[1]:
            for start in range(0, left.shape[1], GROUP):
                stop = start + GROUP
                result[start:stop] = dot_first(left[:, start:stop], right[...]).astype(BF16)
            per = left.shape[1] // right.shape[1]
            for part in range(per):
                spot = lambda block: pl.ds(pl.multiple_of((block * per + part) * BLOCK, BLOCK), BLOCK)
                send(place + part, spot)
        else:
            for group in range(right.shape[1] // GROUP):
                columns = slice(group * GROUP, (group + 1) * GROUP)
                result[: left.shape[1]] = dot_first(left[...], right[:, columns]).astype(BF16)
                send(place + group, lambda block: pl.ds(pl.multiple_of(block * BLOCK, BLOCK), BLOCK))
    for side, first, out in spots:
        pltpu.make_async_copy(stage.at[side, first : first + out.shape[0]], out, sem).wait()


def put_sums(both, slots, outs, odd):
    gate = both[0]["gain_two"].shape[1]
    rows = slots // BLOCK * BLOCK + both[0]["bias_two"].shape[0]
    strips, high = strips_of(rows, gate)
    at = slots % BLOCK
    row = lax.broadcasted_iota(jnp.int32, (8, gate), 0)
    packed = []
    for sums in both:
        one = lambda name: jnp.sum(sums[name][...], 0, keepdims=True)
        bias_two = sums["bias_two"][at : at + 1] + sums["bias_two"][at + 1 : at + 2]
        narrow = [one("b_out")]
        if "gain_one" in sums:
            narrow += [0.5 * one("gain_one"), 0.5 * one("bias_one")]
        filled = sum(part.shape[1] for part in narrow)
        if filled < gate:
            narrow.append(jnp.zeros((1, gate - filled), F32))
        narrow = jnp.concatenate(narrow, 1)
        lines = [0.5 * one("b_left"), 0.5 * one("b_right"), one("gain_two"), bias_two, narrow]
        total = jnp.zeros((8, gate), F32)
        for place, line in enumerate(lines):
            total = jnp.where(row == place, line, total)
        square = [sums["spatial"][strip * high : (strip + 1) * high] for strip in range(strips)]
        packed.append(jnp.concatenate([jnp.concatenate(square, 1), total], 0).astype(BF16))
    outs[0][...] = jnp.where(odd, packed[1], packed[0])
    outs[1][...] = jnp.where(odd, packed[0], packed[1])


def zero(refs):
    for ref in refs:
        ref[...] = jnp.zeros_like(ref)


def whole(shape):
    return pl.BlockSpec(shape, lambda *i: (0,) * len(shape))


def image(rows, columns):
    return pl.BlockSpec((1, rows, columns), lambda i, *unused: (i, 0, 0))


def anywhere(count):
    return [pl.BlockSpec(memory_space=pl.ANY)] * count


def call(kernel, name, grid, in_specs, outs, out_specs, scratch, flops, megabytes, table=0, aliases=None):
    return pl.pallas_call(
        kernel,
        grid_spec=pltpu.PrefetchScalarGridSpec(
            num_scalar_prefetch=table,
            grid=grid,
            in_specs=in_specs,
            out_specs=out_specs,
            scratch_shapes=scratch,
        ),
        out_shape=[jax.ShapeDtypeStruct(shape, dtype) for shape, dtype in outs],
        input_output_aliases=aliases or {},
        compiler_params=pltpu.CompilerParams(vmem_limit_bytes=megabytes << 20),
        cost_estimate=pl.CostEstimate(flops=flops, bytes_accessed=20_000_000, transcendentals=0),
        name=name,
    )


def in_scratch(width, hidden):
    return pltpu.VMEM((hidden // GROUP, width, GROUP), BF16)


def out_scratch(width, hidden):
    return pltpu.VMEM((hidden // 2 // BLOCK, BLOCK, width), BF16)


def strips_of(rows, gate):
    strips = gate // STRIP
    return strips, -(-rows // strips // 8) * 8


def sum_shapes(rows, width, hidden, slots):
    strips, high = strips_of(rows, hidden // 2)
    return {
        "b_out": (8, width),
        "b_left": (8, hidden // 2),
        "b_right": (8, hidden // 2),
        "spatial": (strips * high, STRIP),
        "gain_two": (8, hidden // 2),
        "bias_two": (rows - slots // BLOCK * BLOCK, hidden // 2),
        "gain_one": (8, width),
        "bias_one": (8, width),
    }


def forward_save(values, live, mixer, slot_pad, w, owner, pieces, place, slots, first, count, into=()):
    images, rows, width = values.shape
    hidden = w["b_in"].shape[1]
    gate = hidden // 2
    outs = {name: (gate, BF16) for name in KEPT[:6]}
    outs["normed"] = (width, BF16)
    outs["inverse"] = (1, F32)
    n_w, n_p, n_o, n_i = len(WEIGHTS), len(pieces), len(outs), len(into)

    def kernel(owner_ref, values_ref, live_ref, mixer_ref, pad_ref, *refs):
        weights = dict(zip(WEIGHTS, refs[:n_w]))
        rest = refs[n_w + n_p + n_i :]
        out = dict(zip(outs, rest[:n_o]))
        right, weights["w_in"], sem = rest[n_o:]

        @pl.when(pl.program_id(0) == 0)
        def _():
            load_blocks(owner_ref, refs[n_w : n_w + n_p], [(place, weights["w_in"])], sem)

        kept = {name: ref.at[0] for name, ref in out.items()}
        kept["right"] = right
        here = values_ref[0].astype(F32)
        out["inverse"][0] = forward_image(here, live_ref[...], mixer_ref[0], pad_ref, weights, kept, slots)

    some = lambda columns: pl.BlockSpec((1, rows, columns), lambda i, *unused: (first + i, 0, 0))
    results = call(
        kernel,
        "forward_save",
        (count,),
        [some(width), whole((rows, 1)), some(rows), whole(slot_pad.shape)]
        + [whole(w[name].shape) for name in WEIGHTS]
        + anywhere(n_p + n_i),
        [((images, rows, columns), dtype) for columns, dtype in outs.values()],
        [some(columns) for columns, unused in outs.values()],
        [pltpu.VMEM((rows, gate), F32), in_scratch(width, hidden), pltpu.SemaphoreType.DMA],
        2_000_000_000 * count,
        60,
        table=1,
        aliases={5 + n_w + n_p + at: at for at in range(n_i)},
    )(owner, values, live, mixer, slot_pad, *[w[name] for name in WEIGHTS], *pieces, *into)
    return results


KEPT = ("left", "left_slope", "white", "right_slope", "slot_in", "gated", "normed", "inverse")


def forward_backward(
    values, kept_before, b_out, cotangent, valid, live, mixer, mixer_back, slot_pad, w, owner, pieces, places, slots
):
    images, rows, width = values.shape
    hidden = w["b_in"].shape[1]
    gate = hidden // 2
    groups, per, half = hidden // GROUP, gate // width, width // BLOCK // 2
    outs = {
        "values": (width, BF16),
        "upstream": (width, F32),
        "left_grad_before": (gate, BF16),
        "mixed_grad_before": (gate, BF16),
    }
    shapes = sum_shapes(rows, width, hidden, slots)
    shapes = {name: shapes[name] for name in SUMS} | {
        "b_out_before": shapes["b_out"],
        "b_left_before": shapes["b_left"],
    }
    image_scratch = {"right": F32} | dict.fromkeys(
        ("left", "left_slope", "white", "right_slope", "slot_in", "mixed_grad"), BF16
    )
    all_scratch = {
        "normed": width,
        "gated": gate,
        "hidden_grad": hidden,
        "masked": width,
        "normed_before": width,
        "gated_before": gate,
        "left_grad_before": gate,
        "masked_before": width,
    }
    reads = ("gated", "left", "left_slope", "normed")
    last_shape = (half, groups + per, BLOCK, GROUP)
    before_shape = (half, groups // 2 + per, BLOCK, GROUP)
    n_w, n_p, n_o, n_s, n_r = len(WEIGHTS), len(pieces), len(outs), len(shapes), len(reads)

    def kernel(owner_ref, values_ref, b_out_ref, cot_ref, valid_ref, live_ref, mixer_ref, back_ref, pad_ref, *refs):
        before = {name: ref.at[0] for name, ref in zip(reads, refs)}
        refs = refs[n_r:]
        weights = dict(zip(WEIGHTS, refs[:n_w]))
        rest = refs[n_w + n_p :]
        out = {name: ref.at[0] for name, ref in zip(outs, rest)}
        sums = dict(zip(shapes, rest[n_o:]))
        last_outs, before_outs = rest[n_o + n_s :][:3], rest[n_o + n_s + 3 :][:2]
        rest = rest[n_o + n_s + 5 :]
        kept = dict(zip(image_scratch, rest))
        rest = rest[len(image_scratch) :]
        every = dict(zip(all_scratch, rest))
        w_out_before, weights["w_in"], weights["w_out"], result, last_stage, before_stage, sem, out_sem = rest[len(every) :]
        step = pl.program_id(0)

        @pl.when(step == 0)
        def _():
            targets = (w_out_before, weights["w_in"], weights["w_out"])
            load_blocks(owner_ref, refs[n_w : n_w + n_p], list(zip(places, targets)), sem)
            zero(sums.values())

        mine = pl.ds(pl.multiple_of(step * rows, BLOCK), rows)
        here = {name: ref.at[mine] for name, ref in every.items()}
        kept["normed"], kept["gated"] = here["normed"], here["gated"]
        left_grad, right_grad = (here["hidden_grad"].at[:, at : at + gate] for at in (0, gate))
        here["normed_before"][...] = before["normed"][...]
        here["gated_before"][...] = before["gated"][...]
        valid_column = valid_ref[0]
        inputs = add_branch(values_ref[0].astype(F32), before["gated"][...], valid_column, w_out_before, b_out_ref.at[:1])
        inverse = forward_image(inputs, live_ref[...], mixer_ref[0], pad_ref, weights, kept, slots)
        outputs = add_branch(inputs, kept["gated"][...], valid_column, weights["w_out"], b_out_ref.at[1:])
        out["values"][...] = outputs.astype(BF16)
        upstream = cot_ref[0].astype(F32)
        sums["b_out"][...] += fold_rows(upstream)
        masked = (upstream * valid_column).astype(BF16)
        here["masked"][...] = masked
        backward_left(
            masked, weights["w_out"], kept["left"], kept["left_slope"], kept["mixed_grad"], left_grad, sums["b_left"]
        )
        backward_right(
            valid_column, back_ref[0], inverse, weights["gain_two"], kept, right_grad, sums["b_right"], sums, slots
        )
        upstream = backward_norm(inputs, (left_grad, right_grad), upstream, weights, sums)
        out["upstream"][...] = upstream
        branch_grad = upstream.astype(BF16).astype(F32)
        sums["b_out_before"][...] += fold_rows(branch_grad)
        masked = (branch_grad * valid_column).astype(BF16)
        here["masked_before"][...] = masked
        backward_left(
            masked,
            w_out_before,
            before["left"],
            before["left_slope"],
            out["mixed_grad_before"],
            here["left_grad_before"],
            sums["b_left_before"],
        )
        out["left_grad_before"][...] = here["left_grad_before"][...]

        @pl.when(step == images - 1)
        def _():
            jobs = [(every["normed"], every["hidden_grad"], 0), (every["gated"], every["masked"], groups)]
            put_weight_grads(owner_ref, jobs, result, last_stage, last_outs, out_sem.at[0])
            jobs = [
                (every["normed_before"], every["left_grad_before"], 0),
                (every["gated_before"], every["masked_before"], groups // 2),
            ]
            put_weight_grads(owner_ref, jobs, result, before_stage, before_outs, out_sem.at[1])

    results = call(
        kernel,
        "forward_backward",
        (images,),
        [image(rows, width), whole(b_out.shape), image(rows, width), image(rows, 1), whole((rows, 1))]
        + [image(rows, rows), image(rows, rows), whole(slot_pad.shape)]
        + [image(rows, kept_before[name].shape[2]) for name in reads]
        + [whole(w[name].shape) for name in WEIGHTS]
        + anywhere(n_p),
        [((images, rows, columns), dtype) for columns, dtype in outs.values()]
        + [(shape, F32) for shape in shapes.values()]
        + [(last_shape, BF16)]
        + [((half // 2, *last_shape[1:]), BF16)] * 2
        + [(before_shape, BF16)] * 2,
        [image(rows, columns) for columns, unused in outs.values()]
        + [whole(shape) for shape in shapes.values()]
        + anywhere(5),
        [pltpu.VMEM((rows, gate), dtype) for dtype in image_scratch.values()]
        + [pltpu.VMEM((images * rows, columns), BF16) for columns in all_scratch.values()]
        + [out_scratch(width, hidden), in_scratch(width, hidden), out_scratch(width, hidden)]
        + [pltpu.VMEM((gate, GROUP), BF16), pltpu.VMEM((2,) + last_shape, BF16), pltpu.VMEM((2,) + before_shape, BF16)]
        + [pltpu.SemaphoreType.DMA, pltpu.SemaphoreType.DMA((2,))],
        40_000_000_000,
        60,
        table=1,
    )(
        owner,
        values,
        b_out,
        cotangent,
        valid,
        live,
        mixer,
        mixer_back,
        slot_pad,
        *[kept_before[name] for name in reads],
        *[w[name] for name in WEIGHTS],
        *pieces,
    )
    blocks = results[n_o + n_s :]
    return dict(zip(outs, results)), dict(zip(shapes, results[n_o:])), blocks[:3], blocks[3:]


def backward_slots(kept, mixed_grad, valid, mixer_back, w, owner, both, slots):
    images, rows, gate = mixed_grad.shape
    width = w["gain_one"].shape[1]
    half = width // BLOCK // 2
    shapes = sum_shapes(rows, width, 2 * gate, slots)
    names = ("b_right", "spatial", "gain_two", "bias_two")
    reads = ("white", "right_slope", "slot_in", "inverse", "normed")
    block_shape = (half, gate // GROUP, BLOCK, GROUP)
    high = strips_of(rows, gate)[1]
    flat = [(block, name) for block in range(2) for name in both[block]]
    n_r, n_f, n_s = len(reads), len(flat), len(names)

    def kernel(owner_ref, mixed_ref, valid_ref, back_ref, gain_two, *refs):
        t = {name: ref.at[0] for name, ref in zip(reads, refs)}
        t["mixed_grad"] = mixed_ref.at[0]
        out, *outs = refs[n_r + n_f :][:5]
        rest = refs[n_r + n_f + 5 :]
        own = dict(zip(names, rest))
        normed, right_grad, result, stage, out_sem = rest[n_s:]
        step = pl.program_id(0)

        @pl.when(step == 0)
        def _():
            zero(own.values())

        mine = pl.ds(pl.multiple_of(step * rows, BLOCK), rows)
        normed[mine] = t["normed"][...]
        here = right_grad.at[mine]
        backward_right(valid_ref[0], back_ref[0], t["inverse"][...], gain_two, t, here, own["b_right"], own, slots)
        out[0] = here[...]

        @pl.when(step == images - 1)
        def _():
            put_weight_grads(owner_ref, [(normed, right_grad, 0)], result, stage, outs[:2], out_sem)
            sums = {}, {}
            for (block, name), ref in zip(flat, refs[n_r:]):
                sums[block][name] = ref
            sums[0].update(own)
            put_sums(sums, slots, outs[2:], owner_ref[0] % 2 == 1)

    results = call(
        kernel,
        "backward_slots",
        (images,),
        [image(rows, gate), image(rows, 1), image(rows, rows), whole((1, gate))]
        + [image(rows, kept[name].shape[2]) for name in reads]
        + [whole(both[block][name].shape) for block, name in flat],
        [((images, rows, gate), BF16)] + [(block_shape, BF16)] * 2 + [((high + 8, gate), BF16)] * 2,
        [image(rows, gate)] + anywhere(2) + [whole((high + 8, gate))] * 2,
        [pltpu.VMEM(shapes[name], F32) for name in names]
        + [pltpu.VMEM((images * rows, width), BF16), pltpu.VMEM((images * rows, gate), BF16)]
        + [pltpu.VMEM((width, GROUP), BF16), pltpu.VMEM((2,) + block_shape, BF16), pltpu.SemaphoreType.DMA],
        9_000_000_000,
        60,
        table=1,
    )(
        owner,
        mixed_grad,
        valid,
        mixer_back,
        w["gain_two"],
        *[kept[name] for name in reads],
        *[both[block][name] for block, name in flat],
    )
    return results[0], results[1:3], results[3:]


def backward_first(values, left_grad, right_grad, upstream, w, owner, pieces, place, slots):
    images, rows, width = values.shape
    gate = left_grad.shape[2]
    n_p = len(pieces)

    def kernel(owner_ref, values_ref, left_ref, right_ref, up_ref, gain_ref, *refs):
        out, line, gain_sum, bias_sum, w_in, sem = refs[n_p:]
        step = pl.program_id(0)

        @pl.when(step == 0)
        def _():
            load_blocks(owner_ref, refs[:n_p], [(place, w_in)], sem)
            zero((gain_sum, bias_sum))

        weights = {"w_in": w_in, "gain_one": gain_ref}
        own = {"gain_one": gain_sum, "bias_one": bias_sum}
        halves = left_ref.at[0], right_ref.at[0]
        result = backward_norm(values_ref[0].astype(F32), halves, up_ref[0], weights, own)
        for at in range(images):

            @pl.when(step == at)
            def _(at=at):
                out[at * slots : (at + 1) * slots] = result[:slots]

        @pl.when(step == images - 1)
        def _():
            zero((line,))
            for at, ref in enumerate((gain_sum, bias_sum)):
                line[5:6, (1 + at) * width : (2 + at) * width] = 0.5 * jnp.sum(ref[...], 0, keepdims=True)

    return call(
        kernel,
        "backward_first",
        (images,),
        [image(rows, width), image(rows, gate), image(rows, gate), image(rows, width), whole((1, width))]
        + anywhere(n_p),
        [((images * slots, width), F32), ((8, gate), F32)],
        [whole((images * slots, width)), whole((8, gate))],
        [pltpu.VMEM((8, width), F32)] * 2 + [in_scratch(width, 2 * gate), pltpu.SemaphoreType.DMA],
        6_000_000_000,
        60,
        table=1,
    )(owner, values, left_grad, right_grad, upstream, w["gain_one"], *pieces)


def unpack_sums(odd, mine, theirs, slots, width):
    gate = mine.shape[1]
    high = mine.shape[0] - 8
    strips = gate // STRIP

    def kernel(odd_ref, mine_ref, theirs_ref, gain_one, bias_one, b_in, gain_two, bias_two, spatial, b_sp, b_out):
        is_odd = odd_ref[0] == 1
        held = mine_ref[...].astype(F32), theirs_ref[...].astype(F32)
        for block in range(2):
            value = jnp.where(is_odd, held[1 - block], held[block])
            square = [value[:high, strip * STRIP : (strip + 1) * STRIP] for strip in range(strips)]
            square = jnp.concatenate(square + [jnp.zeros((STRIP, STRIP), F32)], 0)[:STRIP]
            b_sp[block : block + 1] = square[slots : slots + 1, :slots]
            spatial[:, block, :] = square.T[:slots, :slots]
            line = lambda place: value[high + place : high + place + 1]
            b_in[block : block + 1, :gate] = line(0)
            b_in[block : block + 1, gate:] = line(1)
            gain_two[block : block + 1] = line(2)
            bias_two[block : block + 1] = line(3)
            narrow = line(4)
            if block == 0:
                narrow = narrow + (held[0][high + 5 : high + 6] + held[1][high + 5 : high + 6])
            for place, out in enumerate((b_out, gain_one, bias_one)):
                out[block : block + 1] = narrow[:, place * width : (place + 1) * width]

    shapes = [(2, width), (2, width), (2, 2 * gate), (2, gate), (2, gate), (slots, 2, slots), (2, slots), (2, width)]
    results = pl.pallas_call(
        kernel,
        in_specs=[pl.BlockSpec(memory_space=pltpu.SMEM)] + [pl.BlockSpec(memory_space=pltpu.VMEM)] * 2,
        out_shape=[jax.ShapeDtypeStruct(shape, F32) for shape in shapes],
        compiler_params=pltpu.CompilerParams(vmem_limit_bytes=60 << 20),
        name="unpack_sums",
    )(odd, mine, theirs)
    return [*results[:5], results[5].transpose(1, 0, 2), *results[6:]]


def add_blocks(terms, groups, per):
    arrays = []
    for pairs in terms.values():
        arrays += [array for array, unused in pairs if not any(array is other for other in arrays)]
    index = {id(array): at for at, array in enumerate(arrays)}
    width = arrays[0].shape[-1]

    def kernel(*refs):
        in_out, out_out = refs[-2:]
        for (block, group), pairs in terms.items():
            total = None
            for array, at in pairs:
                part = refs[index[id(array)]][0, at].astype(F32)
                total = part if total is None else total + part
            if group < groups:
                in_out[block, :, group * GROUP : (group + 1) * GROUP] = total
            else:
                first = (group - groups) * BLOCK
                out_out[block, first : first + BLOCK] = total

    shapes = [(2, BLOCK, groups * GROUP), (2, per * BLOCK, width)]
    return pl.pallas_call(
        kernel,
        grid=(1,),
        in_specs=[pl.BlockSpec((1,) + array.shape[1:], lambda i: (0, 0, 0, 0)) for array in arrays],
        out_specs=[whole(shape) for shape in shapes],
        out_shape=[jax.ShapeDtypeStruct(shape, F32) for shape in shapes],
        compiler_params=pltpu.CompilerParams(vmem_limit_bytes=60 << 20),
        name="add_blocks",
    )(*arrays)


class Tree:
    def __init__(self, devices):
        self.devices = devices
        far = [1 << bit for bit in range(3, devices.bit_length() - 1)]
        self.bits = far + [2, 4], far[::-1] + [4, 2]
        self.steps = len(far) + 2

    def swap(self, values, *steps):
        bits = [sum(bits[step] for step in steps) or 1 for bits in self.bits]
        return lax.ppermute(values, AXES, [(i, i ^ bits[i % 2]) for i in range(self.devices)])

    def owners(self):
        offsets = np.zeros((2, 1 << self.steps), np.int32)
        for core in range(2):
            for step in range(self.steps):
                offsets[core] ^= (np.arange(1 << self.steps, dtype=np.int32) >> step & 1) * self.bits[core][step]
        me = lax.axis_index(AXES).astype(jnp.int32)
        odd = me % 2 == 1
        mine = me ^ jnp.where(odd, offsets[1], offsets[0])
        theirs = (me ^ 1) ^ jnp.where(odd, offsets[0], offsets[1])
        return jnp.concatenate([mine, theirs])

    def gather(self, own):
        held = pack_blocks(own, 1)
        far = self.steps - 2
        got = [
            self.swap(held, *[step for step in range(far) if index >> step & 1]) for index in range(1, 1 << far)
        ]
        wait = yield held, got
        held = jnp.concatenate(after([held, *got], wait))
        first, second = self.swap(held, far), self.swap(held, far + 1)
        wait = yield held, (first, second)
        last = self.swap(after(first, wait), far + 1)
        pieces = [held, first, second]
        others = [self.swap(piece) for piece in pieces]
        wait = yield held, last
        last = after(last, wait)
        yield [*pieces, last, *others, self.swap(last)]

    def sum(self, mine, *theirs):
        return TreeSum(self, mine, *theirs)

    def finish(self, terms, groups, per):
        return add_blocks(terms, groups, per)

    def total(self, mine, theirs):
        far = self.steps - 2
        order = [*reversed(range(far)), far, far + 1]
        add = lambda one, other: (one.astype(F32) + other.astype(F32)).astype(BF16)
        got = self.swap(theirs)
        wait = yield theirs
        mine = add(mine, after(got, wait))
        got = self.swap(mine, order[0])
        late = yield mine
        late = late.astype(BF16)
        late_got = self.swap(late, order[0])
        wait = yield late
        late = late.astype(F32) + late_got.astype(F32)
        mine = mine.astype(F32) + after(got, wait).astype(F32)
        mine = (mine + jnp.pad(late, ((mine.shape[0] - late.shape[0], 0), (0, 0)))).astype(BF16)
        for step in order[1:]:
            got = self.swap(mine, step)
            wait = yield mine
            mine = add(mine, after(got, wait))
        yield lax.axis_index("narrow") % 2, mine, self.swap(mine)


class TreeSum:
    def __init__(self, links, mine, *theirs):
        self.links, self.step = links, links.steps
        gots = [links.swap(part) for part in theirs[::-1]]
        self.sent, self.got = theirs[-1], gots[0]
        self.columns, self.shared = [[mine, gots[-1]]], []
        self.upper = gots[0] if len(gots) > 1 else None

    def add(self, at):
        total = []
        for column in self.columns:
            total.append(column[0][at].astype(F32))
            for part in column[1:]:
                total[-1] = total[-1] + part[at].astype(F32)
        total = jnp.concatenate(total, 1) if len(total) > 1 else total[0]
        for part in self.shared:
            total = total + part[at].astype(F32)
        return total

    def send(self, wait):
        self.step -= 1
        keep = 1 << self.step
        if self.upper is not None:
            mine, upper = after((self.columns[0][0], self.upper), wait)
            self.sent = (mine[keep:].astype(F32) + upper.astype(F32)).astype(BF16)
            self.upper = None
        else:
            self.columns, self.shared = after((self.columns, self.shared), wait)
            self.sent = self.add(slice(keep, 2 * keep)).astype(BF16)
        self.got = self.links.swap(self.sent, self.step)
        (self.columns[0] if len(self.columns) == 1 else self.shared).append(self.got)
        return self.sent

    def join(self, other):
        self.columns = self.columns + other.columns
        return self

    def terms(self):
        terms = []
        for column in self.columns:
            for at in range(column[0].shape[1]):
                terms.append([(part, at) for part in column] + [(part, len(terms)) for part in self.shared])
        return terms


class PlainSum:
    def __init__(self, mine, *theirs):
        self.blocks = jnp.concatenate([mine, *theirs]).astype(F32)
        self.sent = self.got = theirs[0]

    def send(self, wait):
        return self.sent

    def join(self, other):
        self.blocks = jnp.concatenate([self.blocks, other.blocks], 1)
        return self

    def terms(self):
        return [self.blocks[:, at] for at in range(self.blocks.shape[1])]


class Plain:
    def __init__(self, width, gate):
        self.width, self.gate = width, gate
        self.steps = 4
        self.blocks = width // BLOCK

    def owners(self):
        return jnp.arange(self.blocks, dtype=jnp.int32)

    def gather(self, own):
        gathered = [lax.all_gather(part, AXES, axis=0, tiled=True) for part in own]
        for unused in range(3):
            yield gathered, gathered
        yield [pack_blocks(gathered, self.blocks)]

    def sum(self, mine, *theirs):
        return PlainSum(mine, *theirs)

    def finish(self, terms, groups, per):
        in_grad, out_grad = [], []
        for block in range(2):
            inner = jnp.concatenate([terms[block, group] for group in range(groups)], 2)
            outer = jnp.concatenate([terms[block, groups + part] for part in range(per)], 1)
            in_grad.append(inner.reshape(self.width, -1))
            out_grad.append(outer.reshape(self.gate, -1))
        return [
            lax.psum_scatter(jnp.stack(grad), AXES, scatter_dimension=1, tiled=True) for grad in (in_grad, out_grad)
        ]

    def total(self, mine, theirs):
        yield mine
        late = yield mine
        mine = mine.astype(F32) + jnp.pad(late, ((mine.shape[0] - late.shape[0], 0), (0, 0)))
        yield late
        for unused in range(self.steps - 1):
            yield mine
        yield jnp.int32(0), *lax.psum((mine, theirs.astype(F32)), AXES)


def pack_blocks(parts, blocks):
    packed = []
    for part in parts:
        if part.shape[1] > GROUP:
            packed.append(part.reshape(blocks, BLOCK, -1, GROUP).transpose(0, 2, 1, 3))
        else:
            packed.append(part.reshape(blocks, -1, BLOCK, GROUP))
    return jnp.concatenate(packed, 1)


def after(values, *others):
    return lax.optimization_barrier((values, others))[0] if others != (None,) else values


def bfloat_pair(values):
    top = lax.reduce_precision(values, 8, 7)
    return top.astype(BF16), lax.reduce_precision(values - top, 8, 7).astype(BF16)


def spatial_operands(valid, w_sp, b_sp, gain_two, bias_two, rows):
    images, slots = valid.shape
    gate = gain_two.shape[0]
    cut = slots // BLOCK * BLOCK
    spare = rows - slots
    masked = w_sp[None] * valid[:, None, :].astype(BF16)
    bias = jnp.broadcast_to(jnp.stack(bfloat_pair(b_sp), -1)[None], (images, slots, 2))
    mixer = jnp.concatenate([masked, bias], 2)
    mixer = jnp.pad(mixer, ((0, 0), (0, spare), (0, spare - 2)))
    column_sum = jnp.einsum("ir,pr->ip", valid.astype(BF16), w_sp, preferred_element_type=F32)
    back = jnp.concatenate([jnp.swapaxes(masked, 1, 2), jnp.stack(bfloat_pair(column_sum), 1)], 1)
    back = jnp.pad(back, ((0, 0), (0, spare - 2), (0, spare)))
    one = jnp.ones((gate,), BF16)
    pad = jnp.stack([one, one, *bfloat_pair(bias_two), *bfloat_pair(gain_two)])
    pad = jnp.pad(pad, ((slots - cut, rows - slots - 6), (0, 0))).astype(F32)
    return mixer, back, pad


def shards(
    tokens,
    mask,
    ln1_gain,
    ln1_bias,
    in_weight,
    in_bias,
    ln2_gain,
    ln2_bias,
    spatial_weight,
    spatial_bias,
    out_weight,
    out_bias,
    cotangent,
):
    devices = lax.axis_size(AXES)
    images, slots = mask.shape
    width = tokens.shape[1]
    hidden = in_weight.shape[2]
    gate = hidden // 2
    per = gate // width
    groups = hidden // GROUP
    rows = -(-(slots + 6) // BLOCK) * BLOCK
    spare = rows - slots
    pairwise = devices * BLOCK == width and devices >= 16 and devices & (devices - 1) == 0
    links = Tree(devices) if pairwise else Plain(width, gate)

    owner = links.owners()
    gather_one = links.gather([in_weight[0]])
    unused, got = next(gather_one)
    gather_rest = links.gather(after([out_weight[0], in_weight[1], out_weight[1]], got))
    unused, got = next(gather_rest)
    next(gather_one)
    gather_one.send(got)
    pieces_one = gather_one.send(None)
    column_rest, got_rest = gather_rest.send(None)

    valid = mask.astype(F32)
    padded = lambda array: jnp.pad(array.reshape(images, slots, width), ((0, 0), (0, spare), (0, 0)))
    valid_column = jnp.pad(valid, ((0, 0), (0, spare)))[:, :, None]
    live = (jnp.arange(rows) < slots).astype(F32)[:, None]
    values = padded(tokens)
    layers, spatial = [], []
    for layer in range(2):
        layers.append(
            {
                "b_in": 0.5 * in_bias[layer][None],
                "gain_one": 0.5 * ln1_gain[layer][None],
                "bias_one": 0.5 * ln1_bias[layer][None],
                "gain_two": ln2_gain[layer][None],
                "bias_two": ln2_bias[layer][None],
                "b_out": out_bias[layer][None],
            }
        )
        spatial.append(
            spatial_operands(
                valid, spatial_weight[layer], spatial_bias[layer], ln2_gain[layer], ln2_bias[layer], rows
            )
        )
    cot = padded(cotangent)
    mixer, back, pad = zip(*spatial)

    halfway = images * 2 // 5
    save = lambda array, start, count, into: forward_save(
        array, live, mixer[0], pad[0], layers[0], owner, pieces_one, 0, slots, start, count, into
    )
    kept = save(after(values, column_rest), 0, halfway, ())
    gather_rest.send(kept[0])
    ahead = got_rest[0], valid_column, cot, mixer[1], back, pad[1]
    kept = save(after(values, ahead), halfway, images - halfway, kept)
    pieces_rest = gather_rest.send(kept[0])
    kept = dict(zip(KEPT, kept))
    last, last_sums, last_blocks, before_blocks = forward_backward(
        values,
        kept,
        out_bias,
        cot,
        valid_column,
        live,
        mixer[1],
        back[1],
        pad[1],
        layers[1],
        owner,
        pieces_rest,
        (0, per, per + groups),
        slots,
    )

    unpadded = lambda array: array[:, :slots].reshape(images * slots, width)
    one = links.sum(*last_blocks)
    left = links.sum(before_blocks[0], after(before_blocks[1], one.sent))
    layer_out = unpadded(after(last["values"], left.sent))
    sent = one.send((left.sent, layer_out))
    sums = {"b_out": last_sums.pop("b_out_before"), "b_left": last_sums.pop("b_left_before")}
    right_grad, blocks, packed = backward_slots(
        kept,
        after(last["mixed_grad_before"], sent),
        valid_column,
        back[0],
        layers[0],
        owner,
        (sums, last_sums),
        slots,
    )
    right = links.sum(*after(blocks, one.got, left.got))
    small = links.total(*packed)
    sent = next(small)
    sent = left.send((sent, right.sent))
    sent = one.send(sent)
    sent = right.send(sent)
    sent = small.send(sent)
    input_grad, line = backward_first(
        values, last["left_grad_before"], right_grad, after(last["upstream"], sent), layers[0], owner, pieces_one, 0, slots
    )
    line = after(line, left.got, one.got, right.got)
    sent = small.send(line)
    both = left.join(right)
    sent = both.send(sent)
    for step in range(links.steps - 2):
        sent = one.send(sent)
        sent = small.send(sent)
        sent = both.send(sent)
    for unused in range(2):
        small_end = small.send(sent)
    odd, *summed = small_end
    steps = groups // 2
    spots = [(1, group) for group in range(groups + per)]
    terms = dict(zip(spots, one.terms()))
    spots = [(0, group) for group in range(steps)] + [(0, groups + part) for part in range(per)]
    spots += [(0, steps + group) for group in range(steps)]
    terms |= zip(spots, both.terms())
    in_grad, out_grad = links.finish(terms, groups, per)
    gain_one, bias_one, b_in, gain_two, bias_two, spatial_grad, b_sp, b_out = unpack_sums(
        odd.reshape(1), *summed, slots, width
    )

    return (
        layer_out,
        input_grad,
        gain_one,
        bias_one,
        in_grad,
        b_in,
        gain_two,
        bias_two,
        spatial_grad,
        b_sp,
        out_grad,
        b_out,
    )


def solution(mesh):
    both = P(AXES, None)
    second = P(None, AXES, None)
    in_specs = (both, both, P(), P(), second, P(), P(), P(), P(), P(), second, P(), both)
    out_specs = (both, both, P(), P(), second, P(), P(), P(), P(), P(), second, P())
    return jax.shard_map(shards, mesh=mesh, in_specs=in_specs, out_specs=out_specs, check_vma=False)
```

```python
import jax
import jax.numpy as jnp
import numpy as np
from jax import lax
from jax.experimental import pallas as pl
from jax.experimental.pallas import tpu as pltpu
from jax.sharding import PartitionSpec as P

EPS = 1e-05
AXES = ("wide", "narrow")
F32 = jnp.float32
BF16 = jnp.bfloat16
TANH_ONE = 2 * 0.7978845608028654
TANH_THREE = 8 * 0.7978845608028654 * 0.044715
COLUMNS = 256
BLOCK = 16
GROUP = 512
STRIP = 256
WEIGHTS = ("b_in", "gain_one", "bias_one", "gain_two", "bias_two")
SUMS = ("b_out", "b_left", "b_right", "spatial", "gain_two", "bias_two", "gain_one", "bias_one")


def dot(a, b):
    return jnp.dot(a, b, preferred_element_type=F32)


def dot_last(a, b):
    return lax.dot_general(a, b, (((1,), (1,)), ((), ())), preferred_element_type=F32)


def dot_first(a, b):
    return lax.dot_general(a, b, (((0,), (0,)), ((), ())), preferred_element_type=F32)


def gelu_pair(half):
    square = half * half
    tanh = jnp.tanh(half * (TANH_ONE + TANH_THREE * square))
    upper = 1.0 + tanh
    value = half * upper
    slope = upper + value * (1.0 - tanh) * (TANH_ONE + (3 * TANH_THREE) * square)
    return value, slope


def fold_rows(values):
    total = values[:8]
    for row in range(8, values.shape[0], 8):
        total = total + values[row : row + 8]
    return total


def fold_columns(values):
    total = values[:, :128]
    for column in range(128, values.shape[1], 128):
        total = total + values[:, column : column + 128]
    return total


def white_of(values):
    centred = values - jnp.mean(values, -1, keepdims=True)
    inverse = lax.rsqrt(jnp.mean(centred * centred, -1, keepdims=True) + EPS)
    return centred * inverse, inverse


def cuts(width):
    return [slice(c, c + COLUMNS) for c in range(0, width, COLUMNS)]


def in_columns(w_in, start):
    at = start % GROUP
    return w_in[start // GROUP, :, at : at + COLUMNS]


def forward_image(values, live, mixer, slot_pad, w, t, slots):
    rows = values.shape[0]
    half_width = t["white"].shape[1]
    cut = slots // BLOCK * BLOCK
    white_one, unused_inverse = white_of(values)
    t["normed"][...] = (white_one * w["gain_one"][...] + w["bias_one"][...]).astype(BF16)
    total = None
    for sl in cuts(half_width):
        at = half_width + sl.start
        half = dot(t["normed"][...], in_columns(w["w_in"], at)) + w["b_in"][:, at : at + COLUMNS]
        value, slope = gelu_pair(half)
        t["right"][:, sl] = value
        t["right_slope"][:, sl] = slope.astype(BF16)
        part = fold_columns(value)
        total = part if total is None else total + part
    average = jnp.sum(total, -1, keepdims=True) * (1.0 / half_width)
    total = None
    for sl in cuts(half_width):
        centred = t["right"][:, sl] - average
        part = fold_columns(centred * centred)
        total = part if total is None else total + part
    spread = jnp.sum(total, -1, keepdims=True) * (1.0 / half_width)
    inverse = lax.rsqrt(spread + EPS) * live
    row = lax.broadcasted_iota(jnp.int32, (rows - cut, COLUMNS), 0)
    for sl in cuts(half_width):
        white = (t["right"][:, sl] - average) * inverse
        t["white"][:, sl] = white.astype(BF16)
        slot_in = white * w["gain_two"][:, sl] + w["bias_two"][:, sl]
        t["slot_in"][:cut, sl] = slot_in[:cut].astype(BF16)
        last = jnp.where(row < slots - cut, slot_in[cut:], slot_pad[:, sl])
        t["slot_in"][cut:, sl] = last.astype(BF16)
    for sl in cuts(half_width):
        half = dot(t["normed"][...], in_columns(w["w_in"], sl.start)) + w["b_in"][:, sl]
        left, slope = gelu_pair(half)
        mixed = dot(mixer, t["slot_in"][:, sl])
        t["gated"][:, sl] = (left * mixed).astype(BF16)
        t["left"][:, sl] = left.astype(BF16)
        t["left_slope"][:, sl] = (mixed * slope).astype(BF16)
    return inverse


def add_branch(values, gated, valid, w_out, b_out):
    branch = dot(gated, w_out[...].reshape(gated.shape[1], -1)) * valid
    return values + (branch + b_out[...])


def backward_left(upstream, w_out, left, left_slope, mixed_grad, hidden_grad, b_in_sum):
    for sl in cuts(mixed_grad.shape[1]):
        blocks = slice(sl.start // BLOCK, sl.stop // BLOCK)
        gated_grad = dot_last(upstream, w_out[blocks].reshape(COLUMNS, -1))
        mixed_grad[:, sl] = (gated_grad * left[:, sl].astype(F32)).astype(BF16)
        left_grad = gated_grad * left_slope[:, sl].astype(F32)
        hidden_grad[:, sl] = left_grad.astype(BF16)
        b_in_sum[:, sl] += fold_rows(left_grad)


def backward_right(valid, mixer_back, inverse, gain_two, t, hidden_grad, b_in_sum, sums, slots):
    rows = valid.shape[0]
    half_width = t["white"].shape[1]
    cut = slots // BLOCK * BLOCK
    outer = dot_last(t["slot_in"][...], t["mixed_grad"][...])
    is_slot = lax.broadcasted_iota(jnp.int32, (rows, 1), 0) < slots
    sums["spatial"][:rows, :rows] += outer * jnp.where(is_slot, valid, 1.0)
    back = mixer_back.astype(F32)
    by_bias = outer[slots + 2 : slots + 3] + outer[slots + 3 : slots + 4]
    by_gain = outer[slots + 4 : slots + 5] + outer[slots + 5 : slots + 6]
    mean_scaled = jnp.sum(back * by_gain, -1, keepdims=True) * (1.0 / half_width)
    mean_white = jnp.sum(back * (outer - by_bias), -1, keepdims=True) * (1.0 / half_width)
    for sl in cuts(half_width):
        slot_grad = dot(mixer_back, t["mixed_grad"][:, sl])
        white = t["white"][:, sl].astype(F32)
        sums["gain_two"][:, sl] += fold_rows(slot_grad * white)
        sums["bias_two"][:, sl] += slot_grad[cut:]
        scaled = slot_grad * gain_two[:, sl] - mean_scaled - white * mean_white
        right_grad = scaled * inverse * t["right_slope"][:, sl].astype(F32)
        hidden_grad[:, sl] = right_grad.astype(BF16)
        b_in_sum[:, sl] += fold_rows(right_grad)


def backward_norm(values, halves, upstream, w, sums):
    white, inverse = white_of(values)
    normed_grad = None
    per_half = w["w_in"].shape[0] // 2
    for group in range(2 * per_half):
        at = group % per_half * GROUP
        part = dot_last(halves[group // per_half][:, at : at + GROUP], w["w_in"][group])
        normed_grad = part if normed_grad is None else normed_grad + part
    sums["gain_one"][...] += fold_rows(normed_grad * white)
    sums["bias_one"][...] += fold_rows(normed_grad)
    scaled = normed_grad * w["gain_one"][...]
    mean = jnp.mean(scaled, -1, keepdims=True)
    mean_white = jnp.mean(scaled * white, -1, keepdims=True)
    return upstream + inverse * (scaled - mean - white * mean_white)


def load_blocks(owner, pieces, places, sem):
    position = 0
    for piece in pieces:
        blocks = piece.shape[0]

        def start(at, carry, piece=piece, position=position):
            block = owner[position + at]
            for first, ref in places:
                if ref.shape[1] == BLOCK:
                    count = ref.shape[0] * BLOCK // ref.shape[2]
                    target = ref.at[pl.ds(block * count, count)]
                else:
                    count = ref.shape[0]
                    target = ref.at[:, pl.ds(pl.multiple_of(block * BLOCK, BLOCK), BLOCK)]
                pltpu.make_async_copy(piece.at[at, first : first + count], target, sem).start()
            return carry

        lax.fori_loop(0, blocks, start, 0)
        position += blocks
    for unused, ref in places:
        pltpu.make_async_copy(ref, ref, sem).wait()

def put_weight_grads(owner, jobs, result, stage, outs, sem):
    half = stage.shape[1]
    spots = [(0, 0, outs[0])] + [(1, at * outs[1].shape[0], out) for at, out in enumerate(outs[1:])]

    def send(group, rows):
        for side in range(2):
            for at in range(half):
                stage[side, at, group] = result[rows(owner[side * half + at])]
        for side, first, out in spots:
            part = stage.at[side, first : first + out.shape[0], group]
            pltpu.make_async_copy(part, out.at[:, group], sem).start()

    for left, right, place in jobs:
        if left.shape[1] > right.shape[1]:
            for start in range(0, left.shape[1], GROUP):
                stop = start + GROUP
                result[start:stop] = dot_first(left[:, start:stop], right[...]).astype(BF16)
            per = left.shape[1] // right.shape[1]
            for part in range(per):
                spot = lambda block: pl.ds(pl.multiple_of((block * per + part) * BLOCK, BLOCK), BLOCK)
                send(place + part, spot)
        else:
            for group in range(right.shape[1] // GROUP):
                columns = slice(group * GROUP, (group + 1) * GROUP)
                result[: left.shape[1]] = dot_first(left[...], right[:, columns]).astype(BF16)
                send(place + group, lambda block: pl.ds(pl.multiple_of(block * BLOCK, BLOCK), BLOCK))
    for side, first, out in spots:
        pltpu.make_async_copy(stage.at[side, first : first + out.shape[0]], out, sem).wait()


def put_sums(both, slots, outs, odd):
    gate = both[0]["gain_two"].shape[1]
    rows = slots // BLOCK * BLOCK + both[0]["bias_two"].shape[0]
    strips, high = strips_of(rows, gate)
    at = slots % BLOCK
    row = lax.broadcasted_iota(jnp.int32, (8, gate), 0)
    packed = []
    for sums in both:
        one = lambda name: jnp.sum(sums[name][...], 0, keepdims=True)
        bias_two = sums["bias_two"][at : at + 1] + sums["bias_two"][at + 1 : at + 2]
        narrow = [one("b_out")]
        if "gain_one" in sums:
            narrow += [0.5 * one("gain_one"), 0.5 * one("bias_one")]
        filled = sum(part.shape[1] for part in narrow)
        if filled < gate:
            narrow.append(jnp.zeros((1, gate - filled), F32))
        narrow = jnp.concatenate(narrow, 1)
        lines = [0.5 * one("b_left"), 0.5 * one("b_right"), one("gain_two"), bias_two, narrow]
        total = jnp.zeros((8, gate), F32)
        for place, line in enumerate(lines):
            total = jnp.where(row == place, line, total)
        square = [sums["spatial"][strip * high : (strip + 1) * high] for strip in range(strips)]
        packed.append(jnp.concatenate([jnp.concatenate(square, 1), total], 0).astype(BF16))
    outs[0][...] = jnp.where(odd, packed[1], packed[0])
    outs[1][...] = jnp.where(odd, packed[0], packed[1])


def zero(refs):
    for ref in refs:
        ref[...] = jnp.zeros_like(ref)


def whole(shape):
    return pl.BlockSpec(shape, lambda *i: (0,) * len(shape))


def image(rows, columns):
    return pl.BlockSpec((1, rows, columns), lambda i, *unused: (i, 0, 0))


def anywhere(count):
    return [pl.BlockSpec(memory_space=pl.ANY)] * count


def call(kernel, name, grid, in_specs, outs, out_specs, scratch, flops, megabytes, table=0, aliases=None):
    return pl.pallas_call(
        kernel,
        grid_spec=pltpu.PrefetchScalarGridSpec(
            num_scalar_prefetch=table,
            grid=grid,
            in_specs=in_specs,
            out_specs=out_specs,
            scratch_shapes=scratch,
        ),
        out_shape=[jax.ShapeDtypeStruct(shape, dtype) for shape, dtype in outs],
        input_output_aliases=aliases or {},
        compiler_params=pltpu.CompilerParams(vmem_limit_bytes=megabytes << 20),
        cost_estimate=pl.CostEstimate(flops=flops, bytes_accessed=20_000_000, transcendentals=0),
        name=name,
    )


def in_scratch(width, hidden):
    return pltpu.VMEM((hidden // GROUP, width, GROUP), BF16)


def out_scratch(width, hidden):
    return pltpu.VMEM((hidden // 2 // BLOCK, BLOCK, width), BF16)


def strips_of(rows, gate):
    strips = gate // STRIP
    return strips, -(-rows // strips // 8) * 8


def sum_shapes(rows, width, hidden, slots):
    strips, high = strips_of(rows, hidden // 2)
    return {
        "b_out": (8, width),
        "b_left": (8, hidden // 2),
        "b_right": (8, hidden // 2),
        "spatial": (strips * high, STRIP),
        "gain_two": (8, hidden // 2),
        "bias_two": (rows - slots // BLOCK * BLOCK, hidden // 2),
        "gain_one": (8, width),
        "bias_one": (8, width),
    }


def forward_save(values, live, mixer, slot_pad, w, owner, pieces, place, slots, first, count, into=()):
    images, rows, width = values.shape
    hidden = w["b_in"].shape[1]
    gate = hidden // 2
    outs = {name: (gate, BF16) for name in KEPT[:6]}
    outs["normed"] = (width, BF16)
    outs["inverse"] = (1, F32)
    n_w, n_p, n_o, n_i = len(WEIGHTS), len(pieces), len(outs), len(into)

    def kernel(owner_ref, values_ref, live_ref, mixer_ref, pad_ref, *refs):
        weights = dict(zip(WEIGHTS, refs[:n_w]))
        rest = refs[n_w + n_p + n_i :]
        out = dict(zip(outs, rest[:n_o]))
        right, weights["w_in"], sem = rest[n_o:]

        @pl.when(pl.program_id(0) == 0)
        def _():
            load_blocks(owner_ref, refs[n_w : n_w + n_p], [(place, weights["w_in"])], sem)

        kept = {name: ref.at[0] for name, ref in out.items()}
        kept["right"] = right
        here = values_ref[0].astype(F32)
        out["inverse"][0] = forward_image(here, live_ref[...], mixer_ref[0], pad_ref, weights, kept, slots)

    some = lambda columns: pl.BlockSpec((1, rows, columns), lambda i, *unused: (first + i, 0, 0))
    results = call(
        kernel,
        "forward_save",
        (count,),
        [some(width), whole((rows, 1)), some(rows), whole(slot_pad.shape)]
        + [whole(w[name].shape) for name in WEIGHTS]
        + anywhere(n_p + n_i),
        [((images, rows, columns), dtype) for columns, dtype in outs.values()],
        [some(columns) for columns, unused in outs.values()],
        [pltpu.VMEM((rows, gate), F32), in_scratch(width, hidden), pltpu.SemaphoreType.DMA],
        2_000_000_000 * count,
        60,
        table=1,
        aliases={5 + n_w + n_p + at: at for at in range(n_i)},
    )(owner, values, live, mixer, slot_pad, *[w[name] for name in WEIGHTS], *pieces, *into)
    return results


KEPT = ("left", "left_slope", "white", "right_slope", "slot_in", "gated", "normed", "inverse")


def forward_backward(
    values, kept_before, b_out, cotangent, valid, live, mixer, mixer_back, slot_pad, w, owner, pieces, places, slots
):
    images, rows, width = values.shape
    hidden = w["b_in"].shape[1]
    gate = hidden // 2
    groups, per, half = hidden // GROUP, gate // width, width // BLOCK // 2
    outs = {
        "values": (width, BF16),
        "upstream": (width, F32),
        "left_grad_before": (gate, BF16),
        "mixed_grad_before": (gate, BF16),
    }
    shapes = sum_shapes(rows, width, hidden, slots)
    shapes = {name: shapes[name] for name in SUMS} | {
        "b_out_before": shapes["b_out"],
        "b_left_before": shapes["b_left"],
    }
    image_scratch = {"right": F32} | dict.fromkeys(
        ("left", "left_slope", "white", "right_slope", "slot_in", "mixed_grad"), BF16
    )
    all_scratch = {
        "normed": width,
        "gated": gate,
        "hidden_grad": hidden,
        "masked": width,
        "normed_before": width,
        "gated_before": gate,
        "left_grad_before": gate,
        "masked_before": width,
    }
    reads = ("gated", "left", "left_slope", "normed")
    last_shape = (half, groups + per, BLOCK, GROUP)
    before_shape = (half, groups // 2 + per, BLOCK, GROUP)
    n_w, n_p, n_o, n_s, n_r = len(WEIGHTS), len(pieces), len(outs), len(shapes), len(reads)

    def kernel(owner_ref, values_ref, b_out_ref, cot_ref, valid_ref, live_ref, mixer_ref, back_ref, pad_ref, *refs):
        before = {name: ref.at[0] for name, ref in zip(reads, refs)}
        refs = refs[n_r:]
        weights = dict(zip(WEIGHTS, refs[:n_w]))
        rest = refs[n_w + n_p :]
        out = {name: ref.at[0] for name, ref in zip(outs, rest)}
        sums = dict(zip(shapes, rest[n_o:]))
        last_outs, before_outs = rest[n_o + n_s :][:3], rest[n_o + n_s + 3 :][:2]
        rest = rest[n_o + n_s + 5 :]
        kept = dict(zip(image_scratch, rest))
        rest = rest[len(image_scratch) :]
        every = dict(zip(all_scratch, rest))
        w_out_before, weights["w_in"], weights["w_out"], result, last_stage, before_stage, sem, out_sem = rest[len(every) :]
        step = pl.program_id(0)

        @pl.when(step == 0)
        def _():
            targets = (w_out_before, weights["w_in"], weights["w_out"])
            load_blocks(owner_ref, refs[n_w : n_w + n_p], list(zip(places, targets)), sem)
            zero(sums.values())

        mine = pl.ds(pl.multiple_of(step * rows, BLOCK), rows)
        here = {name: ref.at[mine] for name, ref in every.items()}
        kept["normed"], kept["gated"] = here["normed"], here["gated"]
        left_grad, right_grad = (here["hidden_grad"].at[:, at : at + gate] for at in (0, gate))
        here["normed_before"][...] = before["normed"][...]
        here["gated_before"][...] = before["gated"][...]
        valid_column = valid_ref[0]
        inputs = add_branch(values_ref[0].astype(F32), before["gated"][...], valid_column, w_out_before, b_out_ref.at[:1])
        inverse = forward_image(inputs, live_ref[...], mixer_ref[0], pad_ref, weights, kept, slots)
        outputs = add_branch(inputs, kept["gated"][...], valid_column, weights["w_out"], b_out_ref.at[1:])
        out["values"][...] = outputs.astype(BF16)
        upstream = cot_ref[0].astype(F32)
        sums["b_out"][...] += fold_rows(upstream)
        masked = (upstream * valid_column).astype(BF16)
        here["masked"][...] = masked
        backward_left(
            masked, weights["w_out"], kept["left"], kept["left_slope"], kept["mixed_grad"], left_grad, sums["b_left"]
        )
        backward_right(
            valid_column, back_ref[0], inverse, weights["gain_two"], kept, right_grad, sums["b_right"], sums, slots
        )
        upstream = backward_norm(inputs, (left_grad, right_grad), upstream, weights, sums)
        out["upstream"][...] = upstream
        branch_grad = upstream.astype(BF16).astype(F32)
        sums["b_out_before"][...] += fold_rows(branch_grad)
        masked = (branch_grad * valid_column).astype(BF16)
        here["masked_before"][...] = masked
        backward_left(
            masked,
            w_out_before,
            before["left"],
            before["left_slope"],
            out["mixed_grad_before"],
            here["left_grad_before"],
            sums["b_left_before"],
        )
        out["left_grad_before"][...] = here["left_grad_before"][...]

        @pl.when(step == images - 1)
        def _():
            jobs = [(every["normed"], every["hidden_grad"], 0), (every["gated"], every["masked"], groups)]
            put_weight_grads(owner_ref, jobs, result, last_stage, last_outs, out_sem.at[0])
            jobs = [
                (every["normed_before"], every["left_grad_before"], 0),
                (every["gated_before"], every["masked_before"], groups // 2),
            ]
            put_weight_grads(owner_ref, jobs, result, before_stage, before_outs, out_sem.at[1])

    results = call(
        kernel,
        "forward_backward",
        (images,),
        [image(rows, width), whole(b_out.shape), image(rows, width), image(rows, 1), whole((rows, 1))]
        + [image(rows, rows), image(rows, rows), whole(slot_pad.shape)]
        + [image(rows, kept_before[name].shape[2]) for name in reads]
        + [whole(w[name].shape) for name in WEIGHTS]
        + anywhere(n_p),
        [((images, rows, columns), dtype) for columns, dtype in outs.values()]
        + [(shape, F32) for shape in shapes.values()]
        + [(last_shape, BF16)]
        + [((half // 2, *last_shape[1:]), BF16)] * 2
        + [(before_shape, BF16)] * 2,
        [image(rows, columns) for columns, unused in outs.values()]
        + [whole(shape) for shape in shapes.values()]
        + anywhere(5),
        [pltpu.VMEM((rows, gate), dtype) for dtype in image_scratch.values()]
        + [pltpu.VMEM((images * rows, columns), BF16) for columns in all_scratch.values()]
        + [out_scratch(width, hidden), in_scratch(width, hidden), out_scratch(width, hidden)]
        + [pltpu.VMEM((gate, GROUP), BF16), pltpu.VMEM((2,) + last_shape, BF16), pltpu.VMEM((2,) + before_shape, BF16)]
        + [pltpu.SemaphoreType.DMA, pltpu.SemaphoreType.DMA((2,))],
        40_000_000_000,
        60,
        table=1,
    )(
        owner,
        values,
        b_out,
        cotangent,
        valid,
        live,
        mixer,
        mixer_back,
        slot_pad,
        *[kept_before[name] for name in reads],
        *[w[name] for name in WEIGHTS],
        *pieces,
    )
    blocks = results[n_o + n_s :]
    return dict(zip(outs, results)), dict(zip(shapes, results[n_o:])), blocks[:3], blocks[3:]


def backward_slots(kept, mixed_grad, valid, mixer_back, w, owner, both, slots):
    images, rows, gate = mixed_grad.shape
    width = w["gain_one"].shape[1]
    half = width // BLOCK // 2
    shapes = sum_shapes(rows, width, 2 * gate, slots)
    names = ("b_right", "spatial", "gain_two", "bias_two")
    reads = ("white", "right_slope", "slot_in", "inverse", "normed")
    block_shape = (half, gate // GROUP, BLOCK, GROUP)
    high = strips_of(rows, gate)[1]
    flat = [(block, name) for block in range(2) for name in both[block]]
    n_r, n_f, n_s = len(reads), len(flat), len(names)

    def kernel(owner_ref, mixed_ref, valid_ref, back_ref, gain_two, *refs):
        t = {name: ref.at[0] for name, ref in zip(reads, refs)}
        t["mixed_grad"] = mixed_ref.at[0]
        out, *outs = refs[n_r + n_f :][:5]
        rest = refs[n_r + n_f + 5 :]
        own = dict(zip(names, rest))
        normed, right_grad, result, stage, out_sem = rest[n_s:]
        step = pl.program_id(0)

        @pl.when(step == 0)
        def _():
            zero(own.values())

        mine = pl.ds(pl.multiple_of(step * rows, BLOCK), rows)
        normed[mine] = t["normed"][...]
        here = right_grad.at[mine]
        backward_right(valid_ref[0], back_ref[0], t["inverse"][...], gain_two, t, here, own["b_right"], own, slots)
        out[0] = here[...]

        @pl.when(step == images - 1)
        def _():
            put_weight_grads(owner_ref, [(normed, right_grad, 0)], result, stage, outs[:2], out_sem)
            sums = {}, {}
            for (block, name), ref in zip(flat, refs[n_r:]):
                sums[block][name] = ref
            sums[0].update(own)
            put_sums(sums, slots, outs[2:], owner_ref[0] % 2 == 1)

    results = call(
        kernel,
        "backward_slots",
        (images,),
        [image(rows, gate), image(rows, 1), image(rows, rows), whole((1, gate))]
        + [image(rows, kept[name].shape[2]) for name in reads]
        + [whole(both[block][name].shape) for block, name in flat],
        [((images, rows, gate), BF16)] + [(block_shape, BF16)] * 2 + [((high + 8, gate), BF16)] * 2,
        [image(rows, gate)] + anywhere(2) + [whole((high + 8, gate))] * 2,
        [pltpu.VMEM(shapes[name], F32) for name in names]
        + [pltpu.VMEM((images * rows, width), BF16), pltpu.VMEM((images * rows, gate), BF16)]
        + [pltpu.VMEM((width, GROUP), BF16), pltpu.VMEM((2,) + block_shape, BF16), pltpu.SemaphoreType.DMA],
        9_000_000_000,
        60,
        table=1,
    )(
        owner,
        mixed_grad,
        valid,
        mixer_back,
        w["gain_two"],
        *[kept[name] for name in reads],
        *[both[block][name] for block, name in flat],
    )
    return results[0], results[1:3], results[3:]


def backward_first(values, left_grad, right_grad, upstream, w, owner, pieces, place, slots):
    images, rows, width = values.shape
    gate = left_grad.shape[2]
    n_p = len(pieces)

    def kernel(owner_ref, values_ref, left_ref, right_ref, up_ref, gain_ref, *refs):
        out, line, gain_sum, bias_sum, w_in, sem = refs[n_p:]
        step = pl.program_id(0)

        @pl.when(step == 0)
        def _():
            load_blocks(owner_ref, refs[:n_p], [(place, w_in)], sem)
            zero((gain_sum, bias_sum))

        weights = {"w_in": w_in, "gain_one": gain_ref}
        own = {"gain_one": gain_sum, "bias_one": bias_sum}
        halves = left_ref.at[0], right_ref.at[0]
        result = backward_norm(values_ref[0].astype(F32), halves, up_ref[0], weights, own)
        for at in range(images):

            @pl.when(step == at)
            def _(at=at):
                out[at * slots : (at + 1) * slots] = result[:slots]

        @pl.when(step == images - 1)
        def _():
            zero((line,))
            for at, ref in enumerate((gain_sum, bias_sum)):
                line[5:6, (1 + at) * width : (2 + at) * width] = 0.5 * jnp.sum(ref[...], 0, keepdims=True)

    return call(
        kernel,
        "backward_first",
        (images,),
        [image(rows, width), image(rows, gate), image(rows, gate), image(rows, width), whole((1, width))]
        + anywhere(n_p),
        [((images * slots, width), F32), ((8, gate), F32)],
        [whole((images * slots, width)), whole((8, gate))],
        [pltpu.VMEM((8, width), F32)] * 2 + [in_scratch(width, 2 * gate), pltpu.SemaphoreType.DMA],
        6_000_000_000,
        60,
        table=1,
    )(owner, values, left_grad, right_grad, upstream, w["gain_one"], *pieces)


def put_outputs(is_odd, mine, theirs, outs, slots, width):
    gain_one, bias_one, b_in, gain_two, bias_two, spatial, b_sp, b_out = outs
    gate = mine.shape[1]
    high = mine.shape[0] - 8
    strips = gate // STRIP
    held = mine[...].astype(F32), theirs[...].astype(F32)
    for block in range(2):
        value = jnp.where(is_odd, held[1 - block], held[block])
        square = [value[:high, strip * STRIP : (strip + 1) * STRIP] for strip in range(strips)]
        square = jnp.concatenate(square + [jnp.zeros((STRIP, STRIP), F32)], 0)[:STRIP]
        b_sp[block : block + 1] = square[slots : slots + 1, :slots]
        spatial[:, block, :] = square.T[:slots, :slots]
        line = lambda place: value[high + place : high + place + 1]
        b_in[block : block + 1, :gate] = line(0)
        b_in[block : block + 1, gate:] = line(1)
        gain_two[block : block + 1] = line(2)
        bias_two[block : block + 1] = line(3)
        narrow = line(4)
        if block == 0:
            narrow = narrow + (held[0][high + 5 : high + 6] + held[1][high + 5 : high + 6])
        for place, out in enumerate((b_out, gain_one, bias_one)):
            out[block : block + 1] = narrow[:, place * width : (place + 1) * width]


def small_shapes(slots, gate, width):
    return [(2, width), (2, width), (2, 2 * gate), (2, gate), (2, gate), (slots, 2, slots), (2, slots), (2, width)]


def unpack_sums(odd, mine, theirs, slots, width):
    def kernel(odd_ref, mine_ref, theirs_ref, *outs):
        put_outputs(odd_ref[0] == 1, mine_ref, theirs_ref, outs, slots, width)

    return pl.pallas_call(
        kernel,
        in_specs=[pl.BlockSpec(memory_space=pltpu.SMEM)] + [pl.BlockSpec(memory_space=pltpu.VMEM)] * 2,
        out_shape=[jax.ShapeDtypeStruct(shape, F32) for shape in small_shapes(slots, mine.shape[1], width)],
        compiler_params=pltpu.CompilerParams(vmem_limit_bytes=60 << 20),
        name="unpack_sums",
    )(odd, mine, theirs)


def add_blocks(terms, groups, per, odd, mine, theirs, slots):
    arrays = []
    for pairs in terms.values():
        arrays += [array for array, unused in pairs if not any(array is other for other in arrays)]
    index = {id(array): at for at, array in enumerate(arrays)}
    width = arrays[0].shape[-1]

    n_a = len(arrays)

    def kernel(odd_ref, *refs):
        mine_ref, theirs_ref, in_out, out_out, *outs = refs[n_a:]
        put_outputs(odd_ref[0] == 1, mine_ref, theirs_ref, outs, slots, width)
        for (block, group), pairs in terms.items():
            total = None
            for array, at in pairs:
                part = refs[index[id(array)]][0, at].astype(F32)
                total = part if total is None else total + part
            if group < groups:
                in_out[block, :, group * GROUP : (group + 1) * GROUP] = total
            else:
                first = (group - groups) * BLOCK
                out_out[block, first : first + BLOCK] = total

    shapes = [(2, BLOCK, groups * GROUP), (2, per * BLOCK, width)] + small_shapes(slots, mine.shape[1], width)
    results = pl.pallas_call(
        kernel,
        grid=(1,),
        in_specs=[pl.BlockSpec(memory_space=pltpu.SMEM)]
        + [pl.BlockSpec((1,) + array.shape[1:], lambda i: (0, 0, 0, 0)) for array in arrays]
        + [whole(mine.shape)] * 2,
        out_specs=[whole(shape) for shape in shapes],
        out_shape=[jax.ShapeDtypeStruct(shape, F32) for shape in shapes],
        compiler_params=pltpu.CompilerParams(vmem_limit_bytes=60 << 20),
        name="add_blocks",
    )(odd, *arrays, mine, theirs)
    return results[:2], results[2:]


class Tree:
    def __init__(self, devices):
        self.devices = devices
        far = [1 << bit for bit in range(3, devices.bit_length() - 1)]
        self.bits = far + [2, 4], far[::-1] + [4, 2]
        self.steps = len(far) + 2

    def swap(self, values, *steps):
        bits = [sum(bits[step] for step in steps) or 1 for bits in self.bits]
        return lax.ppermute(values, AXES, [(i, i ^ bits[i % 2]) for i in range(self.devices)])

    def owners(self):
        offsets = np.zeros((2, 1 << self.steps), np.int32)
        for core in range(2):
            for step in range(self.steps):
                offsets[core] ^= (np.arange(1 << self.steps, dtype=np.int32) >> step & 1) * self.bits[core][step]
        me = lax.axis_index(AXES).astype(jnp.int32)
        odd = me % 2 == 1
        mine = me ^ jnp.where(odd, offsets[1], offsets[0])
        theirs = (me ^ 1) ^ jnp.where(odd, offsets[0], offsets[1])
        return jnp.concatenate([mine, theirs])

    def gather(self, own):
        held = pack_blocks(own, 1)
        far = self.steps - 2
        got = [
            self.swap(held, *[step for step in range(far) if index >> step & 1]) for index in range(1, 1 << far)
        ]
        wait = yield held, got
        held = jnp.concatenate(after([held, *got], wait))
        first, second = self.swap(held, far), self.swap(held, far + 1)
        wait = yield held, (first, second)
        last = self.swap(after(first, wait), far + 1)
        pieces = [held, first, second]
        others = [self.swap(piece) for piece in pieces]
        wait = yield held, last
        last = after(last, wait)
        yield [*pieces, last, *others, self.swap(last)]

    def sum(self, mine, *theirs):
        return TreeSum(self, mine, *theirs)

    def finish(self, terms, groups, per, ends, slots):
        return add_blocks(terms, groups, per, *ends, slots)

    def total(self, mine, theirs):
        far = self.steps - 2
        order = [*reversed(range(far)), far, far + 1]
        add = lambda one, other: (one.astype(F32) + other.astype(F32)).astype(BF16)
        got = self.swap(theirs)
        wait = yield theirs
        mine = add(mine, after(got, wait))
        got = self.swap(mine, order[0])
        late = yield mine
        late = late.astype(BF16)
        late_got = self.swap(late, order[0])
        wait = yield late
        late = late.astype(F32) + late_got.astype(F32)
        mine = mine.astype(F32) + after(got, wait).astype(F32)
        mine = (mine + jnp.pad(late, ((mine.shape[0] - late.shape[0], 0), (0, 0)))).astype(BF16)
        for step in order[1:]:
            got = self.swap(mine, step)
            wait = yield mine
            mine = add(mine, after(got, wait))
        yield lax.axis_index("narrow") % 2, mine, self.swap(mine)


class TreeSum:
    def __init__(self, links, mine, *theirs):
        self.links, self.step = links, links.steps
        gots = [links.swap(part) for part in theirs[::-1]]
        self.sent, self.got = theirs[-1], gots[0]
        self.columns, self.shared = [[mine, gots[-1]]], []
        self.upper = gots[0] if len(gots) > 1 else None

    def add(self, at):
        total = []
        for column in self.columns:
            total.append(column[0][at].astype(F32))
            for part in column[1:]:
                total[-1] = total[-1] + part[at].astype(F32)
        total = jnp.concatenate(total, 1) if len(total) > 1 else total[0]
        for part in self.shared:
            total = total + part[at].astype(F32)
        return total

    def send(self, wait):
        self.step -= 1
        keep = 1 << self.step
        if self.upper is not None:
            mine, upper = after((self.columns[0][0], self.upper), wait)
            self.sent = (mine[keep:].astype(F32) + upper.astype(F32)).astype(BF16)
            self.upper = None
        else:
            self.columns, self.shared = after((self.columns, self.shared), wait)
            self.sent = self.add(slice(keep, 2 * keep)).astype(BF16)
        self.got = self.links.swap(self.sent, self.step)
        (self.columns[0] if len(self.columns) == 1 else self.shared).append(self.got)
        return self.sent

    def join(self, other):
        self.columns = self.columns + other.columns
        return self

    def terms(self):
        terms = []
        for column in self.columns:
            for at in range(column[0].shape[1]):
                terms.append([(part, at) for part in column] + [(part, len(terms)) for part in self.shared])
        return terms


class PlainSum:
    def __init__(self, mine, *theirs):
        self.blocks = jnp.concatenate([mine, *theirs]).astype(F32)
        self.sent = self.got = theirs[0]

    def send(self, wait):
        return self.sent

    def join(self, other):
        self.blocks = jnp.concatenate([self.blocks, other.blocks], 1)
        return self

    def terms(self):
        return [self.blocks[:, at] for at in range(self.blocks.shape[1])]


class Plain:
    def __init__(self, width, gate):
        self.width, self.gate = width, gate
        self.steps = 4
        self.blocks = width // BLOCK

    def owners(self):
        return jnp.arange(self.blocks, dtype=jnp.int32)

    def gather(self, own):
        gathered = [lax.all_gather(part, AXES, axis=0, tiled=True) for part in own]
        for unused in range(3):
            yield gathered, gathered
        yield [pack_blocks(gathered, self.blocks)]

    def sum(self, mine, *theirs):
        return PlainSum(mine, *theirs)

    def finish(self, terms, groups, per, ends, slots):
        in_grad, out_grad = [], []
        for block in range(2):
            inner = jnp.concatenate([terms[block, group] for group in range(groups)], 2)
            outer = jnp.concatenate([terms[block, groups + part] for part in range(per)], 1)
            in_grad.append(inner.reshape(self.width, -1))
            out_grad.append(outer.reshape(self.gate, -1))
        large = [
            lax.psum_scatter(jnp.stack(grad), AXES, scatter_dimension=1, tiled=True) for grad in (in_grad, out_grad)
        ]
        return large, unpack_sums(*ends, slots, self.width)

    def total(self, mine, theirs):
        yield mine
        late = yield mine
        mine = mine.astype(F32) + jnp.pad(late, ((mine.shape[0] - late.shape[0], 0), (0, 0)))
        yield late
        for unused in range(self.steps - 1):
            yield mine
        yield jnp.int32(0), *lax.psum((mine, theirs.astype(F32)), AXES)


def pack_blocks(parts, blocks):
    packed = []
    for part in parts:
        if part.shape[1] > GROUP:
            packed.append(part.reshape(blocks, BLOCK, -1, GROUP).transpose(0, 2, 1, 3))
        else:
            packed.append(part.reshape(blocks, -1, BLOCK, GROUP))
    return jnp.concatenate(packed, 1)


def after(values, *others):
    return lax.optimization_barrier((values, others))[0] if others != (None,) else values


def bfloat_pair(values):
    top = lax.reduce_precision(values, 8, 7)
    return top.astype(BF16), lax.reduce_precision(values - top, 8, 7).astype(BF16)


def spatial_operands(valid, w_sp, b_sp, gain_two, bias_two, rows):
    images, slots = valid.shape
    gate = gain_two.shape[0]
    cut = slots // BLOCK * BLOCK
    spare = rows - slots
    masked = w_sp[None] * valid[:, None, :].astype(BF16)
    bias = jnp.broadcast_to(jnp.stack(bfloat_pair(b_sp), -1)[None], (images, slots, 2))
    mixer = jnp.concatenate([masked, bias], 2)
    mixer = jnp.pad(mixer, ((0, 0), (0, spare), (0, spare - 2)))
    column_sum = jnp.einsum("ir,pr->ip", valid.astype(BF16), w_sp, preferred_element_type=F32)
    back = jnp.concatenate([jnp.swapaxes(masked, 1, 2), jnp.stack(bfloat_pair(column_sum), 1)], 1)
    back = jnp.pad(back, ((0, 0), (0, spare - 2), (0, spare)))
    one = jnp.ones((gate,), BF16)
    pad = jnp.stack([one, one, *bfloat_pair(bias_two), *bfloat_pair(gain_two)])
    pad = jnp.pad(pad, ((slots - cut, rows - slots - 6), (0, 0))).astype(F32)
    return mixer, back, pad


def shards(
    tokens,
    mask,
    ln1_gain,
    ln1_bias,
    in_weight,
    in_bias,
    ln2_gain,
    ln2_bias,
    spatial_weight,
    spatial_bias,
    out_weight,
    out_bias,
    cotangent,
):
    devices = lax.axis_size(AXES)
    images, slots = mask.shape
    width = tokens.shape[1]
    hidden = in_weight.shape[2]
    gate = hidden // 2
    per = gate // width
    groups = hidden // GROUP
    rows = -(-(slots + 6) // BLOCK) * BLOCK
    spare = rows - slots
    pairwise = devices * BLOCK == width and devices >= 16 and devices & (devices - 1) == 0
    links = Tree(devices) if pairwise else Plain(width, gate)

    owner = links.owners()
    gather_one = links.gather([in_weight[0]])
    unused, got = next(gather_one)
    gather_rest = links.gather(after([out_weight[0], in_weight[1], out_weight[1]], got))
    unused, got = next(gather_rest)
    next(gather_one)
    gather_one.send(got)
    pieces_one = gather_one.send(None)
    column_rest, got_rest = gather_rest.send(None)

    valid = mask.astype(F32)
    padded = lambda array: jnp.pad(array.reshape(images, slots, width), ((0, 0), (0, spare), (0, 0)))
    valid_column = jnp.pad(valid, ((0, 0), (0, spare)))[:, :, None]
    live = (jnp.arange(rows) < slots).astype(F32)[:, None]
    values = padded(tokens)
    layers, spatial = [], []
    for layer in range(2):
        layers.append(
            {
                "b_in": 0.5 * in_bias[layer][None],
                "gain_one": 0.5 * ln1_gain[layer][None],
                "bias_one": 0.5 * ln1_bias[layer][None],
                "gain_two": ln2_gain[layer][None],
                "bias_two": ln2_bias[layer][None],
                "b_out": out_bias[layer][None],
            }
        )
        spatial.append(
            spatial_operands(
                valid, spatial_weight[layer], spatial_bias[layer], ln2_gain[layer], ln2_bias[layer], rows
            )
        )
    cot = padded(cotangent)
    mixer, back, pad = zip(*spatial)

    halfway = images * 2 // 5
    save = lambda array, start, count, into: forward_save(
        array, live, mixer[0], pad[0], layers[0], owner, pieces_one, 0, slots, start, count, into
    )
    kept = save(after(values, column_rest), 0, halfway, ())
    gather_rest.send(kept[0])
    ahead = got_rest[0], valid_column, cot, mixer[1], back, pad[1]
    kept = save(after(values, ahead), halfway, images - halfway, kept)
    pieces_rest = gather_rest.send(kept[0])
    kept = dict(zip(KEPT, kept))
    last, last_sums, last_blocks, before_blocks = forward_backward(
        values,
        kept,
        out_bias,
        cot,
        valid_column,
        live,
        mixer[1],
        back[1],
        pad[1],
        layers[1],
        owner,
        pieces_rest,
        (0, per, per + groups),
        slots,
    )

    unpadded = lambda array: array[:, :slots].reshape(images * slots, width)
    one = links.sum(*last_blocks)
    left = links.sum(before_blocks[0], after(before_blocks[1], one.sent))
    layer_out = unpadded(after(last["values"], left.sent))
    sent = one.send((left.sent, layer_out))
    sums = {"b_out": last_sums.pop("b_out_before"), "b_left": last_sums.pop("b_left_before")}
    right_grad, blocks, packed = backward_slots(
        kept,
        after(last["mixed_grad_before"], sent),
        valid_column,
        back[0],
        layers[0],
        owner,
        (sums, last_sums),
        slots,
    )
    right = links.sum(*after(blocks, one.got, left.got))
    small = links.total(*packed)
    sent = next(small)
    sent = left.send((sent, right.sent))
    sent = one.send(sent)
    sent = right.send(sent)
    sent = small.send(sent)
    input_grad, line = backward_first(
        values, last["left_grad_before"], right_grad, after(last["upstream"], sent), layers[0], owner, pieces_one, 0, slots
    )
    line = after(line, left.got, one.got, right.got)
    sent = small.send(line)
    both = left.join(right)
    sent = both.send(sent)
    for step in range(links.steps - 2):
        sent = one.send(sent)
        sent = small.send(sent)
        sent = both.send(sent)
    for unused in range(2):
        small_end = small.send(sent)
    odd, *summed = small_end
    steps = groups // 2
    spots = [(1, group) for group in range(groups + per)]
    terms = dict(zip(spots, one.terms()))
    spots = [(0, group) for group in range(steps)] + [(0, groups + part) for part in range(per)]
    spots += [(0, steps + group) for group in range(steps)]
    terms |= zip(spots, both.terms())
    large, small = links.finish(terms, groups, per, (odd.reshape(1), *summed), slots)
    in_grad, out_grad = large
    gain_one, bias_one, b_in, gain_two, bias_two, spatial_grad, b_sp, b_out = small
    spatial_grad = spatial_grad.transpose(1, 0, 2)

    return (
        layer_out,
        input_grad,
        gain_one,
        bias_one,
        in_grad,
        b_in,
        gain_two,
        bias_two,
        spatial_grad,
        b_sp,
        out_grad,
        b_out,
    )


def solution(mesh):
    both = P(AXES, None)
    second = P(None, AXES, None)
    in_specs = (both, both, P(), P(), second, P(), P(), P(), P(), P(), second, P(), both)
    out_specs = (both, both, P(), P(), second, P(), P(), P(), P(), P(), second, P())
    return jax.shard_map(shards, mesh=mesh, in_specs=in_specs, out_specs=out_specs, check_vma=False)
```
